256 devices in a mesh: sect: 8 (over y, core), dev: 32 (over z, x).
Axes of the slice: x: 4, y: 4, z: 8, core: 2. Of those that a mesh axis runs over, the one named last changes fastest.
Arguments:
- prompt_lengths: int32 [8, 256], P(None, 'dev'), may hold values from 64 to 128, as said below
- owner_map: int32 [8, 256], P(None, 'dev'), may hold values from 0 to 63, as said below
- block_table: int32 [8, 256, 2], P(None, 'dev'), may hold values from 0 to 15, as said below
- pool_blocks: bfloat16 [8, 512, 64, 576], P('sect', 'dev'), may hold values from -4.5 to 4.5
- queries: bfloat16 [4, 2048, 128, 576], P(None, ('sect', 'dev')), may hold values from -48 to 48
- new_latents: bfloat16 [4, 2048, 576], P(None, ('sect', 'dev')), may hold values from -4.5 to 4.5
- value_up: bfloat16 [128, 512, 128], P('dev'), may hold values from -1.5 to 1.5
- out_proj: bfloat16 [16384, 7168], P('dev'), may hold values from -0.046875 to 0.046875
Outputs:
- decoded: bfloat16 [4, 2048, 7168], P(None, ('sect', 'dev'))
The draws below stay inside these ranges and needn't reach their ends.
Inputs may be any that keep to these rules, and one draw needn't show every extreme that they name: `prompt_lengths`: in each section some request has length 128. Within each device index d, the entries owner_map[p, d * 8 + i] over all p and i name every decode slot 0 to 63 once, and the 8 requests of one section and device index name 8 different sections g. `block_table`: the entries of the 8 requests of one section and device index form a permutation of 0 to 15.
All inputs are finite; a program needn't handle non-finite values.
Results may differ from the reference program's by a relative error of at most 0.02.
Values may be sent and summed in bfloat16 or wider, within the bound.
A program may use at most 128 MiB of HBM per device.

```python
import jax
import jax.numpy as jnp
from jax import lax

D = 7168
H = 128
LAT = 512
ROPE = 64
VDIM = 128
BLOCK = 64
MAXBLK = 2
STEPS = 4
REQ_DEV = 8
CACHE_W = 576
POOL = 16
SECTIONS = 8
N_SECT = 8
N_DEV = 32


def shared_latents(key):
    return jnp.clip(jax.random.normal(key, (STEPS, N_SECT * N_DEV * REQ_DEV, LAT + ROPE), jnp.float32), -4.5, 4.5)


def draw_new_latents(key, part):
    return shared_latents(key).astype(jnp.bfloat16)


def draw_queries(key, part):
    key = jax.random.fold_in(key, 7)
    first = jax.random.fold_in(key, 0)
    shape = (STEPS, N_SECT * N_DEV * REQ_DEV, H, LAT + ROPE)
    return jnp.clip(jax.random.normal(first, shape, jnp.float32), -4.5, 4.5).astype(jnp.bfloat16)


def draw_prompt_lengths(key, part):
    key = jax.random.fold_in(key, 1)
    first, third = jax.random.split(key, 2)
    longest = MAXBLK * BLOCK
    shape = (N_SECT, N_DEV * REQ_DEV)
    lengths = jax.random.randint(first, shape, longest // 2, longest + 1)
    column = jax.random.randint(third, (N_SECT,), 0, N_DEV * REQ_DEV)
    lengths = jnp.where(jnp.arange(N_DEV * REQ_DEV)[None, :] == column[:, None], longest, lengths)
    return lengths.astype(jnp.int32)


def lane_owners(lane_key):
    first, second = jax.random.split(lane_key)
    shifts = jax.random.permutation(first, N_SECT)[:REQ_DEV]
    ranks = jax.vmap(lambda sub_key: jax.random.permutation(sub_key, REQ_DEV))(jax.random.split(second, N_SECT))
    group = (jnp.arange(N_SECT)[:, None] + shifts[None, :]) % N_SECT
    slot = ranks[group, jnp.arange(REQ_DEV)[None, :]]
    return group * REQ_DEV + slot


def draw_owner_map(key, part):
    key = jax.random.fold_in(key, 2)
    lanes = jax.vmap(lane_owners)(jax.random.split(key, N_DEV))
    return jnp.transpose(lanes, (1, 0, 2)).reshape(N_SECT, N_DEV * REQ_DEV).astype(jnp.int32)


def draw_block_table(key, part):
    key = jax.random.fold_in(key, 3)
    orders = jax.vmap(lambda sub_key: jax.random.permutation(sub_key, REQ_DEV * MAXBLK))(jax.random.split(key, N_SECT * N_DEV))
    return orders.reshape(N_SECT, N_DEV * REQ_DEV, MAXBLK).astype(jnp.int32)


def levels(rng, shape, cuts, least, high):
    level, own = 1.0, jax.random.fold_in(rng, 6)
    for dim, blocks in cuts:
        draws = jnp.exp(jax.random.uniform(jax.random.fold_in(own, dim), (blocks,), jnp.float32, least / len(cuts), high / len(cuts)))
        level = level * jnp.repeat(draws, shape[dim] // blocks).reshape([-1 if axis == dim else 1 for axis in range(len(shape))])
    return level


def bell_draw(key, extent, scale, limit, shards=(), kind=jnp.bfloat16):
    factor_of = levels(key, extent, shards, -0.22, 0.18) if shards else 1.0
    values = jax.random.normal(key, extent, jnp.float32) * scale * factor_of
    return jnp.minimum(jnp.maximum(values, -limit), limit).astype(kind)


def setup_inputs(seed: int = 0) -> dict:
    key_of = jax.random.split(jax.random.key(seed), 9)
    prompt_lengths = draw_prompt_lengths(jax.random.fold_in(key_of[8], 71), 0)
    owner_map = draw_owner_map(jax.random.fold_in(key_of[8], 71), 0)
    block_table = draw_block_table(jax.random.fold_in(key_of[8], 71), 0)
    pool_blocks = bell_draw(key_of[3], (SECTIONS, N_DEV * POOL, BLOCK, CACHE_W), 1.0, 4.5, ((0, 8), (1, 32)))
    queries = draw_queries(jax.random.fold_in(key_of[8], 71), 0)
    new_latents = draw_new_latents(jax.random.fold_in(key_of[8], 71), 0)
    value_up = bell_draw(key_of[6], (H, LAT, VDIM), 16 ** -0.5, 1.5, ((0, 32),))
    out_proj = bell_draw(key_of[7], (H * VDIM, D), (H * VDIM) ** -0.5, 0.046875, ((0, 32),))
    return dict(prompt_lengths=prompt_lengths, owner_map=owner_map, block_table=block_table, pool_blocks=pool_blocks, queries=queries, new_latents=new_latents, value_up=value_up, out_proj=out_proj)


score_scale = 192.0 ** -0.5
masked_score = -1.0e30


def reference(prompt_lengths, owner_map, block_table, pool_blocks, queries, new_latents, value_up, out_proj):
    lane_cols = N_DEV * REQ_DEV
    cached_rows = MAXBLK * BLOCK
    requests = N_SECT * lane_cols
    sect_grid = jnp.broadcast_to(jnp.arange(N_SECT, dtype=jnp.int32)[:, None], (N_SECT, lane_cols))
    col_grid = jnp.broadcast_to(jnp.arange(lane_cols, dtype=jnp.int32)[None, :], (N_SECT, lane_cols))
    target = ((owner_map // REQ_DEV) * N_DEV + col_grid // REQ_DEV) * REQ_DEV + owner_map % REQ_DEV
    anchor = jnp.zeros((requests,), jnp.int32).at[target.reshape(-1)].set((sect_grid * lane_cols + col_grid).reshape(-1))
    step_ids = jnp.arange(STEPS, dtype=jnp.int32)
    position = jnp.arange(cached_rows + STEPS, dtype=jnp.int32)

    def attend_one(item):
        source, query_rows, fresh_rows = item
        section = source // lane_cols
        column = source % lane_cols
        length = prompt_lengths[section, column]
        pool_index = (column // REQ_DEV) * (REQ_DEV * MAXBLK) + block_table[section, column]
        cache = pool_blocks[section, pool_index].reshape(cached_rows, LAT + ROPE)
        key_rows = jnp.concatenate([cache, fresh_rows], axis=0).astype(jnp.float32)
        scores = jnp.einsum("shw,tw->sht", query_rows.astype(jnp.float32), key_rows) * score_scale
        live_mask = jnp.where(position[None, :] < cached_rows, position[None, :] < length, position[None, :] - cached_rows <= step_ids[:, None])
        scores = jnp.where(live_mask[:, None, :], scores, masked_score)
        highest = jnp.max(scores, axis=-1, keepdims=True)
        weights = jnp.exp(scores - highest)
        rounded = (weights / jnp.sum(weights, axis=-1, keepdims=True)).astype(jnp.bfloat16)
        rounded = lax.optimization_barrier(rounded).astype(jnp.float32)
        return jnp.einsum("sht,tc->shc", rounded, key_rows[:, :LAT]).astype(jnp.bfloat16)

    latent_out = lax.map(attend_one, (anchor, jnp.transpose(queries, (1, 0, 2, 3)), jnp.transpose(new_latents, (1, 0, 2))))
    latent_out = jnp.transpose(latent_out, (1, 0, 2, 3))
    heads_dev = H // N_DEV
    latent_groups = latent_out.reshape(STEPS, requests, N_DEV, heads_dev, LAT)
    value_groups = value_up.reshape(N_DEV, heads_dev, LAT, VDIM)
    weight_groups = out_proj.reshape(N_DEV, heads_dev * VDIM, D)

    def add_group(running, group):
        latent_part = lax.dynamic_index_in_dim(latent_groups, group, 2, keepdims=False).astype(jnp.float32)
        value_part = lax.dynamic_index_in_dim(value_groups, group, 0, keepdims=False).astype(jnp.float32)
        values = jnp.einsum("sqhc,hcv->sqhv", latent_part, value_part).astype(jnp.bfloat16)
        values = lax.optimization_barrier(values).astype(jnp.float32).reshape(STEPS, requests, heads_dev * VDIM)
        weight_part = lax.dynamic_index_in_dim(weight_groups, group, 0, keepdims=False).astype(jnp.float32)
        partial_value = jnp.einsum("sqk,kd->sqd", values, weight_part).astype(jnp.bfloat16)
        partial_value = lax.optimization_barrier(partial_value).astype(jnp.float32)
        return running + partial_value, None

    summed, ignored = lax.scan(add_group, jnp.zeros((STEPS, requests, D), jnp.float32), jnp.arange(N_DEV, dtype=jnp.int32))
    return summed.astype(jnp.bfloat16)
```

```python
import jax
import jax.numpy as jnp
from jax import lax
from jax.experimental import pallas as pl
from jax.experimental.pallas import tpu as pltpu
from jax.sharding import PartitionSpec as P

MESH = pl.DeviceIdType.MESH
CHIPS_X = 4
GROUP = 4
score_scale = 192.0 ** (-0.5)
masked_score = -1e30


def ilog2(n):
    return n.bit_length() - 1


def nt_dot(a, b):
    return lax.dot_general(a, b, (((1,), (1,)), ((), ())), preferred_element_type=jnp.float32)


def mm(a, b):
    return jnp.dot(a, b, preferred_element_type=jnp.float32)


def make_kernel(sections, chips_z, chips_x, steps, req, heads, lat_w, width, vdim, model, block):
    Y, Z, X = sections // 2, chips_z, chips_x
    HD = heads // (Z * X)
    HZ = HD * X
    NPG = req // GROUP
    PS = GROUP * steps
    CR = 2 * block
    KR = CR + 128
    NX = model // X
    NT = 256
    KD = HD * vdim
    PV, PW = lat_w // (2 * Y), KD // (2 * Y)

    def kernel(
        owner_ref, table_ref, len_ref, pool_hbm, q_hbm, new_ref, vu_hbm, op_hbm, out_ref,
        pool, q, pk, keys, lat, snd, rcv, vu, val, va, w, po, rs, so, fin,
        lsem, cs, cr, v1s, v1r, v2s, v2r, v3s, v3r, w1s, w1r, w2s, w2r, w3s, w3r,
        ls, lr, zs, zr, gs, gr, ss, sr, fs, fr,
    ):
        sect = lax.axis_index("sect")
        dev = lax.axis_index("dev")
        y, c = sect // 2, sect % 2
        z, x = dev // X, dev % X
        sibling = y * 2 + (1 - c)
        piece = c * Y + y
        sends = []

        def at_sect(r):
            return ((sect + r) % sections, dev)

        def at_y(r):
            return (((y + r) % Y) * 2 + c, dev)

        def at_z(r):
            return (sect, ((z + r) % Z) * X + x)

        def at_x(r):
            return (sect, z * X + (x + r) % X)

        def remote(src, dst, send_sem, recv_sem, to):
            return pltpu.make_async_remote_copy(
                src_ref=src, dst_ref=dst, send_sem=send_sem, recv_sem=recv_sem,
                device_id=to, device_id_type=MESH,
            )

        def send(src, dst, send_sem, recv_sem, to):
            copy = remote(src, dst, send_sem, recv_sem, to)
            copy.start()
            sends.append(copy)

        def arrived(src, dst, send_sem, recv_sem, to):
            remote(src, dst, send_sem, recv_sem, to).wait_recv()

        load_pool = pltpu.make_async_copy(pool_hbm.at[0], pool, lsem.at[0])
        load_q = pltpu.make_async_copy(q_hbm, q, lsem.at[1])
        load_vu = pltpu.make_async_copy(vu_hbm, vu.at[0], lsem.at[2])
        own_cols = pl.ds(pl.multiple_of(x * NX, 128), NX)
        load_w = pltpu.make_async_copy(op_hbm.at[:, own_cols], w.at[0], lsem.at[3])
        load_pool.start()
        load_q.start()
        load_vu.start()
        load_w.start()

        barrier = pltpu.get_barrier_semaphore()
        peers = [at_sect(r) for r in range(1, sections)]
        peers += [at_z(r) for r in range(1, Z)] + [at_x(r) for r in range(1, X)]
        for peer in peers:
            pl.semaphore_signal(barrier, inc=1, device_id=peer, device_id_type=MESH)

        new_rows = new_ref[...].astype(jnp.float32).reshape(steps * req, width)
        new_rows = new_rows.astype(jnp.bfloat16)
        pick_u = lax.broadcasted_iota(jnp.int32, (16, steps * req), 0)
        pick_i = lax.broadcasted_iota(jnp.int32, (16, steps * req), 1)

        def slot_and_length(k):
            source = lax.rem(sect - k + sections, sections)
            slot, length = jnp.int32(0), jnp.int32(0)
            for i in range(req):
                owner = owner_ref[source, i]
                mine = lax.div(owner, req) == sect
                slot += jnp.where(mine, lax.rem(owner, req), 0)
                length += jnp.where(mine, len_ref[source, i], 0)
            return slot, length

        def fresh(k, carry):
            slot, _ = slot_and_length(k)
            pick = (pick_u == (pick_i >> ilog2(req))) & ((pick_i & (req - 1)) == slot)
            rows = mm(pick.astype(jnp.bfloat16), new_rows)
            keys[k, pl.ds(CR, 16), :] = rows.astype(jnp.bfloat16)
            keys[k, pl.ds(CR + 16, KR - CR - 16), :] = jnp.zeros((KR - CR - 16, width), jnp.bfloat16)
            return carry

        lax.fori_loop(0, req, fresh, 0)
        load_pool.wait()

        def pack(r):
            target = lax.rem(sect + r, sections)
            first, second = jnp.int32(0), jnp.int32(0)
            for i in range(req):
                hit = lax.div(owner_ref[sect, i], req) == target
                first += jnp.where(hit, table_ref[sect, i, 0], 0)
                second += jnp.where(hit, table_ref[sect, i, 1], 0)
            return pool[first], pool[second]

        def pack_remote(r, carry):
            a, b = pack(r)
            pk[r, 0:block, :] = a
            pk[r, block:CR, :] = b
            return carry

        lax.fori_loop(1, sections, pack_remote, 0)
        a, b = pack(0)
        keys[0, 0:block, :] = a
        keys[0, block:CR, :] = b

        pl.semaphore_wait(barrier, len(peers))

        def cache_args(r):
            return pk.at[r], keys.at[r, pl.ds(0, CR), :], cs.at[r], cr.at[r], at_sect(r)

        for r in range(1, sections):
            send(*cache_args(r))

        vrows = pl.ds(pl.multiple_of(piece * PV, PV), PV)
        wrows = pl.ds(pl.multiple_of(piece * PW, PW), PW)

        def v1_args(r):
            return vu_hbm.at[:, vrows, :], vu.at[r, :, vrows, :], v1s.at[r], v1r.at[r], at_z(r)

        def w1_args(r):
            cols = pl.ds(pl.multiple_of(((x + r) % X) * NX, 128), NX)
            return op_hbm.at[wrows, cols], w.at[r, wrows, :], w1s.at[r], w1r.at[r], at_x(r)

        def v2_args(r, rows):
            part = vu.at[pl.ds(1, Z - 1), :, rows, :]
            return part, part, v2s.at[r], v2r.at[r], at_y(r)

        def w2_args(r, rows):
            part = w.at[pl.ds(1, X - 1), rows, :]
            return part, part, w2s.at[r], w2r.at[r], at_y(r)

        def v3_args(core):
            rows = pl.ds(pl.multiple_of(core * (lat_w // 2), PV), lat_w // 2)
            part = vu.at[pl.ds(1, Z - 1), :, rows, :]
            return part, part, v3s.at[0], v3r.at[0], (sibling, dev)

        def w3_args(core):
            rows = pl.ds(pl.multiple_of(core * (KD // 2), PW), KD // 2)
            part = w.at[pl.ds(1, X - 1), rows, :]
            return part, part, w3s.at[0], w3r.at[0], (sibling, dev)

        def piece_rows(r, size):
            return pl.ds(pl.multiple_of((c * Y + (y - r + Y) % Y) * size, size), size)

        for r in range(1, Z):
            send(*v1_args(r))
        for r in range(1, X):
            send(*w1_args(r))

        swap_out = lax.broadcasted_iota(jnp.int32, (HZ * PS, HZ * PS), 0)
        swap_in = lax.broadcasted_iota(jnp.int32, (HZ * PS, HZ * PS), 1)
        swap = ((swap_out >> ilog2(PS)) == (swap_in & (HZ - 1))) & (
            (swap_out & (PS - 1)) == (swap_in >> ilog2(HZ))
        )
        swap = swap.astype(jnp.bfloat16)
        load_q.wait()

        def attend(k, k4):
            slot, length = slot_and_length(k)
            q_lat = q[:, slot, :, 0:lat_w].reshape(steps * heads, lat_w)
            q_rope = q[:, slot, :, lat_w:width].reshape(steps * heads, width - lat_w)
            key_lat = keys[k, :, 0:lat_w]
            key_rope = keys[k, :, lat_w:width]
            scores = (nt_dot(q_lat, key_lat) + nt_dot(q_rope, key_rope)) * score_scale
            scores = scores.reshape(steps, heads, KR)
            col = lax.broadcasted_iota(jnp.int32, scores.shape, 2)
            step = lax.broadcasted_iota(jnp.int32, scores.shape, 0)
            held = jnp.where(col < CR, length, CR + 1 + step)
            scores = jnp.where(col < held, scores, masked_score)
            weights = jnp.exp(scores - jnp.max(scores, axis=-1, keepdims=True))
            probs = weights * (1.0 / jnp.sum(weights, axis=-1, keepdims=True))
            probs = probs.astype(jnp.bfloat16).reshape(steps * heads, KR)
            out = mm(probs, key_lat).astype(jnp.bfloat16)
            lat[k4] = out.reshape(steps, heads, lat_w)

        def latent_args(r, pg):
            to = (x + r) % X
            return snd.at[to, pg], rcv.at[x, pg], ls.at[pg, r], lr.at[pg, r], at_x(r)

        def latent_from(r, pg):
            source = (x - r + X) % X
            return snd.at[source, pg], rcv.at[source, pg], ls.at[pg, r], lr.at[pg, r], at_x(r)

        local_latents = []

        def attention(pg):
            def one(k4, carry):
                k = pg * GROUP + k4

                @pl.when(k > 0)
                def _():
                    arrived(pk.at[k], keys.at[k, pl.ds(0, CR), :], cs.at[k], cr.at[k], at_sect(k))

                attend(k, k4)
                return carry

            lax.fori_loop(0, GROUP, one, 0)

            def turn(zz, carry):
                part = lat[:, :, pl.ds(pl.multiple_of(zz * HZ, HZ), HZ), :]
                turned = mm(swap, part.reshape(PS * HZ, lat_w)).astype(jnp.bfloat16)
                snd[:, pg, zz] = turned.reshape(X, HD, PS, lat_w)
                return carry

            lax.fori_loop(0, Z, turn, 0)
            for r in range(1, X):
                send(*latent_args(r, pg))
            own = pltpu.make_async_copy(snd.at[x, pg], rcv.at[x, pg], lsem.at[4 + pg])
            own.start()
            local_latents.append(own)

        def value_args(r, pg):
            to = (z + r) % Z
            return val.at[to, pg], va.at[0, pg, z], zs.at[pg, r], zr.at[pg, r], at_z(r)

        def value_from(r, pg):
            source = (z - r + Z) % Z
            return val.at[source, pg], va.at[0, pg, source], zs.at[pg, r], zr.at[pg, r], at_z(r)

        local_values = []

        def values(pg):
            for r in range(1, X):
                arrived(*latent_from(r, pg))
            local_latents[pg].wait()

            def ring(r, carry):
                zz = lax.rem(z - r + Z, Z)
                for hh in range(HD):
                    rows = rcv[:, pg, zz, hh].reshape(X * PS, lat_w)
                    part = mm(rows, vu[r, hh]).astype(jnp.bfloat16)
                    val[zz, pg, :, hh * vdim : (hh + 1) * vdim] = part
                return carry

            lax.fori_loop(0, Z, ring, 0)
            for r in range(1, Z):
                send(*value_args(r, pg))
            own = pltpu.make_async_copy(val.at[z, pg], va.at[0, pg, z], lsem.at[4 + NPG + pg])
            own.start()
            local_values.append(own)

        def gather_args(r, pg):
            return va.at[0, pg], va.at[r, pg], gs.at[pg, r], gr.at[pg, r], at_x(r)

        def gather_start(pg):
            for r in range(1, Z):
                arrived(*value_from(r, pg))
            local_values[pg].wait()
            for r in range(1, X):
                send(*gather_args(r, pg))

        def sum_args(r, pg):
            to = (z + r) % Z
            return po.at[to, pg], rs.at[r, pg], ss.at[pg, r], sr.at[pg, r], at_z(r)

        def project(pg):
            for r in range(1, X):
                arrived(*gather_args(r, pg))

            def tile(n, carry):
                cols = pl.ds(pl.multiple_of(n * NT, NT), NT)
                acc = mm(va[0, pg].reshape(Z * X * PS, KD), w[0, :, cols])
                for r in range(1, X):
                    acc += mm(va[r, pg].reshape(Z * X * PS, KD), w[r, :, cols])
                po[:, pg, :, cols] = acc.astype(jnp.bfloat16).reshape(Z, X * PS, NT)
                return carry

            lax.fori_loop(0, NX // NT, tile, 0)
            for r in range(1, Z):
                send(*sum_args(r, pg))

        def final_args(r, pg):
            to = (x + r) % X
            return so.at[pg, to], fin.at[x, pg], fs.at[pg, r], fr.at[pg, r], at_x(r)

        def final_from(r, pg):
            source = (x - r + X) % X
            return so.at[pg, source], fin.at[source, pg], fs.at[pg, r], fr.at[pg, r], at_x(r)

        local_final = []

        def reduce(pg):
            for r in range(1, Z):
                arrived(*sum_args(r, pg))

            def rows_of(xx, carry):
                rows = pl.ds(pl.multiple_of(xx * PS, PS), PS)
                total = po[z, pg, rows, :].astype(jnp.float32)
                for r in range(1, Z):
                    total += rs[r, pg, rows, :].astype(jnp.float32)
                so[pg, xx] = total.astype(jnp.bfloat16)
                return carry

            lax.fori_loop(0, X, rows_of, 0)
            for r in range(1, X):
                send(*final_args(r, pg))
            own = pltpu.make_async_copy(so.at[pg, x], fin.at[x, pg], lsem.at[4 + 2 * NPG + pg])
            own.start()
            local_final.append(own)

        for r in range(1, Z):
            arrived(*v1_args(r))
        for r in range(1, Y):
            send(*v2_args(r, vrows))
        attention(0)
        for r in range(1, X):
            arrived(*w1_args(r))
        for r in range(1, Y):
            send(*w2_args(r, wrows))
        for pg in range(1, NPG):
            attention(pg)
        load_vu.wait()
        for r in range(1, Y):
            arrived(*v2_args(r, piece_rows(r, PV)))
        send(*v3_args(c))
        arrived(*v3_args(1 - c))
        for pg in range(NPG):
            values(pg)
            gather_start(pg)
        load_w.wait()
        for r in range(1, Y):
            arrived(*w2_args(r, piece_rows(r, PW)))
        send(*w3_args(c))
        arrived(*w3_args(1 - c))
        for pg in range(NPG):
            project(pg)
        for pg in range(NPG):
            reduce(pg)

        place_out = lax.broadcasted_iota(jnp.int32, (steps * req, steps * req), 0)
        place_in = lax.broadcasted_iota(jnp.int32, (steps * req, steps * req), 1)
        slots = jnp.zeros((steps * req, steps * req), jnp.int32)
        for k in range(req):
            slot, _ = slot_and_length(k)
            slots = jnp.where((place_in >> ilog2(steps)) == k, slot, slots)
        place = ((place_out >> ilog2(req)) == (place_in & (steps - 1))) & (
            (place_out & (req - 1)) == slots
        )
        place = place.astype(jnp.bfloat16)
        for pg in range(NPG):
            for r in range(1, X):
                arrived(*final_from(r, pg))
            local_final[pg].wait()
        for xs in range(X):
            rows = mm(place, fin[xs].reshape(NPG * PS, NX))
            for s in range(steps):
                part = rows[s * req : (s + 1) * req].astype(jnp.bfloat16)
                out_ref[s, :, xs * NX : (xs + 1) * NX] = part

        for copy in sends:
            copy.wait_send()

    bf = jnp.bfloat16
    dma = pltpu.SemaphoreType.DMA
    scratch = [
        pltpu.VMEM((2 * req, block, width), bf),
        pltpu.VMEM((steps, req, heads, width), bf),
        pltpu.VMEM((sections, CR, width), bf),
        pltpu.VMEM((req, KR, width), bf),
        pltpu.VMEM((GROUP, steps, heads, lat_w), bf),
        pltpu.VMEM((X, NPG, Z, HD, PS, lat_w), bf),
        pltpu.VMEM((X, NPG, Z, HD, PS, lat_w), bf),
        pltpu.VMEM((Z, HD, lat_w, vdim), bf),
        pltpu.VMEM((Z, NPG, X * PS, KD), bf),
        pltpu.VMEM((X, NPG, Z, X * PS, KD), bf),
        pltpu.VMEM((X, KD, NX), bf),
        pltpu.VMEM((Z, NPG, X * PS, NX), bf),
        pltpu.VMEM((Z, NPG, X * PS, NX), bf),
        pltpu.VMEM((NPG, X, PS, NX), bf),
        pltpu.VMEM((X, NPG, PS, NX), bf),
        dma((4 + 3 * NPG,)),
        dma((sections,)), dma((sections,)),
        dma((Z,)), dma((Z,)), dma((Y,)), dma((Y,)), dma((1,)), dma((1,)),
        dma((X,)), dma((X,)), dma((Y,)), dma((Y,)), dma((1,)), dma((1,)),
        dma((NPG, X)), dma((NPG, X)), dma((NPG, Z)), dma((NPG, Z)),
        dma((NPG, X)), dma((NPG, X)), dma((NPG, Z)), dma((NPG, Z)),
        dma((NPG, X)), dma((NPG, X)),
    ]
    return kernel, scratch


def on_device(
    prompt_lengths, owner_map, block_table, pool_blocks, queries, new_latents, value_up, out_proj
):
    sections, devices = lax.axis_size("sect"), lax.axis_size("dev")
    steps, req, heads, width = queries.shape
    _, lat_w, vdim = value_up.shape
    model = out_proj.shape[1]
    block = pool_blocks.shape[2]
    kernel, scratch = make_kernel(
        sections, devices // CHIPS_X, CHIPS_X, steps, req, heads, lat_w, width, vdim, model, block
    )
    smem = pl.BlockSpec(memory_space=pltpu.SMEM)
    vmem = pl.BlockSpec(memory_space=pltpu.VMEM)
    hbm = pl.BlockSpec(memory_space=pl.ANY)
    return pl.pallas_call(
        kernel,
        out_shape=jax.ShapeDtypeStruct((steps, req, model), jnp.bfloat16),
        in_specs=[smem, smem, smem, hbm, hbm, vmem, hbm, hbm],
        out_specs=vmem,
        scratch_shapes=scratch,
        compiler_params=pltpu.CompilerParams(
            collective_id=0, has_side_effects=True, vmem_limit_bytes=60 * 1024 * 1024
        ),
    )(owner_map, block_table, prompt_lengths, pool_blocks, queries, new_latents, value_up, out_proj)


def solution(mesh):
    in_specs = (
        P(None, "dev"),
        P(None, "dev"),
        P(None, "dev", None),
        P("sect", "dev", None, None),
        P(None, ("sect", "dev"), None, None),
        P(None, ("sect", "dev"), None),
        P("dev", None, None),
        P("dev", None),
    )
    out_specs = P(None, ("sect", "dev"), None)
    return jax.shard_map(
        on_device, mesh=mesh, in_specs=in_specs, out_specs=out_specs, check_vma=False
    )
```

```python
import jax
import jax.numpy as jnp
from jax import lax
from jax.experimental import pallas as pl
from jax.experimental.pallas import tpu as pltpu
from jax.sharding import PartitionSpec as P

MESH = pl.DeviceIdType.MESH
CHIPS_X = 4
GROUP = 4
score_scale = 192.0 ** (-0.5)
masked_score = -1e30


def ilog2(n):
    return n.bit_length() - 1


def tn_dot(a, b):
    return lax.dot_general(a, b, (((0,), (0,)), ((), ())), preferred_element_type=jnp.float32)


def mm(a, b):
    return jnp.dot(a, b, preferred_element_type=jnp.float32)


def make_kernel(sections, chips_z, chips_x, steps, req, heads, lat_w, width, vdim, model, block):
    Y, Z, X = sections // 2, chips_z, chips_x
    HD = heads // (Z * X)
    HZ = HD * X
    NPG = req // GROUP
    PS = GROUP * steps
    CR = 2 * block
    KR = CR + 16
    PAIRS = X // 2
    NX = model // 2
    HX = NX // 2
    PR = 2 * PS
    NT = 256
    KD = HD * vdim
    PV, PW = lat_w // (2 * Y), KD // (2 * Y)

    def kernel(
        owner_ref, table_ref, len_ref, pool_hbm, q_hbm, new_ref, vu_hbm, op_hbm, out_ref,
        pool, q, pk, keys, lat, snd, rcv, vu, val, vz, va, w, po, rs, so, fin,
        lsem, cs, cr, v1s, v1r, v2s, v2r, v3s, v3r, w1s, w1r, w2s, w2r, w3s, w3r,
        ls, lr, zs, zr, gs, gr, ss, sr, fs, fr,
    ):
        sect = lax.axis_index("sect")
        dev = lax.axis_index("dev")
        y, c = sect // 2, sect % 2
        z, x = dev // X, dev % X
        sibling = y * 2 + (1 - c)
        piece = c * Y + y
        pair, half = x // 2, x % 2
        sends = []

        def at_sect(r):
            return ((sect + r) % sections, dev)

        def at_y(r):
            return (((y + r) % Y) * 2 + c, dev)

        def at_z(r):
            return (sect, ((z + r) % Z) * X + x)

        def at_x(r):
            return (sect, z * X + (x + r) % X)

        def remote(src, dst, send_sem, recv_sem, to):
            return pltpu.make_async_remote_copy(
                src_ref=src, dst_ref=dst, send_sem=send_sem, recv_sem=recv_sem,
                device_id=to, device_id_type=MESH,
            )

        def send(src, dst, send_sem, recv_sem, to):
            copy = remote(src, dst, send_sem, recv_sem, to)
            copy.start()
            sends.append(copy)

        def arrived(src, dst, send_sem, recv_sem, to):
            remote(src, dst, send_sem, recv_sem, to).wait_recv()

        load_pool = pltpu.make_async_copy(pool_hbm.at[0], pool, lsem.at[0])
        load_q = pltpu.make_async_copy(q_hbm, q, lsem.at[1])
        load_vu = pltpu.make_async_copy(vu_hbm, vu.at[0], lsem.at[2])
        own_cols = pl.ds(pl.multiple_of(half * NX, 128), NX)
        load_w = pltpu.make_async_copy(op_hbm.at[:, own_cols], w.at[0], lsem.at[3])
        load_pool.start()
        load_q.start()
        load_vu.start()
        load_w.start()

        barrier = pltpu.get_barrier_semaphore()
        peers = [at_sect(r) for r in range(1, sections)]
        peers += [at_z(r) for r in range(1, Z)] + [at_x(r) for r in range(1, X)]
        for peer in peers:
            pl.semaphore_signal(barrier, inc=1, device_id=peer, device_id_type=MESH)

        new_rows = new_ref[...].astype(jnp.float32).reshape(steps * req, width)
        new_rows = new_rows.astype(jnp.bfloat16)
        pick_u = lax.broadcasted_iota(jnp.int32, (16, steps * req), 0)
        pick_i = lax.broadcasted_iota(jnp.int32, (16, steps * req), 1)

        def slot_and_length(k):
            source = lax.rem(sect - k + sections, sections)
            slot, length = jnp.int32(0), jnp.int32(0)
            for i in range(req):
                owner = owner_ref[source, i]
                mine = lax.div(owner, req) == sect
                slot += jnp.where(mine, lax.rem(owner, req), 0)
                length += jnp.where(mine, len_ref[source, i], 0)
            return slot, length

        def fresh(k, carry):
            slot, _ = slot_and_length(k)
            pick = (pick_u == (pick_i >> ilog2(req))) & ((pick_i & (req - 1)) == slot)
            rows = mm(pick.astype(jnp.bfloat16), new_rows)
            keys[k, pl.ds(CR, 16), :] = rows.astype(jnp.bfloat16)
            return carry

        lax.fori_loop(0, req, fresh, 0)
        load_pool.wait()

        def pack(r):
            target = lax.rem(sect + r, sections)
            first, second = jnp.int32(0), jnp.int32(0)
            for i in range(req):
                hit = lax.div(owner_ref[sect, i], req) == target
                first += jnp.where(hit, table_ref[sect, 0, i], 0)
                second += jnp.where(hit, table_ref[sect, 1, i], 0)
            return pool[first], pool[second]

        def pack_remote(r, carry):
            a, b = pack(r)
            pk[r, 0:block, :] = a
            pk[r, block:CR, :] = b
            return carry

        lax.fori_loop(1, sections, pack_remote, 0)
        a, b = pack(0)
        keys[0, 0:block, :] = a
        keys[0, block:CR, :] = b

        pl.semaphore_wait(barrier, len(peers))

        def cache_args(r):
            return pk.at[r], keys.at[r, pl.ds(0, CR), :], cs.at[r], cr.at[r], at_sect(r)

        for r in range(1, sections):
            send(*cache_args(r))

        vrows = pl.ds(pl.multiple_of(piece * PV, PV), PV)
        wrows = pl.ds(pl.multiple_of(piece * PW, PW), PW)

        def v1_args(r):
            return vu_hbm.at[:, vrows, :], vu.at[r, :, vrows, :], v1s.at[r], v1r.at[r], at_z(r)

        def w1_args(r):
            cols = pl.ds(pl.multiple_of(((x + r) % X) % 2 * NX, 128), NX)
            return op_hbm.at[wrows, cols], w.at[r, wrows, :], w1s.at[r], w1r.at[r], at_x(r)

        def from_y(r, size, part, parts):
            start = (c * Y + (y - r + Y) % Y) * size + part * (size // parts)
            return pl.ds(pl.multiple_of(start, size // parts), size // parts)

        def v2_args(r, rows, slot):
            part = vu.at[pl.ds(1, Z - 1), :, rows, :]
            return part, part, v2s.at[slot], v2r.at[slot], at_y(r)

        def w2_args(r, rows, slot):
            part = w.at[pl.ds(1, X - 1), rows, :]
            return part, part, w2s.at[slot], w2r.at[slot], at_y(r)

        def y_start(args, size):
            send(*args(1, from_y(0, size, 0, 1), 0))
            if Y > 2:
                send(*args(Y - 1, from_y(0, size, 0, 1), 1))

        def y_forward(args, size):
            arrived(*args(1, from_y(1, size, 0, 1), 0))
            if Y > 2:
                send(*args(1, from_y(1, size, 0, 2), 2))
                arrived(*args(Y - 1, from_y(Y - 1, size, 0, 1), 1))
                send(*args(Y - 1, from_y(Y - 1, size, 1, 2), 3))

        def y_finish(args, size):
            if Y > 2:
                arrived(*args(1, from_y(2, size, 0, 2), 2))
                arrived(*args(Y - 1, from_y(2, size, 1, 2), 3))

        def v3_args(core):
            rows = pl.ds(pl.multiple_of(core * (lat_w // 2), PV), lat_w // 2)
            part = vu.at[pl.ds(1, Z - 1), :, rows, :]
            return part, part, v3s.at[0], v3r.at[0], (sibling, dev)

        def w3_args(core):
            rows = pl.ds(pl.multiple_of(core * (KD // 2), PW), KD // 2)
            part = w.at[pl.ds(1, X - 1), rows, :]
            return part, part, w3s.at[0], w3r.at[0], (sibling, dev)

        for r in range(1, Z):
            send(*v1_args(r))
        for r in range(1, X):
            send(*w1_args(r))

        swap_out = lax.broadcasted_iota(jnp.int32, (HZ * PS, HZ * PS), 0)
        swap_in = lax.broadcasted_iota(jnp.int32, (HZ * PS, HZ * PS), 1)
        swap = ((swap_out >> ilog2(PS)) == (swap_in & (HZ - 1))) & (
            (swap_out & (PS - 1)) == (swap_in >> ilog2(HZ))
        )
        swap = swap.astype(jnp.bfloat16)
        load_q.wait()

        def attend(k, k4):
            slot, length = slot_and_length(k)
            key_rows = keys[k]
            key_lat = keys[k, :, 0:lat_w]
            q_cols = jnp.concatenate([q[s, slot] for s in range(steps)], axis=1)
            scores = mm(key_rows, q_cols) * score_scale
            row = lax.broadcasted_iota(jnp.int32, scores.shape, 0)
            step = lax.broadcasted_iota(jnp.int32, scores.shape, 1) >> ilog2(heads)
            held = jnp.where(row < CR, length, CR + 1 + step)
            scores = jnp.where(row < held, scores, masked_score)
            weights = jnp.exp(scores - jnp.max(scores, axis=0, keepdims=True))
            probs = weights * (1.0 / jnp.sum(weights, axis=0, keepdims=True))
            out = tn_dot(probs.astype(jnp.bfloat16), key_lat).astype(jnp.bfloat16)
            lat[k4] = out.reshape(steps, heads, lat_w)

        def latent_args(r, pg):
            to = (x + r) % X
            return snd.at[to, pg], rcv.at[x, pg], ls.at[pg, r], lr.at[pg, r], at_x(r)

        def latent_from(r, pg):
            source = (x - r + X) % X
            return snd.at[source, pg], rcv.at[source, pg], ls.at[pg, r], lr.at[pg, r], at_x(r)

        local_latents = []

        def attention(pg):
            def one(k4, carry):
                k = pg * GROUP + k4

                @pl.when(k > 0)
                def _():
                    arrived(pk.at[k], keys.at[k, pl.ds(0, CR), :], cs.at[k], cr.at[k], at_sect(k))

                attend(k, k4)
                return carry

            lax.fori_loop(0, GROUP, one, 0)

            def turn(zz, carry):
                part = lat[:, :, pl.ds(pl.multiple_of(zz * HZ, HZ), HZ), :]
                turned = mm(swap, part.reshape(PS * HZ, lat_w)).astype(jnp.bfloat16)
                snd[:, pg, zz] = turned.reshape(X, HD, PS, lat_w)
                return carry

            lax.fori_loop(0, Z, turn, 0)
            for r in range(1, X):
                send(*latent_args(r, pg))
            own = pltpu.make_async_copy(snd.at[x, pg], rcv.at[x, pg], lsem.at[4 + pg])
            own.start()
            local_latents.append(own)

        def value_args(r, pg):
            to = (z + r) % Z
            return val.at[to, pg], vz.at[pg, :, z], zs.at[pg, r], zr.at[pg, r], at_z(r)

        def value_from(r, pg):
            source = (z - r + Z) % Z
            return val.at[source, pg], vz.at[pg, :, source], zs.at[pg, r], zr.at[pg, r], at_z(r)

        local_values = []

        def values(pg):
            for r in range(1, X):
                arrived(*latent_from(r, pg))
            local_latents[pg].wait()

            def ring(r, carry):
                zz = lax.rem(z - r + Z, Z)
                for hh in range(HD):
                    rows = rcv[:, pg, zz, hh].reshape(X * PS, lat_w)
                    part = mm(rows, vu[r, hh]).astype(jnp.bfloat16)
                    val[zz, pg, :, :, hh * vdim : (hh + 1) * vdim] = part.reshape(PAIRS, PR, vdim)
                return carry

            lax.fori_loop(0, Z, ring, 0)
            for r in range(1, Z):
                send(*value_args(r, pg))
            own = pltpu.make_async_copy(val.at[z, pg], vz.at[pg, :, z], lsem.at[4 + NPG + pg])
            own.start()
            local_values.append(own)

        def gather_args(r, pg):
            to = ((x + r) % X) // 2
            return vz.at[pg, to], va.at[r, pg], gs.at[pg, r], gr.at[pg, r], at_x(r)

        def gather_start(pg):
            for r in range(1, Z):
                arrived(*value_from(r, pg))
            local_values[pg].wait()
            for r in range(1, X):
                send(*gather_args(r, pg))

        def ring_args(d, i, pg):
            sign = 1 - 2 * d
            target = (z - sign * (1 + i) + Z) % Z
            held = po.at[target, pg, d] if i == 0 else rs.at[d, pg, i - 1]
            return held, rs.at[d, pg, i], ss.at[d, pg, i], sr.at[d, pg, i], at_z(sign + Z)

        def add_own(d, i, pg, target):
            def rows_of(m, carry):
                rows = pl.ds(pl.multiple_of(m * PS, PS), PS)
                total = rs[d, pg, i, rows, :].astype(jnp.float32)
                total += po[target, pg, d, rows, :].astype(jnp.float32)
                rs[d, pg, i, rows, :] = total.astype(jnp.bfloat16)
                return carry

            lax.fori_loop(0, 2, rows_of, 0)

        def ring_step(i, pg):
            for d in range(2):
                arrived(*ring_args(d, i - 1, pg))
                add_own(d, i - 1, pg, (z - (1 - 2 * d) * (1 + i) + 2 * Z) % Z)
                send(*ring_args(d, i, pg))

        def project(pg):
            for r in range(1, X):
                arrived(*gather_args(r, pg))
            for d in range(2):

                def tile(n, carry):
                    cols = pl.ds(pl.multiple_of(d * HX + n * NT, NT), NT)
                    acc = mm(vz[pg, pair].reshape(Z * PR, KD), w[0, :, cols])
                    for r in range(1, X):
                        acc += mm(va[r, pg].reshape(Z * PR, KD), w[r, :, cols])
                    part = acc.astype(jnp.bfloat16).reshape(Z, PR, NT)
                    po[:, pg, d, :, pl.ds(pl.multiple_of(n * NT, NT), NT)] = part
                    return carry

                lax.fori_loop(0, HX // NT, tile, 0)
                send(*ring_args(d, 0, pg))

        def final_args(pg, side):
            return so.at[pg, 1 - side], fin.at[side, pg], fs.at[pg], fr.at[pg], at_x(1 - 2 * half + X)

        local_final = []

        def reduce(pg):
            for d in range(2):
                arrived(*ring_args(d, Z - 2, pg))
                for m in range(2):
                    rows = pl.ds(m * PS, PS)
                    total = po[z, pg, d, rows, :].astype(jnp.float32)
                    total += rs[d, pg, Z - 2, rows, :].astype(jnp.float32)
                    so[pg, m, :, pl.ds(d * HX, HX)] = total.astype(jnp.bfloat16)
            send(*final_args(pg, half))
            own = pltpu.make_async_copy(so.at[pg, half], fin.at[half, pg], lsem.at[4 + 2 * NPG + pg])
            own.start()
            local_final.append(own)

        for r in range(1, Z):
            arrived(*v1_args(r))
        y_start(v2_args, PV)
        attention(0)
        y_forward(v2_args, PV)
        for r in range(1, X):
            arrived(*w1_args(r))
        y_start(w2_args, PW)
        for pg in range(1, NPG):
            attention(pg)
        load_vu.wait()
        y_finish(v2_args, PV)
        send(*v3_args(c))
        y_forward(w2_args, PW)
        arrived(*v3_args(1 - c))
        for pg in range(NPG):
            values(pg)
            gather_start(pg)
        load_w.wait()
        y_finish(w2_args, PW)
        send(*w3_args(c))
        arrived(*w3_args(1 - c))
        first = Z // 2 + 1
        project(0)
        if NPG == 1:
            for i in range(1, Z - 1):
                ring_step(i, 0)
        else:
            for i in range(1, first):
                ring_step(i, 0)
            project(1)
            for i in range(1, Z - 1):
                if first <= i + first - 1 < Z - 1:
                    ring_step(i + first - 1, 0)
                elif i + first - 1 == Z - 1:
                    reduce(0)
                ring_step(i, 1)
        reduce(NPG - 1)

        place_out = lax.broadcasted_iota(jnp.int32, (steps * req, steps * req), 0)
        place_in = lax.broadcasted_iota(jnp.int32, (steps * req, steps * req), 1)
        slots = jnp.zeros((steps * req, steps * req), jnp.int32)
        for k in range(req):
            slot, _ = slot_and_length(k)
            slots = jnp.where((place_in >> ilog2(steps)) == k, slot, slots)
        place = ((place_out >> ilog2(req)) == (place_in & (steps - 1))) & (
            (place_out & (req - 1)) == slots
        )
        place = place.astype(jnp.bfloat16)
        for pg in range(NPG):
            arrived(*final_args(pg, 1 - half))
            local_final[pg].wait()
        for side in range(2):
            rows = mm(place, fin[side].reshape(NPG * PS, NX))
            for s in range(steps):
                part = rows[s * req : (s + 1) * req].astype(jnp.bfloat16)
                out_ref[s, :, side * NX : (side + 1) * NX] = part

        for copy in sends:
            copy.wait_send()

    bf = jnp.bfloat16
    dma = pltpu.SemaphoreType.DMA
    scratch = [
        pltpu.VMEM((2 * req, block, width), bf),
        pltpu.VMEM((steps, req, width, heads), bf),
        pltpu.VMEM((sections, CR, width), bf),
        pltpu.VMEM((req, KR, width), bf),
        pltpu.VMEM((GROUP, steps, heads, lat_w), bf),
        pltpu.VMEM((X, NPG, Z, HD, PS, lat_w), bf),
        pltpu.VMEM((X, NPG, Z, HD, PS, lat_w), bf),
        pltpu.VMEM((Z, HD, lat_w, vdim), bf),
        pltpu.VMEM((Z, NPG, PAIRS, PR, KD), bf),
        pltpu.VMEM((NPG, PAIRS, Z, PR, KD), bf),
        pltpu.VMEM((X, NPG, Z, PR, KD), bf),
        pltpu.VMEM((X, KD, NX), bf),
        pltpu.VMEM((Z, NPG, 2, PR, HX), bf),
        pltpu.VMEM((2, NPG, Z - 1, PR, HX), bf),
        pltpu.VMEM((NPG, 2, PS, NX), bf),
        pltpu.VMEM((2, NPG, PS, NX), bf),
        dma((4 + 3 * NPG,)),
        dma((sections,)), dma((sections,)),
        dma((Z,)), dma((Z,)), dma((4,)), dma((4,)), dma((1,)), dma((1,)),
        dma((X,)), dma((X,)), dma((4,)), dma((4,)), dma((1,)), dma((1,)),
        dma((NPG, X)), dma((NPG, X)), dma((NPG, Z)), dma((NPG, Z)),
        dma((NPG, X)), dma((NPG, X)), dma((2, NPG, Z)), dma((2, NPG, Z)),
        dma((NPG,)), dma((NPG,)),
    ]
    return kernel, scratch


def on_device(
    prompt_lengths, owner_map, block_table, pool_blocks, queries, new_latents, value_up, out_proj
):
    sections, devices = lax.axis_size("sect"), lax.axis_size("dev")
    steps, req, heads, width = queries.shape
    _, lat_w, vdim = value_up.shape
    model = out_proj.shape[1]
    block = pool_blocks.shape[2]
    kernel, scratch = make_kernel(
        sections, devices // CHIPS_X, CHIPS_X, steps, req, heads, lat_w, width, vdim, model, block
    )
    smem = pl.BlockSpec(memory_space=pltpu.SMEM)
    vmem = pl.BlockSpec(memory_space=pltpu.VMEM)
    hbm = pl.BlockSpec(memory_space=pl.ANY)
    return pl.pallas_call(
        kernel,
        out_shape=jax.ShapeDtypeStruct((steps, req, model), jnp.bfloat16),
        in_specs=[smem, smem, smem, hbm, hbm, vmem, hbm, hbm],
        out_specs=vmem,
        scratch_shapes=scratch,
        compiler_params=pltpu.CompilerParams(
            collective_id=0, has_side_effects=True, vmem_limit_bytes=60 * 1024 * 1024
        ),
    )(
        owner_map,
        jnp.swapaxes(block_table, 1, 2),
        prompt_lengths,
        pool_blocks,
        jnp.swapaxes(queries, 2, 3),
        new_latents,
        value_up,
        out_proj,
    )


def solution(mesh):
    in_specs = (
        P(None, "dev"),
        P(None, "dev"),
        P(None, "dev", None),
        P("sect", "dev", None, None),
        P(None, ("sect", "dev"), None, None),
        P(None, ("sect", "dev"), None),
        P("dev", None, None),
        P("dev", None),
    )
    out_specs = P(None, ("sect", "dev"), None)
    return jax.shard_map(
        on_device, mesh=mesh, in_specs=in_specs, out_specs=out_specs, check_vma=False
    )
```

```python
import jax
import jax.numpy as jnp
from jax import lax
from jax.experimental import pallas as pl
from jax.experimental.pallas import tpu as pltpu
from jax.sharding import PartitionSpec as P

MESH = pl.DeviceIdType.MESH
CHIPS_X = 4
GROUP = 4
score_scale = 192.0 ** (-0.5)
masked_score = -1e30


def ilog2(n):
    return n.bit_length() - 1


def tn_dot(a, b):
    return lax.dot_general(a, b, (((0,), (0,)), ((), ())), preferred_element_type=jnp.float32)


def mm(a, b):
    return jnp.dot(a, b, preferred_element_type=jnp.float32)


def make_kernel(sections, chips_z, chips_x, steps, req, heads, lat_w, width, vdim, model, block):
    Y, Z, X = sections // 2, chips_z, chips_x
    HD = heads // (Z * X)
    HZ = HD * X
    NPG = req // GROUP
    PS = GROUP * steps
    CR = 2 * block
    KR = CR + 16
    PAIRS = X // 2
    NX = model // 2
    HX = NX // 2
    PR = 2 * PS
    NT = 256
    KD = HD * vdim
    PV, PW = lat_w // (2 * Y), KD // (2 * Y)

    def kernel(
        owner_ref, table_ref, len_ref, pool_hbm, q_hbm, new_ref, vu_hbm, op_hbm, out_ref,
        pool, q, pk, keys, lat, snd, rcv, vu, val, vz, va, w, po, rs, so, fin,
        lsem, cs, cr, v1s, v1r, v2s, v2r, v3s, v3r, w1s, w1r, w2s, w2r, w3s, w3r,
        ls, lr, zs, zr, gs, gr, ss, sr, fs, fr,
    ):
        sect = lax.axis_index("sect")
        dev = lax.axis_index("dev")
        y, c = sect // 2, sect % 2
        z, x = dev // X, dev % X
        sibling = y * 2 + (1 - c)
        piece = c * Y + y
        pair, half = x // 2, x % 2
        sends = []

        hops = [(0, 0), (0, 1), (1, 0), (Y - 1, 0), (1, 1), (Y - 1, 1), (2, 0), (2, 1)]
        if Y == 2:
            hops = [(0, 0), (0, 1), (1, 0), (1, 1)]

        def hop(k):
            if isinstance(k, int):
                return hops[k]
            over, across = jnp.int32(0), jnp.int32(0)
            for i, (a, b) in enumerate(hops):
                over += jnp.where(k == i, a, 0)
                across += jnp.where(k == i, b, 0)
            return over, across

        def at_sect(k):
            over, across = hops[k]
            return ((y + over) % Y * 2 + (c + across) % 2, dev)

        def at_y(r):
            return (((y + r) % Y) * 2 + c, dev)

        def at_z(r):
            return (sect, ((z + r) % Z) * X + x)

        def at_x(r):
            return (sect, z * X + (x + r) % X)

        def remote(src, dst, send_sem, recv_sem, to):
            return pltpu.make_async_remote_copy(
                src_ref=src, dst_ref=dst, send_sem=send_sem, recv_sem=recv_sem,
                device_id=to, device_id_type=MESH,
            )

        def send(src, dst, send_sem, recv_sem, to):
            copy = remote(src, dst, send_sem, recv_sem, to)
            copy.start()
            sends.append(copy)

        def arrived(src, dst, send_sem, recv_sem, to):
            remote(src, dst, send_sem, recv_sem, to).wait_recv()

        load_pool = pltpu.make_async_copy(pool_hbm.at[0], pool, lsem.at[0])
        load_q = pltpu.make_async_copy(q_hbm, q, lsem.at[1])
        load_vu = pltpu.make_async_copy(vu_hbm, vu.at[0], lsem.at[2])
        own_cols = pl.ds(pl.multiple_of(half * NX, 128), NX)
        load_w = pltpu.make_async_copy(op_hbm.at[:, own_cols], w.at[0], lsem.at[3])
        load_pool.start()
        load_q.start()
        load_vu.start()
        load_w.start()

        barrier = pltpu.get_barrier_semaphore()
        peers = [at_sect(r) for r in range(1, sections)]
        peers += [at_z(r) for r in range(1, Z)] + [at_x(r) for r in range(1, X)]
        for peer in peers:
            pl.semaphore_signal(barrier, inc=1, device_id=peer, device_id_type=MESH)

        new_rows = new_ref[...].astype(jnp.float32).reshape(steps * req, width)
        new_rows = new_rows.astype(jnp.bfloat16)
        pick_u = lax.broadcasted_iota(jnp.int32, (16, steps * req), 0)
        pick_i = lax.broadcasted_iota(jnp.int32, (16, steps * req), 1)

        def slot_and_length(k):
            over, across = hop(k)
            source = lax.rem(y - over + Y, Y) * 2 + lax.rem(c + across, 2)
            slot, length = jnp.int32(0), jnp.int32(0)
            for i in range(req):
                owner = owner_ref[source, i]
                mine = lax.div(owner, req) == sect
                slot += jnp.where(mine, lax.rem(owner, req), 0)
                length += jnp.where(mine, len_ref[source, i], 0)
            return slot, length

        def fresh(k, carry):
            slot, _ = slot_and_length(k)
            pick = (pick_u == (pick_i >> ilog2(req))) & ((pick_i & (req - 1)) == slot)
            rows = mm(pick.astype(jnp.bfloat16), new_rows)
            keys[k, pl.ds(CR, 16), :] = rows.astype(jnp.bfloat16)
            return carry

        lax.fori_loop(0, req, fresh, 0)
        load_pool.wait()

        def pack(r):
            over, across = hop(r)
            target = lax.rem(y + over, Y) * 2 + lax.rem(c + across, 2)
            first, second = jnp.int32(0), jnp.int32(0)
            for i in range(req):
                hit = lax.div(owner_ref[sect, i], req) == target
                first += jnp.where(hit, table_ref[sect, 0, i], 0)
                second += jnp.where(hit, table_ref[sect, 1, i], 0)
            return pool[first], pool[second]

        def pack_remote(r, carry):
            a, b = pack(r)
            pk[r, 0:block, :] = a
            pk[r, block:CR, :] = b
            return carry

        lax.fori_loop(1, sections, pack_remote, 0)
        a, b = pack(0)
        keys[0, 0:block, :] = a
        keys[0, block:CR, :] = b

        pl.semaphore_wait(barrier, len(peers))

        def cache_args(r):
            return pk.at[r], keys.at[r, pl.ds(0, CR), :], cs.at[r], cr.at[r], at_sect(r)

        for r in range(1, sections):
            send(*cache_args(r))

        vrows = pl.ds(pl.multiple_of(piece * PV, PV), PV)
        wrows = pl.ds(pl.multiple_of(piece * PW, PW), PW)

        def v1_args(r):
            return vu_hbm.at[:, vrows, :], vu.at[r, :, vrows, :], v1s.at[r], v1r.at[r], at_z(r)

        def w1_args(r):
            cols = pl.ds(pl.multiple_of(((x + r) % X) % 2 * NX, 128), NX)
            return op_hbm.at[wrows, cols], w.at[r, wrows, :], w1s.at[r], w1r.at[r], at_x(r)

        def from_y(r, size, part, parts):
            start = (c * Y + (y - r + Y) % Y) * size + part * (size // parts)
            return pl.ds(pl.multiple_of(start, size // parts), size // parts)

        def v2_args(r, rows, slot):
            part = vu.at[pl.ds(1, Z - 1), :, rows, :]
            return part, part, v2s.at[slot], v2r.at[slot], at_y(r)

        def w2_args(r, rows, slot):
            part = w.at[pl.ds(1, X - 1), rows, :]
            return part, part, w2s.at[slot], w2r.at[slot], at_y(r)

        def y_start(args, size):
            send(*args(1, from_y(0, size, 0, 1), 0))
            if Y > 2:
                send(*args(Y - 1, from_y(0, size, 0, 1), 1))

        def v3_args(r, core):
            rows = pl.ds(pl.multiple_of((core * Y + (y - r + Y) % Y) * PV, PV), PV)
            part = vu.at[pl.ds(1, Z - 1), :, rows, :]
            return part, part, v3s.at[r], v3r.at[r], (sibling, dev)

        def w3_args(r, core):
            rows = pl.ds(pl.multiple_of((core * Y + (y - r + Y) % Y) * PW, PW), PW)
            part = w.at[pl.ds(1, X - 1), rows, :]
            return part, part, w3s.at[r], w3r.at[r], (sibling, dev)

        def y_forward(args, size, across):
            send(*across(0, c))
            arrived(*args(1, from_y(1, size, 0, 1), 0))
            if Y > 2:
                send(*args(1, from_y(1, size, 0, 2), 2))
                arrived(*args(Y - 1, from_y(Y - 1, size, 0, 1), 1))
                send(*args(Y - 1, from_y(Y - 1, size, 1, 2), 3))
                send(*across(Y - 1, c))
            send(*across(1, c))

        def y_finish(args, size, across):
            if Y > 2:
                arrived(*args(1, from_y(2, size, 0, 2), 2))
                arrived(*args(Y - 1, from_y(2, size, 1, 2), 3))
                send(*across(2, c))

        for r in range(1, Z):
            send(*v1_args(r))
        for r in range(1, X):
            send(*w1_args(r))

        swap_out = lax.broadcasted_iota(jnp.int32, (HZ * PS, HZ * PS), 0)
        swap_in = lax.broadcasted_iota(jnp.int32, (HZ * PS, HZ * PS), 1)
        swap = ((swap_out >> ilog2(PS)) == (swap_in & (HZ - 1))) & (
            (swap_out & (PS - 1)) == (swap_in >> ilog2(HZ))
        )
        swap = swap.astype(jnp.bfloat16)
        load_q.wait()

        def attend(k, k4):
            slot, length = slot_and_length(k)
            key_rows = keys[k]
            key_lat = keys[k, :, 0:lat_w]
            q_cols = jnp.concatenate([q[s, slot] for s in range(steps)], axis=1)
            scores = mm(key_rows, q_cols) * score_scale
            row = lax.broadcasted_iota(jnp.int32, scores.shape, 0)
            step = lax.broadcasted_iota(jnp.int32, scores.shape, 1) >> ilog2(heads)
            held = jnp.where(row < CR, length, CR + 1 + step)
            scores = jnp.where(row < held, scores, masked_score)
            weights = jnp.exp(scores - jnp.max(scores, axis=0, keepdims=True))
            probs = weights * (1.0 / jnp.sum(weights, axis=0, keepdims=True))
            out = tn_dot(probs.astype(jnp.bfloat16), key_lat).astype(jnp.bfloat16)
            lat[k4] = out.reshape(steps, heads, lat_w)

        def latent_args(r, pg):
            to = (x + r) % X
            return snd.at[to, pg], rcv.at[x, pg], ls.at[pg, r], lr.at[pg, r], at_x(r)

        def latent_from(r, pg):
            source = (x - r + X) % X
            return snd.at[source, pg], rcv.at[source, pg], ls.at[pg, r], lr.at[pg, r], at_x(r)

        local_latents = []

        def attention(pg):
            def one(k4, carry):
                k = pg * GROUP + k4

                @pl.when(k > 0)
                def _():
                    arrived(pk.at[k], keys.at[k, pl.ds(0, CR), :], cs.at[k], cr.at[k], at_sect(1))

                attend(k, k4)
                return carry

            lax.fori_loop(0, GROUP, one, 0)

            def turn(zz, carry):
                part = lat[:, :, pl.ds(pl.multiple_of(zz * HZ, HZ), HZ), :]
                turned = mm(swap, part.reshape(PS * HZ, lat_w)).astype(jnp.bfloat16)
                snd[:, pg, zz] = turned.reshape(X, HD, PS, lat_w)
                return carry

            lax.fori_loop(0, Z, turn, 0)
            for r in range(1, X):
                send(*latent_args(r, pg))
            own = pltpu.make_async_copy(snd.at[x, pg], rcv.at[x, pg], lsem.at[4 + pg])
            own.start()
            local_latents.append(own)

        def value_args(r, pg):
            to = (z + r) % Z
            return val.at[to, pg], vz.at[pg, :, z], zs.at[pg, r], zr.at[pg, r], at_z(r)

        def value_from(r, pg):
            source = (z - r + Z) % Z
            return val.at[source, pg], vz.at[pg, :, source], zs.at[pg, r], zr.at[pg, r], at_z(r)

        local_values = []

        def values(pg):
            for r in range(1, X):
                arrived(*latent_from(r, pg))
            local_latents[pg].wait()

            def ring(r, carry):
                zz = lax.rem(z - r + Z, Z)
                for hh in range(HD):
                    rows = rcv[:, pg, zz, hh].reshape(X * PS, lat_w)
                    part = mm(rows, vu[r, hh]).astype(jnp.bfloat16)
                    val[zz, pg, :, :, hh * vdim : (hh + 1) * vdim] = part.reshape(PAIRS, PR, vdim)
                return carry

            lax.fori_loop(0, Z, ring, 0)
            for r in range(1, Z):
                send(*value_args(r, pg))
            own = pltpu.make_async_copy(val.at[z, pg], vz.at[pg, :, z], lsem.at[4 + NPG + pg])
            own.start()
            local_values.append(own)

        def gather_args(r, pg):
            to = ((x + r) % X) // 2
            return vz.at[pg, to], va.at[r, pg], gs.at[pg, r], gr.at[pg, r], at_x(r)

        def gather_start(pg):
            for r in range(1, Z):
                arrived(*value_from(r, pg))
            local_values[pg].wait()
            for r in range(1, X):
                send(*gather_args(r, pg))

        def ring_args(d, m, i, pg):
            sign = 1 - 2 * d
            target = (z - sign * (1 + i) + Z) % Z
            held = po.at[target, pg, d, m] if i == 0 else rs.at[d, pg, i - 1, m]
            sem = 2 * d + m
            return held, rs.at[d, pg, i, m], ss.at[sem, pg, i], sr.at[sem, pg, i], at_z(sign + Z)

        def ring_step(i, pg):
            for m in range(2):
                for d in range(2):
                    arrived(*ring_args(d, m, i - 1, pg))
                    target = (z - (1 - 2 * d) * (1 + i) + 2 * Z) % Z
                    total = rs[d, pg, i - 1, m].astype(jnp.float32)
                    total += po[target, pg, d, m].astype(jnp.float32)
                    rs[d, pg, i - 1, m] = total.astype(jnp.bfloat16)
                    send(*ring_args(d, m, i, pg))

        def project(pg):
            for r in range(1, X):
                arrived(*gather_args(r, pg))
            for d in range(2):

                def tile(n, carry):
                    cols = pl.ds(pl.multiple_of(d * HX + n * NT, NT), NT)
                    acc = mm(vz[pg, pair].reshape(Z * PR, KD), w[0, :, cols])
                    for r in range(1, X):
                        acc += mm(va[r, pg].reshape(Z * PR, KD), w[r, :, cols])
                    part = acc.astype(jnp.bfloat16).reshape(Z, 2, PS, NT)
                    po[:, pg, d, :, :, pl.ds(pl.multiple_of(n * NT, NT), NT)] = part
                    return carry

                lax.fori_loop(0, HX // NT, tile, 0)
                for m in range(2):
                    send(*ring_args(d, m, 0, pg))

        def final_args(pg, side):
            return so.at[pg, 1 - side], fin.at[side, pg], fs.at[pg], fr.at[pg], at_x(1 - 2 * half + X)

        local_final = []

        def reduce(pg):
            for m in range(2):
                for d in range(2):
                    arrived(*ring_args(d, m, Z - 2, pg))
                    total = po[z, pg, d, m].astype(jnp.float32)
                    total += rs[d, pg, Z - 2, m].astype(jnp.float32)
                    so[pg, m, :, pl.ds(d * HX, HX)] = total.astype(jnp.bfloat16)
            send(*final_args(pg, half))
            own = pltpu.make_async_copy(so.at[pg, half], fin.at[half, pg], lsem.at[4 + 2 * NPG + pg])
            own.start()
            local_final.append(own)

        attention(0)
        for r in range(1, Z):
            arrived(*v1_args(r))
        y_start(v2_args, PV)
        for pg in range(1, NPG):
            attention(pg)
        y_forward(v2_args, PV, v3_args)
        for r in range(1, X):
            arrived(*w1_args(r))
        y_start(w2_args, PW)
        load_vu.wait()
        y_finish(v2_args, PV, v3_args)
        for r in range(Y):
            arrived(*v3_args(r, 1 - c))
        values(0)
        gather_start(0)
        y_forward(w2_args, PW, w3_args)
        for pg in range(1, NPG):
            values(pg)
            gather_start(pg)
        load_w.wait()
        y_finish(w2_args, PW, w3_args)
        for r in range(Y):
            arrived(*w3_args(r, 1 - c))
        first = Z // 4 + 1
        project(0)
        if NPG == 1:
            for i in range(1, Z - 1):
                ring_step(i, 0)
        else:
            for i in range(1, first):
                ring_step(i, 0)
            project(1)
            for i in range(1, Z - 1):
                if first <= i + first - 1 < Z - 1:
                    ring_step(i + first - 1, 0)
                elif i + first - 1 == Z - 1:
                    reduce(0)
                ring_step(i, 1)
        reduce(NPG - 1)

        place_out = lax.broadcasted_iota(jnp.int32, (steps * req, steps * req), 0)
        place_in = lax.broadcasted_iota(jnp.int32, (steps * req, steps * req), 1)
        slots = jnp.zeros((steps * req, steps * req), jnp.int32)
        for k in range(req):
            slot, _ = slot_and_length(k)
            slots = jnp.where((place_in >> ilog2(steps)) == k, slot, slots)
        place = ((place_out >> ilog2(req)) == (place_in & (steps - 1))) & (
            (place_out & (req - 1)) == slots
        )
        place = place.astype(jnp.bfloat16)
        for pg in range(NPG):
            arrived(*final_args(pg, 1 - half))
            local_final[pg].wait()
        for side in range(2):
            rows = mm(place, fin[side].reshape(NPG * PS, NX))
            for s in range(steps):
                part = rows[s * req : (s + 1) * req].astype(jnp.bfloat16)
                out_ref[s, :, side * NX : (side + 1) * NX] = part

        for copy in sends:
            copy.wait_send()

    bf = jnp.bfloat16
    dma = pltpu.SemaphoreType.DMA
    scratch = [
        pltpu.VMEM((2 * req, block, width), bf),
        pltpu.VMEM((steps, req, width, heads), bf),
        pltpu.VMEM((sections, CR, width), bf),
        pltpu.VMEM((req, KR, width), bf),
        pltpu.VMEM((GROUP, steps, heads, lat_w), bf),
        pltpu.VMEM((X, NPG, Z, HD, PS, lat_w), bf),
        pltpu.VMEM((X, NPG, Z, HD, PS, lat_w), bf),
        pltpu.VMEM((Z, HD, lat_w, vdim), bf),
        pltpu.VMEM((Z, NPG, PAIRS, PR, KD), bf),
        pltpu.VMEM((NPG, PAIRS, Z, PR, KD), bf),
        pltpu.VMEM((X, NPG, Z, PR, KD), bf),
        pltpu.VMEM((X, KD, NX), bf),
        pltpu.VMEM((Z, NPG, 2, 2, PS, HX), bf),
        pltpu.VMEM((2, NPG, Z - 1, 2, PS, HX), bf),
        pltpu.VMEM((NPG, 2, PS, NX), bf),
        pltpu.VMEM((2, NPG, PS, NX), bf),
        dma((4 + 3 * NPG,)),
        dma((sections,)), dma((sections,)),
        dma((Z,)), dma((Z,)), dma((4,)), dma((4,)), dma((Y,)), dma((Y,)),
        dma((X,)), dma((X,)), dma((4,)), dma((4,)), dma((Y,)), dma((Y,)),
        dma((NPG, X)), dma((NPG, X)), dma((NPG, Z)), dma((NPG, Z)),
        dma((NPG, X)), dma((NPG, X)), dma((4, NPG, Z)), dma((4, NPG, Z)),
        dma((NPG,)), dma((NPG,)),
    ]
    return kernel, scratch


def on_device(
    prompt_lengths, owner_map, block_table, pool_blocks, queries, new_latents, value_up, out_proj
):
    sections, devices = lax.axis_size("sect"), lax.axis_size("dev")
    steps, req, heads, width = queries.shape
    _, lat_w, vdim = value_up.shape
    model = out_proj.shape[1]
    block = pool_blocks.shape[2]
    kernel, scratch = make_kernel(
        sections, devices // CHIPS_X, CHIPS_X, steps, req, heads, lat_w, width, vdim, model, block
    )
    smem = pl.BlockSpec(memory_space=pltpu.SMEM)
    vmem = pl.BlockSpec(memory_space=pltpu.VMEM)
    hbm = pl.BlockSpec(memory_space=pl.ANY)
    return pl.pallas_call(
        kernel,
        out_shape=jax.ShapeDtypeStruct((steps, req, model), jnp.bfloat16),
        in_specs=[smem, smem, smem, hbm, hbm, vmem, hbm, hbm],
        out_specs=vmem,
        scratch_shapes=scratch,
        compiler_params=pltpu.CompilerParams(
            collective_id=0, has_side_effects=True, vmem_limit_bytes=60 * 1024 * 1024
        ),
    )(
        owner_map,
        jnp.swapaxes(block_table, 1, 2),
        prompt_lengths,
        pool_blocks,
        jnp.swapaxes(queries, 2, 3),
        new_latents,
        value_up,
        out_proj,
    )


def solution(mesh):
    in_specs = (
        P(None, "dev"),
        P(None, "dev"),
        P(None, "dev", None),
        P("sect", "dev", None, None),
        P(None, ("sect", "dev"), None, None),
        P(None, ("sect", "dev"), None),
        P("dev", None, None),
        P("dev", None),
    )
    out_specs = P(None, ("sect", "dev"), None)
    return jax.shard_map(
        on_device, mesh=mesh, in_specs=in_specs, out_specs=out_specs, check_vma=False
    )
```

```python
import jax
import jax.numpy as jnp
from jax import lax
from jax.experimental import pallas as pl
from jax.experimental.pallas import tpu as pltpu
from jax.sharding import PartitionSpec as P

MESH = pl.DeviceIdType.MESH
CHIPS_X = 4
GROUP = 2
score_scale = 192.0 ** (-0.5)
masked_score = -1e30


def ilog2(n):
    return n.bit_length() - 1


def tn_dot(a, b):
    return lax.dot_general(a, b, (((0,), (0,)), ((), ())), preferred_element_type=jnp.float32)


def mm(a, b):
    return jnp.dot(a, b, preferred_element_type=jnp.float32)


def make_kernel(sections, chips_z, chips_x, steps, req, heads, lat_w, width, vdim, model, block):
    Y, Z, X = sections // 2, chips_z, chips_x
    HD = heads // (Z * X)
    HZ = HD * X
    NG = req // GROUP
    NPG = NG // 2
    PS = GROUP * steps
    CR = 2 * block
    KR = CR + 16
    PAIRS = X // 2
    NX = model // 2
    HX = NX // 2
    PR = 2 * PS
    NT = 256
    KD = HD * vdim
    PV, PW = lat_w // (2 * Y), KD // (2 * Y)

    def kernel(
        owner_ref, table_ref, len_ref, pool_hbm, q_hbm, new_ref, vu_hbm, op_hbm, out_ref,
        pool, q, pk, keys, lat, snd, rcv, vu, val, vz, va, w, po, rs, so, fin,
        lsem, cs, cr, v1s, v1r, v2s, v2r, v3s, v3r, w1s, w1r, w2s, w2r, w3s, w3r,
        ls, lr, zs, zr, gs, gr, ss, sr, fs, fr,
    ):
        sect = lax.axis_index("sect")
        dev = lax.axis_index("dev")
        y, c = sect // 2, sect % 2
        z, x = dev // X, dev % X
        sibling = y * 2 + (1 - c)
        piece = c * Y + y
        pair, half = x // 2, x % 2
        sends = []

        hops = [(0, 0), (0, 1), (1, 0), (Y - 1, 0), (1, 1), (Y - 1, 1), (2, 0), (2, 1)]
        if Y == 2:
            hops = [(0, 0), (0, 1), (1, 0), (1, 1)]

        def hop(k):
            if isinstance(k, int):
                return hops[k]
            over, across = jnp.int32(0), jnp.int32(0)
            for i, (a, b) in enumerate(hops):
                over += jnp.where(k == i, a, 0)
                across += jnp.where(k == i, b, 0)
            return over, across

        def at_sect(k):
            over, across = hops[k]
            return ((y + over) % Y * 2 + (c + across) % 2, dev)

        def at_y(r):
            return (((y + r) % Y) * 2 + c, dev)

        def at_z(r):
            return (sect, ((z + r) % Z) * X + x)

        def at_x(r):
            return (sect, z * X + (x + r) % X)

        def remote(src, dst, send_sem, recv_sem, to):
            return pltpu.make_async_remote_copy(
                src_ref=src, dst_ref=dst, send_sem=send_sem, recv_sem=recv_sem,
                device_id=to, device_id_type=MESH,
            )

        def send(src, dst, send_sem, recv_sem, to):
            copy = remote(src, dst, send_sem, recv_sem, to)
            copy.start()
            sends.append(copy)

        def arrived(src, dst, send_sem, recv_sem, to):
            remote(src, dst, send_sem, recv_sem, to).wait_recv()

        load_pool = pltpu.make_async_copy(pool_hbm.at[0], pool, lsem.at[0])
        load_q = pltpu.make_async_copy(q_hbm, q, lsem.at[1])
        load_vu = pltpu.make_async_copy(vu_hbm, vu.at[0], lsem.at[2])
        own_cols = pl.ds(pl.multiple_of(half * NX, 128), NX)
        load_w = pltpu.make_async_copy(op_hbm.at[:, own_cols], w.at[0], lsem.at[3])
        load_pool.start()
        load_q.start()
        load_vu.start()
        load_w.start()

        barrier = pltpu.get_barrier_semaphore()
        peers = [at_sect(r) for r in range(1, sections)]
        peers += [at_z(r) for r in range(1, Z)] + [at_x(r) for r in range(1, X)]
        for peer in peers:
            pl.semaphore_signal(barrier, inc=1, device_id=peer, device_id_type=MESH)

        new_rows = new_ref[...].astype(jnp.float32).reshape(steps * req, width)
        new_rows = new_rows.astype(jnp.bfloat16)
        pick_u = lax.broadcasted_iota(jnp.int32, (16, steps * req), 0)
        pick_i = lax.broadcasted_iota(jnp.int32, (16, steps * req), 1)

        def slot_and_length(k):
            over, across = hop(k)
            source = lax.rem(y - over + Y, Y) * 2 + lax.rem(c + across, 2)
            slot, length = jnp.int32(0), jnp.int32(0)
            for i in range(req):
                owner = owner_ref[source, i]
                mine = lax.div(owner, req) == sect
                slot += jnp.where(mine, lax.rem(owner, req), 0)
                length += jnp.where(mine, len_ref[source, i], 0)
            return slot, length

        def fresh(k, carry):
            slot, _ = slot_and_length(k)
            pick = (pick_u == (pick_i >> ilog2(req))) & ((pick_i & (req - 1)) == slot)
            rows = mm(pick.astype(jnp.bfloat16), new_rows)
            keys[k, pl.ds(CR, 16), :] = rows.astype(jnp.bfloat16)
            return carry

        lax.fori_loop(0, req, fresh, 0)
        load_pool.wait()

        def pack(r):
            over, across = hop(r)
            target = lax.rem(y + over, Y) * 2 + lax.rem(c + across, 2)
            first, second = jnp.int32(0), jnp.int32(0)
            for i in range(req):
                hit = lax.div(owner_ref[sect, i], req) == target
                first += jnp.where(hit, table_ref[sect, 0, i], 0)
                second += jnp.where(hit, table_ref[sect, 1, i], 0)
            return pool[first], pool[second]

        def pack_remote(r, carry):
            a, b = pack(r)
            pk[r, 0:block, :] = a
            pk[r, block:CR, :] = b
            return carry

        lax.fori_loop(1, sections, pack_remote, 0)
        a, b = pack(0)
        keys[0, 0:block, :] = a
        keys[0, block:CR, :] = b

        pl.semaphore_wait(barrier, len(peers))

        def cache_args(r):
            return pk.at[r], keys.at[r, pl.ds(0, CR), :], cs.at[r], cr.at[r], at_sect(r)

        for r in range(1, sections):
            send(*cache_args(r))

        vrows = pl.ds(pl.multiple_of(piece * PV, PV), PV)
        wrows = pl.ds(pl.multiple_of(piece * PW, PW), PW)

        def v1_args(r):
            return vu_hbm.at[:, vrows, :], vu.at[r, :, vrows, :], v1s.at[r], v1r.at[r], at_z(r)

        def w1_args(r):
            cols = pl.ds(pl.multiple_of(((x + r) % X) % 2 * NX, 128), NX)
            return op_hbm.at[wrows, cols], w.at[r, wrows, :], w1s.at[r], w1r.at[r], at_x(r)

        def from_y(r, size, part, parts):
            start = (c * Y + (y - r + Y) % Y) * size + part * (size // parts)
            return pl.ds(pl.multiple_of(start, size // parts), size // parts)

        def v2_args(r, rows, slot):
            part = vu.at[pl.ds(1, Z - 1), :, rows, :]
            return part, part, v2s.at[slot], v2r.at[slot], at_y(r)

        def w2_args(r, rows, slot):
            part = w.at[pl.ds(1, X - 1), rows, :]
            return part, part, w2s.at[slot], w2r.at[slot], at_y(r)

        def y_start(args, size):
            send(*args(1, from_y(0, size, 0, 1), 0))
            if Y > 2:
                send(*args(Y - 1, from_y(0, size, 0, 1), 1))

        def v3_args(r, core):
            rows = pl.ds(pl.multiple_of((core * Y + (y - r + Y) % Y) * PV, PV), PV)
            part = vu.at[pl.ds(1, Z - 1), :, rows, :]
            return part, part, v3s.at[r], v3r.at[r], (sibling, dev)

        def w3_args(r, core):
            rows = pl.ds(pl.multiple_of((core * Y + (y - r + Y) % Y) * PW, PW), PW)
            part = w.at[pl.ds(1, X - 1), rows, :]
            return part, part, w3s.at[r], w3r.at[r], (sibling, dev)

        def y_forward(args, size, across):
            send(*across(0, c))
            arrived(*args(1, from_y(1, size, 0, 1), 0))
            if Y > 2:
                send(*args(1, from_y(1, size, 0, 2), 2))
                arrived(*args(Y - 1, from_y(Y - 1, size, 0, 1), 1))
                send(*args(Y - 1, from_y(Y - 1, size, 1, 2), 3))
                send(*across(Y - 1, c))
            send(*across(1, c))

        def y_finish(args, size, across):
            if Y > 2:
                arrived(*args(1, from_y(2, size, 0, 2), 2))
                arrived(*args(Y - 1, from_y(2, size, 1, 2), 3))
                send(*across(2, c))

        for r in range(1, Z):
            send(*v1_args(r))
        for r in range(1, X):
            send(*w1_args(r))

        swap_out = lax.broadcasted_iota(jnp.int32, (HZ * PS, HZ * PS), 0)
        swap_in = lax.broadcasted_iota(jnp.int32, (HZ * PS, HZ * PS), 1)
        swap = ((swap_out >> ilog2(PS)) == (swap_in & (HZ - 1))) & (
            (swap_out & (PS - 1)) == (swap_in >> ilog2(HZ))
        )
        swap = swap.astype(jnp.bfloat16)
        load_q.wait()

        def attend(k, k4):
            slot, length = slot_and_length(k)
            key_rows = keys[k]
            key_lat = keys[k, :, 0:lat_w]
            q_cols = jnp.concatenate([q[s, slot] for s in range(steps)], axis=1)
            scores = mm(key_rows, q_cols) * score_scale
            row = lax.broadcasted_iota(jnp.int32, scores.shape, 0)
            step = lax.broadcasted_iota(jnp.int32, scores.shape, 1) >> ilog2(heads)
            held = jnp.where(row < CR, length, CR + 1 + step)
            scores = jnp.where(row < held, scores, masked_score)
            weights = jnp.exp(scores - jnp.max(scores, axis=0, keepdims=True))
            probs = weights * (1.0 / jnp.sum(weights, axis=0, keepdims=True))
            out = tn_dot(probs.astype(jnp.bfloat16), key_lat).astype(jnp.bfloat16)
            lat[k4] = out.reshape(steps, heads, lat_w)

        def latent_args(r, pg):
            to = (x + r) % X
            return snd.at[to, pg], rcv.at[x, pg], ls.at[pg, r], lr.at[pg, r], at_x(r)

        def latent_from(r, pg):
            source = (x - r + X) % X
            return snd.at[source, pg], rcv.at[source, pg], ls.at[pg, r], lr.at[pg, r], at_x(r)

        local_latents = []

        def attention(pg):
            def one(k4, carry):
                k = pg * GROUP + k4

                @pl.when(k > 0)
                def _():
                    arrived(pk.at[k], keys.at[k, pl.ds(0, CR), :], cs.at[k], cr.at[k], at_sect(1))

                attend(k, k4)
                return carry

            lax.fori_loop(0, GROUP, one, 0)

            def turn(zz, carry):
                part = lat[:, :, pl.ds(pl.multiple_of(zz * HZ, HZ), HZ), :]
                turned = mm(swap, part.reshape(PS * HZ, lat_w)).astype(jnp.bfloat16)
                snd[:, pg, zz] = turned.reshape(X, HD * PS, lat_w)
                return carry

            lax.fori_loop(0, Z, turn, 0)
            for r in range(1, X):
                send(*latent_args(r, pg))
            own = pltpu.make_async_copy(snd.at[x, pg], rcv.at[x, pg], lsem.at[4 + pg])
            own.start()
            local_latents.append(own)

        def value_args(r, pg):
            to = (z + r) % Z
            return val.at[to, pg], vz.at[pg, :, z], zs.at[pg, r], zr.at[pg, r], at_z(r)

        def value_from(r, pg):
            source = (z - r + Z) % Z
            return val.at[source, pg], vz.at[pg, :, source], zs.at[pg, r], zr.at[pg, r], at_z(r)

        local_values = []

        def values(pg):
            for r in range(1, X):
                arrived(*latent_from(r, pg))
            local_latents[pg].wait()

            def ring(r, carry):
                zz = lax.rem(z - r + Z, Z)
                maps = jnp.concatenate([vu[r, hh] for hh in range(HD)], axis=1)
                full = mm(rcv[:, pg, zz].reshape(X * HD * PS, lat_w), maps)
                full = full.reshape(X, HD, PS, KD)
                for hh in range(HD):
                    cols = slice(hh * vdim, (hh + 1) * vdim)
                    part = full[:, hh, :, cols].reshape(PAIRS, PR, vdim).astype(jnp.bfloat16)
                    val[zz, pg, :, :, cols] = part
                return carry

            lax.fori_loop(0, Z, ring, 0)
            for r in range(1, Z):
                send(*value_args(r, pg))
            own = pltpu.make_async_copy(val.at[z, pg], vz.at[pg, :, z], lsem.at[4 + NG + pg])
            own.start()
            local_values.append(own)

        def gather_args(r, pg):
            to = ((x + r) % X) // 2
            return vz.at[pg, to], va.at[r, pg], gs.at[pg, r], gr.at[pg, r], at_x(r)

        def gather_start(pg):
            for r in range(1, Z):
                arrived(*value_from(r, pg))
            local_values[pg].wait()
            for r in range(1, X):
                send(*gather_args(r, pg))

        def ring_args(d, m, i, pg):
            sign = 1 - 2 * d
            target = (z - sign * (1 + i) + Z) % Z
            held = po.at[target, pg, d, m] if i == 0 else rs.at[d, pg, i - 1, m]
            sem = 2 * d + m
            return held, rs.at[d, pg, i, m], ss.at[sem, pg, i], sr.at[sem, pg, i], at_z(sign + Z)

        def ring_step(i, pg):
            for m in range(2):
                for d in range(2):
                    arrived(*ring_args(d, m, i - 1, pg))
                    target = (z - (1 - 2 * d) * (1 + i) + 2 * Z) % Z
                    total = rs[d, pg, i - 1, m].astype(jnp.float32)
                    total += po[target, pg, d, m].astype(jnp.float32)
                    rs[d, pg, i - 1, m] = total.astype(jnp.bfloat16)
                    send(*ring_args(d, m, i, pg))

        def project(pg):
            groups = pl.ds(2 * pg, 2)
            for g in range(2 * pg, 2 * pg + 2):
                for r in range(1, X):
                    arrived(*gather_args(r, g))
            for d in range(2):

                def tile(n, carry):
                    cols = pl.ds(pl.multiple_of(d * HX + n * NT, NT), NT)
                    acc = mm(vz[groups, pair].reshape(2 * Z * PR, KD), w[0, :, cols])
                    for r in range(1, X):
                        acc += mm(va[r, groups].reshape(2 * Z * PR, KD), w[r, :, cols])
                    part = acc.astype(jnp.bfloat16).reshape(2, Z, PR, NT)
                    cols = pl.ds(pl.multiple_of(n * NT, NT), NT)
                    for g in range(2):
                        po[:, pg, d, g, :, cols] = part[g]
                    return carry

                lax.fori_loop(0, HX // NT, tile, 0)
                for m in range(2):
                    send(*ring_args(d, m, 0, pg))

        def final_args(pg, side):
            return so.at[pg, 1 - side], fin.at[side, pg], fs.at[pg], fr.at[pg], at_x(1 - 2 * half + X)

        local_final = []

        def reduce(pg):
            for d in range(2):
                totals = []
                for g in range(2):
                    arrived(*ring_args(d, g, Z - 2, pg))
                    total = po[z, pg, d, g].astype(jnp.float32)
                    totals.append(total + rs[d, pg, Z - 2, g].astype(jnp.float32))
                for m in range(2):
                    rows = jnp.concatenate([t[m * PS : (m + 1) * PS] for t in totals], axis=0)
                    so[pg, m, :, pl.ds(d * HX, HX)] = rows.astype(jnp.bfloat16)
            send(*final_args(pg, half))
            own = pltpu.make_async_copy(so.at[pg, half], fin.at[half, pg], lsem.at[4 + 2 * NG + pg])
            own.start()
            local_final.append(own)

        for g in range(NG // 2):
            attention(g)
        for r in range(1, Z):
            arrived(*v1_args(r))
        y_start(v2_args, PV)
        for g in range(NG // 2, NG):
            attention(g)
        y_forward(v2_args, PV, v3_args)
        for r in range(1, X):
            arrived(*w1_args(r))
        y_start(w2_args, PW)
        load_vu.wait()
        y_finish(v2_args, PV, v3_args)
        for r in range(Y):
            arrived(*v3_args(r, 1 - c))
        for g in range(NG):
            values(g)
            if g:
                gather_start(g - 1)
            if g == 1:
                y_forward(w2_args, PW, w3_args)
        load_w.wait()
        y_finish(w2_args, PW, w3_args)
        gather_start(NG - 1)
        for r in range(Y):
            arrived(*w3_args(r, 1 - c))
        first = Z // 4 + 1
        project(0)
        if NPG == 1:
            for i in range(1, Z - 1):
                ring_step(i, 0)
        else:
            for i in range(1, first):
                ring_step(i, 0)
            project(1)
            for i in range(1, Z - 1):
                if first <= i + first - 1 < Z - 1:
                    ring_step(i + first - 1, 0)
                elif i + first - 1 == Z - 1:
                    reduce(0)
                ring_step(i, 1)
        reduce(NPG - 1)

        place_out = lax.broadcasted_iota(jnp.int32, (steps * req, steps * req), 0)
        place_in = lax.broadcasted_iota(jnp.int32, (steps * req, steps * req), 1)
        slots = jnp.zeros((steps * req, steps * req), jnp.int32)
        for k in range(req):
            slot, _ = slot_and_length(k)
            slots = jnp.where((place_in >> ilog2(steps)) == k, slot, slots)
        place = ((place_out >> ilog2(req)) == (place_in & (steps - 1))) & (
            (place_out & (req - 1)) == slots
        )
        place = place.astype(jnp.bfloat16)
        for pg in range(NPG):
            arrived(*final_args(pg, 1 - half))
            local_final[pg].wait()
        for side in range(2):
            rows = mm(place, fin[side].reshape(steps * req, NX))
            for s in range(steps):
                part = rows[s * req : (s + 1) * req].astype(jnp.bfloat16)
                out_ref[s, :, side * NX : (side + 1) * NX] = part

        for copy in sends:
            copy.wait_send()

    bf = jnp.bfloat16
    dma = pltpu.SemaphoreType.DMA
    scratch = [
        pltpu.VMEM((2 * req, block, width), bf),
        pltpu.VMEM((steps, req, width, heads), bf),
        pltpu.VMEM((sections, CR, width), bf),
        pltpu.VMEM((req, KR, width), bf),
        pltpu.VMEM((GROUP, steps, heads, lat_w), bf),
        pltpu.VMEM((X, NG, Z, HD * PS, lat_w), bf),
        pltpu.VMEM((X, NG, Z, HD * PS, lat_w), bf),
        pltpu.VMEM((Z, HD, lat_w, vdim), bf),
        pltpu.VMEM((Z, NG, PAIRS, PR, KD), bf),
        pltpu.VMEM((NG, PAIRS, Z, PR, KD), bf),
        pltpu.VMEM((X, NG, Z, PR, KD), bf),
        pltpu.VMEM((X, KD, NX), bf),
        pltpu.VMEM((Z, NPG, 2, 2, PR, HX), bf),
        pltpu.VMEM((2, NPG, Z - 1, 2, PR, HX), bf),
        pltpu.VMEM((NPG, 2, 2 * PS, NX), bf),
        pltpu.VMEM((2, NPG, 2 * PS, NX), bf),
        dma((4 + 2 * NG + NPG,)),
        dma((sections,)), dma((sections,)),
        dma((Z,)), dma((Z,)), dma((4,)), dma((4,)), dma((Y,)), dma((Y,)),
        dma((X,)), dma((X,)), dma((4,)), dma((4,)), dma((Y,)), dma((Y,)),
        dma((NG, X)), dma((NG, X)), dma((NG, Z)), dma((NG, Z)),
        dma((NG, X)), dma((NG, X)), dma((4, NPG, Z)), dma((4, NPG, Z)),
        dma((NPG,)), dma((NPG,)),
    ]
    return kernel, scratch


def on_device(
    prompt_lengths, owner_map, block_table, pool_blocks, queries, new_latents, value_up, out_proj
):
    sections, devices = lax.axis_size("sect"), lax.axis_size("dev")
    steps, req, heads, width = queries.shape
    _, lat_w, vdim = value_up.shape
    model = out_proj.shape[1]
    block = pool_blocks.shape[2]
    kernel, scratch = make_kernel(
        sections, devices // CHIPS_X, CHIPS_X, steps, req, heads, lat_w, width, vdim, model, block
    )
    smem = pl.BlockSpec(memory_space=pltpu.SMEM)
    vmem = pl.BlockSpec(memory_space=pltpu.VMEM)
    hbm = pl.BlockSpec(memory_space=pl.ANY)
    return pl.pallas_call(
        kernel,
        out_shape=jax.ShapeDtypeStruct((steps, req, model), jnp.bfloat16),
        in_specs=[smem, smem, smem, hbm, hbm, vmem, hbm, hbm],
        out_specs=vmem,
        scratch_shapes=scratch,
        compiler_params=pltpu.CompilerParams(
            collective_id=0, has_side_effects=True, vmem_limit_bytes=60 * 1024 * 1024
        ),
    )(
        owner_map,
        jnp.swapaxes(block_table, 1, 2),
        prompt_lengths,
        pool_blocks,
        jnp.swapaxes(queries, 2, 3),
        new_latents,
        value_up,
        out_proj,
    )


def solution(mesh):
    in_specs = (
        P(None, "dev"),
        P(None, "dev"),
        P(None, "dev", None),
        P("sect", "dev", None, None),
        P(None, ("sect", "dev"), None, None),
        P(None, ("sect", "dev"), None),
        P("dev", None, None),
        P("dev", None),
    )
    out_specs = P(None, ("sect", "dev"), None)
    return jax.shard_map(
        on_device, mesh=mesh, in_specs=in_specs, out_specs=out_specs, check_vma=False
    )
```

```python
import jax
import jax.numpy as jnp
from jax import lax
from jax.experimental import pallas as pl
from jax.experimental.pallas import tpu as pltpu
from jax.sharding import PartitionSpec as P

MESH = pl.DeviceIdType.MESH
CHIPS_X = 4
GROUP = 2
score_scale = 192.0 ** (-0.5)
masked_score = -1e30


def ilog2(n):
    return n.bit_length() - 1


def tn_dot(a, b):
    return lax.dot_general(a, b, (((0,), (0,)), ((), ())), preferred_element_type=jnp.float32)


def mm(a, b):
    return jnp.dot(a, b, preferred_element_type=jnp.float32)


def make_kernel(sections, chips_z, chips_x, steps, req, heads, lat_w, width, vdim, model, block):
    Y, Z, X = sections // 2, chips_z, chips_x
    HD = heads // (Z * X)
    HZ = HD * X
    NG = req // GROUP
    NPG = NG // 2
    PS = GROUP * steps
    CR = 2 * block
    KR = CR + 16
    PAIRS = X // 2
    NX = model // 2
    HX = NX // 2
    PR = 2 * PS
    NT = 256
    KD = HD * vdim
    PW = KD // (2 * Y)

    def kernel(
        owner_ref, table_ref, len_ref, pool_hbm, q_hbm, new_ref, vu_hbm, op_hbm, out_ref,
        pool, q, pk, keys, lat, snd, rcv, vu, val, vz, va, w, po, rs, so, fin,
        lsem, cs, cr, v1s, v1r, v3s, v3r, w1s, w1r, w2s, w2r, w3s, w3r,
        ls, lr, zs, zr, gs, gr, ss, sr, fs, fr,
    ):
        sect = lax.axis_index("sect")
        dev = lax.axis_index("dev")
        y, c = sect // 2, sect % 2
        z, x = dev // X, dev % X
        sibling = y * 2 + (1 - c)
        piece = c * Y + y
        pair, half = x // 2, x % 2
        sends = []

        hops = [(0, 0), (0, 1), (1, 0), (Y - 1, 0), (1, 1), (Y - 1, 1), (2, 0), (2, 1)]
        if Y == 2:
            hops = [(0, 0), (0, 1), (1, 0), (1, 1)]

        def hop(k):
            if isinstance(k, int):
                return hops[k]
            over, across = jnp.int32(0), jnp.int32(0)
            for i, (a, b) in enumerate(hops):
                over += jnp.where(k == i, a, 0)
                across += jnp.where(k == i, b, 0)
            return over, across

        def at_sect(k):
            over, across = hops[k]
            return ((y + over) % Y * 2 + (c + across) % 2, dev)

        def at_y(r):
            return (((y + r) % Y) * 2 + c, dev)

        def at_z(r):
            return (sect, ((z + r) % Z) * X + x)

        def at_x(r):
            return (sect, z * X + (x + r) % X)

        def remote(src, dst, send_sem, recv_sem, to):
            return pltpu.make_async_remote_copy(
                src_ref=src, dst_ref=dst, send_sem=send_sem, recv_sem=recv_sem,
                device_id=to, device_id_type=MESH,
            )

        def send(src, dst, send_sem, recv_sem, to):
            copy = remote(src, dst, send_sem, recv_sem, to)
            copy.start()
            sends.append(copy)

        def arrived(src, dst, send_sem, recv_sem, to):
            remote(src, dst, send_sem, recv_sem, to).wait_recv()

        load_pool = pltpu.make_async_copy(pool_hbm.at[0], pool, lsem.at[0])
        load_q = pltpu.make_async_copy(q_hbm, q, lsem.at[1])
        load_vu = pltpu.make_async_copy(vu_hbm, vu.at[0], lsem.at[2])
        own_cols = pl.ds(pl.multiple_of(half * NX, 128), NX)
        load_w = pltpu.make_async_copy(op_hbm.at[:, own_cols], w.at[0], lsem.at[3])
        load_pool.start()
        load_q.start()
        load_vu.start()
        load_w.start()

        barrier = pltpu.get_barrier_semaphore()
        peers = [at_sect(r) for r in range(1, sections)]
        peers += [at_z(r) for r in range(1, Z)] + [at_x(r) for r in range(1, X)]
        for peer in peers:
            pl.semaphore_signal(barrier, inc=1, device_id=peer, device_id_type=MESH)

        new_rows = new_ref[...].astype(jnp.float32).reshape(steps * req, width)
        new_rows = new_rows.astype(jnp.bfloat16)
        pick_u = lax.broadcasted_iota(jnp.int32, (16, steps * req), 0)
        pick_i = lax.broadcasted_iota(jnp.int32, (16, steps * req), 1)

        def slot_and_length(k):
            over, across = hop(k)
            source = lax.rem(y - over + Y, Y) * 2 + lax.rem(c + across, 2)
            slot, length = jnp.int32(0), jnp.int32(0)
            for i in range(req):
                owner = owner_ref[source, i]
                mine = lax.div(owner, req) == sect
                slot += jnp.where(mine, lax.rem(owner, req), 0)
                length += jnp.where(mine, len_ref[source, i], 0)
            return slot, length

        def fresh(k, carry):
            slot, _ = slot_and_length(k)
            pick = (pick_u == (pick_i >> ilog2(req))) & ((pick_i & (req - 1)) == slot)
            rows = mm(pick.astype(jnp.bfloat16), new_rows)
            keys[k, pl.ds(CR, 16), :] = rows.astype(jnp.bfloat16)
            return carry

        lax.fori_loop(0, req, fresh, 0)
        load_pool.wait()

        def pack(r):
            over, across = hop(r)
            target = lax.rem(y + over, Y) * 2 + lax.rem(c + across, 2)
            first, second = jnp.int32(0), jnp.int32(0)
            for i in range(req):
                hit = lax.div(owner_ref[sect, i], req) == target
                first += jnp.where(hit, table_ref[sect, 0, i], 0)
                second += jnp.where(hit, table_ref[sect, 1, i], 0)
            return pool[first], pool[second]

        def pack_remote(r, carry):
            a, b = pack(r)
            pk[r, 0:block, :] = a
            pk[r, block:CR, :] = b
            return carry

        lax.fori_loop(1, sections, pack_remote, 0)
        a, b = pack(0)
        keys[0, 0:block, :] = a
        keys[0, block:CR, :] = b

        pl.semaphore_wait(barrier, len(peers))

        def cache_args(r):
            return pk.at[r], keys.at[r, pl.ds(0, CR), :], cs.at[r], cr.at[r], at_sect(r)

        for r in range(1, sections):
            send(*cache_args(r))

        wrows = pl.ds(pl.multiple_of(piece * PW, PW), PW)

        VH = lat_w // 2
        ways = Z // 2

        def core_rows(core):
            return pl.ds(pl.multiple_of(core * VH, VH), VH)

        def v1_args(h, d):
            sign = 1 - 2 * d
            some = pl.ds(d * (HD // 2), HD // 2) if h == ways else pl.ds(0, HD)
            rows = core_rows(c)
            if h == 1:
                part = vu_hbm.at[some, rows, :]
            else:
                part = vu.at[sign * (h - 1) % Z, some, rows, :]
            return part, vu.at[sign * h % Z, some, rows, :], v1s.at[d, h], v1r.at[d, h], at_z(sign + Z)

        def v3_args(r, core):
            part = vu.at[r, :, core_rows(core), :]
            return part, part, v3s.at[r], v3r.at[r], (sibling, dev)

        def v_step(h):
            if h > 1:
                for d in range(2):
                    arrived(*v1_args(h - 1, d))
            if h <= ways:
                for d in range(2):
                    send(*v1_args(h, d))
            if 1 < h <= ways:
                for r in (h - 1, Z - h + 1):
                    send(*v3_args(r, c))
            if h == ways + 1:
                send(*v3_args(ways, c))

        def w1_args(r):
            cols = pl.ds(pl.multiple_of(((x + r) % X) % 2 * NX, 128), NX)
            return op_hbm.at[wrows, cols], w.at[r, wrows, :], w1s.at[r], w1r.at[r], at_x(r)

        def from_y(r, size, part, parts):
            start = (c * Y + (y - r + Y) % Y) * size + part * (size // parts)
            return pl.ds(pl.multiple_of(start, size // parts), size // parts)

        def w2_args(r, rows, slot):
            part = w.at[pl.ds(1, X - 1), rows, :]
            return part, part, w2s.at[slot], w2r.at[slot], at_y(r)

        def y_start(args, size):
            send(*args(1, from_y(0, size, 0, 1), 0))
            if Y > 2:
                send(*args(Y - 1, from_y(0, size, 0, 1), 1))

        def w3_args(r, core):
            rows = pl.ds(pl.multiple_of((core * Y + (y - r + Y) % Y) * PW, PW), PW)
            part = w.at[pl.ds(1, X - 1), rows, :]
            return part, part, w3s.at[r], w3r.at[r], (sibling, dev)

        def y_forward(args, size, across):
            send(*across(0, c))
            arrived(*args(1, from_y(1, size, 0, 1), 0))
            if Y > 2:
                send(*args(1, from_y(1, size, 0, 2), 2))
                arrived(*args(Y - 1, from_y(Y - 1, size, 0, 1), 1))
                send(*args(Y - 1, from_y(Y - 1, size, 1, 2), 3))
                send(*across(Y - 1, c))
            send(*across(1, c))

        def y_finish(args, size, across):
            if Y > 2:
                arrived(*args(1, from_y(2, size, 0, 2), 2))
                arrived(*args(Y - 1, from_y(2, size, 1, 2), 3))
                send(*across(2, c))

        v_step(1)
        for r in range(1, X):
            send(*w1_args(r))

        swap_out = lax.broadcasted_iota(jnp.int32, (HZ * PS, HZ * PS), 0)
        swap_in = lax.broadcasted_iota(jnp.int32, (HZ * PS, HZ * PS), 1)
        swap = ((swap_out >> ilog2(PS)) == (swap_in & (HZ - 1))) & (
            (swap_out & (PS - 1)) == (swap_in >> ilog2(HZ))
        )
        swap = swap.astype(jnp.bfloat16)
        load_q.wait()

        def attend(k, k4):
            slot, length = slot_and_length(k)
            key_rows = keys[k]
            key_lat = keys[k, :, 0:lat_w]
            q_cols = jnp.concatenate([q[s, slot] for s in range(steps)], axis=1)
            scores = mm(key_rows, q_cols) * score_scale
            row = lax.broadcasted_iota(jnp.int32, scores.shape, 0)
            step = lax.broadcasted_iota(jnp.int32, scores.shape, 1) >> ilog2(heads)
            held = jnp.where(row < CR, length, CR + 1 + step)
            scores = jnp.where(row < held, scores, masked_score)
            weights = jnp.exp(scores - jnp.max(scores, axis=0, keepdims=True))
            probs = weights * (1.0 / jnp.sum(weights, axis=0, keepdims=True))
            out = tn_dot(probs.astype(jnp.bfloat16), key_lat).astype(jnp.bfloat16)
            lat[k4] = out.reshape(steps, heads, lat_w)

        def latent_args(r, pg):
            to = (x + r) % X
            return snd.at[to, pg], rcv.at[x, pg], ls.at[pg, r], lr.at[pg, r], at_x(r)

        def latent_from(r, pg):
            source = (x - r + X) % X
            return snd.at[source, pg], rcv.at[source, pg], ls.at[pg, r], lr.at[pg, r], at_x(r)

        local_latents = []

        def attention(pg):
            def one(k4, carry):
                k = pg * GROUP + k4

                @pl.when(k > 0)
                def _():
                    arrived(pk.at[k], keys.at[k, pl.ds(0, CR), :], cs.at[k], cr.at[k], at_sect(1))

                attend(k, k4)
                return carry

            lax.fori_loop(0, GROUP, one, 0)

            def turn(zz, carry):
                part = lat[:, :, pl.ds(pl.multiple_of(zz * HZ, HZ), HZ), :]
                turned = mm(swap, part.reshape(PS * HZ, lat_w)).astype(jnp.bfloat16)
                snd[:, pg, zz] = turned.reshape(X, HD * PS, lat_w)
                return carry

            lax.fori_loop(0, Z, turn, 0)
            for r in range(1, X):
                send(*latent_args(r, pg))
            own = pltpu.make_async_copy(snd.at[x, pg], rcv.at[x, pg], lsem.at[4 + pg])
            own.start()
            local_latents.append(own)

        def value_args(r, pg):
            to = (z + r) % Z
            return val.at[to, pg], vz.at[pg, :, z], zs.at[pg, r], zr.at[pg, r], at_z(r)

        def value_from(r, pg):
            source = (z - r + Z) % Z
            return val.at[source, pg], vz.at[pg, :, source], zs.at[pg, r], zr.at[pg, r], at_z(r)

        local_values = []

        def values(pg):
            for r in range(1, X):
                arrived(*latent_from(r, pg))
            local_latents[pg].wait()

            def ring(r, carry):
                zz = lax.rem(z - r + Z, Z)
                maps = jnp.concatenate([vu[r, hh] for hh in range(HD)], axis=1)
                full = mm(rcv[:, pg, zz].reshape(X * HD * PS, lat_w), maps)
                full = full.reshape(X, HD, PS, KD)
                for hh in range(HD):
                    cols = slice(hh * vdim, (hh + 1) * vdim)
                    part = full[:, hh, :, cols].reshape(PAIRS, PR, vdim).astype(jnp.bfloat16)
                    val[zz, pg, :, :, cols] = part
                return carry

            lax.fori_loop(0, Z, ring, 0)
            for r in range(1, Z):
                send(*value_args(r, pg))
            own = pltpu.make_async_copy(val.at[z, pg], vz.at[pg, :, z], lsem.at[4 + NG + pg])
            own.start()
            local_values.append(own)

        def gather_args(r, pg):
            to = ((x + r) % X) // 2
            return vz.at[pg, to], va.at[r, pg], gs.at[pg, r], gr.at[pg, r], at_x(r)

        def gather_start(pg):
            for r in range(1, Z):
                arrived(*value_from(r, pg))
            local_values[pg].wait()
            for r in range(1, X):
                send(*gather_args(r, pg))

        def ring_args(d, m, i, pg):
            sign = 1 - 2 * d
            target = (z - sign * (1 + i) + Z) % Z
            held = po.at[target, pg, d, m] if i == 0 else rs.at[d, pg, i - 1, m]
            sem = 2 * d + m
            return held, rs.at[d, pg, i, m], ss.at[sem, pg, i], sr.at[sem, pg, i], at_z(sign + Z)

        def ring_step(i, pg):
            for m in range(2):
                for d in range(2):
                    arrived(*ring_args(d, m, i - 1, pg))
                    target = (z - (1 - 2 * d) * (1 + i) + 2 * Z) % Z
                    total = rs[d, pg, i - 1, m].astype(jnp.float32)
                    total += po[target, pg, d, m].astype(jnp.float32)
                    rs[d, pg, i - 1, m] = total.astype(jnp.bfloat16)
                    send(*ring_args(d, m, i, pg))

        first = Z // 4 + 1

        def project(pg):
            groups = pl.ds(2 * pg, 2)
            for g in range(2 * pg, 2 * pg + 2):
                for r in range(1, X):
                    arrived(*gather_args(r, g))
            for d in range(2):

                def tile(n, carry):
                    cols = pl.ds(pl.multiple_of(d * HX + n * NT, NT), NT)
                    acc = mm(vz[groups, pair].reshape(2 * Z * PR, KD), w[0, :, cols])
                    for r in range(1, X):
                        acc += mm(va[r, groups].reshape(2 * Z * PR, KD), w[r, :, cols])
                    part = acc.astype(jnp.bfloat16).reshape(2, Z, PR, NT)
                    cols = pl.ds(pl.multiple_of(n * NT, NT), NT)
                    for g in range(2):
                        po[:, pg, d, g, :, cols] = part[g]
                    return carry

                lax.fori_loop(0, HX // NT, tile, 0)
                for m in range(2):
                    send(*ring_args(d, m, 0, pg))

        def final_args(pg, side):
            return so.at[pg, 1 - side], fin.at[side, pg], fs.at[pg], fr.at[pg], at_x(1 - 2 * half + X)

        local_final = []

        def reduce(pg):
            for d in range(2):
                totals = []
                for g in range(2):
                    arrived(*ring_args(d, g, Z - 2, pg))
                    total = po[z, pg, d, g].astype(jnp.float32)
                    totals.append(total + rs[d, pg, Z - 2, g].astype(jnp.float32))
                for m in range(2):
                    rows = jnp.concatenate([t[m * PS : (m + 1) * PS] for t in totals], axis=0)
                    so[pg, m, :, pl.ds(d * HX, HX)] = rows.astype(jnp.bfloat16)
            send(*final_args(pg, half))
            own = pltpu.make_async_copy(so.at[pg, half], fin.at[half, pg], lsem.at[4 + 2 * NG + pg])
            own.start()
            local_final.append(own)

        step = 2
        for g in range(NG):
            attention(g)
            if g != 1 and step <= ways:
                v_step(step)
                step += 1
        for r in range(1, X):
            arrived(*w1_args(r))
        y_start(w2_args, PW)
        while step <= ways + 1:
            v_step(step)
            step += 1
        load_vu.wait()
        for r in range(1, Z):
            arrived(*v3_args(r, 1 - c))
        for g in range(NG):
            values(g)
            if g:
                gather_start(g - 1)
            if g == 1:
                y_forward(w2_args, PW, w3_args)
            if g == NG - 2:
                y_finish(w2_args, PW, w3_args)
        load_w.wait()
        for r in range(Y):
            arrived(*w3_args(r, 1 - c))
        if NPG > 1:
            project(0)
        gather_start(NG - 1)
        if NPG == 1:
            project(0)
            for i in range(1, Z - 1):
                ring_step(i, 0)
        else:
            for i in range(1, first):
                ring_step(i, 0)
            project(1)
            for i in range(1, Z - 1):
                if first <= i + first - 1 < Z - 1:
                    ring_step(i + first - 1, 0)
                elif i + first - 1 == Z - 1:
                    reduce(0)
                ring_step(i, 1)
        reduce(NPG - 1)

        place_out = lax.broadcasted_iota(jnp.int32, (steps * req, steps * req), 0)
        place_in = lax.broadcasted_iota(jnp.int32, (steps * req, steps * req), 1)
        slots = jnp.zeros((steps * req, steps * req), jnp.int32)
        for k in range(req):
            slot, _ = slot_and_length(k)
            slots = jnp.where((place_in >> ilog2(steps)) == k, slot, slots)
        place = ((place_out >> ilog2(req)) == (place_in & (steps - 1))) & (
            (place_out & (req - 1)) == slots
        )
        place = place.astype(jnp.bfloat16)
        for pg in range(NPG):
            arrived(*final_args(pg, 1 - half))
            local_final[pg].wait()
        for side in range(2):
            rows = mm(place, fin[side].reshape(steps * req, NX))
            for s in range(steps):
                part = rows[s * req : (s + 1) * req].astype(jnp.bfloat16)
                out_ref[s, :, side * NX : (side + 1) * NX] = part

        for copy in sends:
            copy.wait_send()

    bf = jnp.bfloat16
    dma = pltpu.SemaphoreType.DMA
    scratch = [
        pltpu.VMEM((2 * req, block, width), bf),
        pltpu.VMEM((steps, req, width, heads), bf),
        pltpu.VMEM((sections, CR, width), bf),
        pltpu.VMEM((req, KR, width), bf),
        pltpu.VMEM((GROUP, steps, heads, lat_w), bf),
        pltpu.VMEM((X, NG, Z, HD * PS, lat_w), bf),
        pltpu.VMEM((X, NG, Z, HD * PS, lat_w), bf),
        pltpu.VMEM((Z, HD, lat_w, vdim), bf),
        pltpu.VMEM((Z, NG, PAIRS, PR, KD), bf),
        pltpu.VMEM((NG, PAIRS, Z, PR, KD), bf),
        pltpu.VMEM((X, NG, Z, PR, KD), bf),
        pltpu.VMEM((X, KD, NX), bf),
        pltpu.VMEM((Z, NPG, 2, 2, PR, HX), bf),
        pltpu.VMEM((2, NPG, Z - 1, 2, PR, HX), bf),
        pltpu.VMEM((NPG, 2, 2 * PS, NX), bf),
        pltpu.VMEM((2, NPG, 2 * PS, NX), bf),
        dma((4 + 2 * NG + NPG,)),
        dma((sections,)), dma((sections,)),
        dma((2, Z)), dma((2, Z)), dma((Z,)), dma((Z,)),
        dma((X,)), dma((X,)), dma((4,)), dma((4,)), dma((Y,)), dma((Y,)),
        dma((NG, X)), dma((NG, X)), dma((NG, Z)), dma((NG, Z)),
        dma((NG, X)), dma((NG, X)), dma((4, NPG, Z)), dma((4, NPG, Z)),
        dma((NPG,)), dma((NPG,)),
    ]
    return kernel, scratch


def on_device(
    prompt_lengths, owner_map, block_table, pool_blocks, queries, new_latents, value_up, out_proj
):
    sections, devices = lax.axis_size("sect"), lax.axis_size("dev")
    steps, req, heads, width = queries.shape
    _, lat_w, vdim = value_up.shape
    model = out_proj.shape[1]
    block = pool_blocks.shape[2]
    kernel, scratch = make_kernel(
        sections, devices // CHIPS_X, CHIPS_X, steps, req, heads, lat_w, width, vdim, model, block
    )
    smem = pl.BlockSpec(memory_space=pltpu.SMEM)
    vmem = pl.BlockSpec(memory_space=pltpu.VMEM)
    hbm = pl.BlockSpec(memory_space=pl.ANY)
    return pl.pallas_call(
        kernel,
        out_shape=jax.ShapeDtypeStruct((steps, req, model), jnp.bfloat16),
        in_specs=[smem, smem, smem, hbm, hbm, vmem, hbm, hbm],
        out_specs=vmem,
        scratch_shapes=scratch,
        compiler_params=pltpu.CompilerParams(
            collective_id=0, has_side_effects=True, vmem_limit_bytes=60 * 1024 * 1024
        ),
    )(
        owner_map,
        jnp.swapaxes(block_table, 1, 2),
        prompt_lengths,
        pool_blocks,
        jnp.swapaxes(queries, 2, 3),
        new_latents,
        value_up,
        out_proj,
    )


def solution(mesh):
    in_specs = (
        P(None, "dev"),
        P(None, "dev"),
        P(None, "dev", None),
        P("sect", "dev", None, None),
        P(None, ("sect", "dev"), None, None),
        P(None, ("sect", "dev"), None),
        P("dev", None, None),
        P("dev", None),
    )
    out_specs = P(None, ("sect", "dev"), None)
    return jax.shard_map(
        on_device, mesh=mesh, in_specs=in_specs, out_specs=out_specs, check_vma=False
    )
```

```python
import jax
import jax.numpy as jnp
from jax import lax
from jax.experimental import pallas as pl
from jax.experimental.pallas import tpu as pltpu
from jax.sharding import PartitionSpec as P

MESH = pl.DeviceIdType.MESH
CHIPS_X = 4
GROUP = 2
score_scale = 192.0 ** (-0.5)
masked_score = -1e30


def ilog2(n):
    return n.bit_length() - 1


def tn_dot(a, b):
    return lax.dot_general(a, b, (((0,), (0,)), ((), ())), preferred_element_type=jnp.float32)


def mm(a, b):
    return jnp.dot(a, b, preferred_element_type=jnp.float32)


def make_kernel(sections, chips_z, chips_x, steps, req, heads, lat_w, width, vdim, model, block):
    Y, Z, X = sections // 2, chips_z, chips_x
    HD = heads // (Z * X)
    HZ = HD * X
    NG = req // GROUP
    NPG = NG // 2
    PS = GROUP * steps
    CR = 2 * block
    KR = CR + 16
    PAIRS = X // 2
    NX = model // 2
    HX = NX // 2
    PR = 2 * PS
    NT = 256
    KD = HD * vdim
    PW = KD // (2 * Y)

    def kernel(
        owner_ref, table_ref, len_ref, pool_hbm, q_hbm, new_ref, vu_hbm, op_hbm, out_ref,
        pool, q, pk, keys, lat, snd, rcv, vu, val, vz, va, w, po, rs, so, fin,
        lsem, cs, cr, v1s, v1r, v3s, v3r, w1s, w1r, w2s, w2r, w3s, w3r,
        ls, lr, zs, zr, gs, gr, ss, sr, fs, fr,
    ):
        sect = lax.axis_index("sect")
        dev = lax.axis_index("dev")
        y, c = sect // 2, sect % 2
        z, x = dev // X, dev % X
        sibling = y * 2 + (1 - c)
        piece = c * Y + y
        pair, half = x // 2, x % 2
        sends = []

        hops = [(0, 0), (0, 1), (1, 0), (Y - 1, 0), (1, 1), (Y - 1, 1), (2, 0), (2, 1)]
        if Y == 2:
            hops = [(0, 0), (0, 1), (1, 0), (1, 1)]

        def hop(k):
            if isinstance(k, int):
                return hops[k]
            over, across = jnp.int32(0), jnp.int32(0)
            for i, (a, b) in enumerate(hops):
                over += jnp.where(k == i, a, 0)
                across += jnp.where(k == i, b, 0)
            return over, across

        def at_sect(k):
            over, across = hops[k]
            return ((y + over) % Y * 2 + (c + across) % 2, dev)

        def at_y(r):
            return (((y + r) % Y) * 2 + c, dev)

        def at_z(r):
            return (sect, ((z + r) % Z) * X + x)

        def at_x(r):
            return (sect, z * X + (x + r) % X)

        def remote(src, dst, send_sem, recv_sem, to):
            return pltpu.make_async_remote_copy(
                src_ref=src, dst_ref=dst, send_sem=send_sem, recv_sem=recv_sem,
                device_id=to, device_id_type=MESH,
            )

        def send(src, dst, send_sem, recv_sem, to):
            copy = remote(src, dst, send_sem, recv_sem, to)
            copy.start()
            sends.append(copy)

        def arrived(src, dst, send_sem, recv_sem, to):
            remote(src, dst, send_sem, recv_sem, to).wait_recv()

        load_pool = pltpu.make_async_copy(pool_hbm.at[0], pool, lsem.at[0])
        load_q = pltpu.make_async_copy(q_hbm, q, lsem.at[1])
        load_vu = pltpu.make_async_copy(vu_hbm, vu.at[0], lsem.at[2])
        own_cols = pl.ds(pl.multiple_of(half * NX, 128), NX)
        load_w = pltpu.make_async_copy(op_hbm.at[:, own_cols], w.at[0], lsem.at[3])
        load_pool.start()
        load_q.start()
        load_vu.start()
        load_w.start()

        barrier = pltpu.get_barrier_semaphore()
        peers = [at_sect(r) for r in range(1, sections)]
        peers += [at_z(r) for r in range(1, Z)] + [at_x(r) for r in range(1, X)]
        for peer in peers:
            pl.semaphore_signal(barrier, inc=1, device_id=peer, device_id_type=MESH)

        new_rows = new_ref[...].astype(jnp.float32).reshape(steps * req, width)
        new_rows = new_rows.astype(jnp.bfloat16)
        pick_u = lax.broadcasted_iota(jnp.int32, (16, steps * req), 0)
        pick_i = lax.broadcasted_iota(jnp.int32, (16, steps * req), 1)

        def slot_and_length(k):
            over, across = hop(k)
            source = lax.rem(y - over + Y, Y) * 2 + lax.rem(c + across, 2)
            slot, length = jnp.int32(0), jnp.int32(0)
            for i in range(req):
                owner = owner_ref[source, i]
                mine = lax.div(owner, req) == sect
                slot += jnp.where(mine, lax.rem(owner, req), 0)
                length += jnp.where(mine, len_ref[source, i], 0)
            return slot, length

        def fresh(k, carry):
            slot, _ = slot_and_length(k)
            pick = (pick_u == (pick_i >> ilog2(req))) & ((pick_i & (req - 1)) == slot)
            rows = mm(pick.astype(jnp.bfloat16), new_rows)
            keys[k, pl.ds(CR, 16), :] = rows.astype(jnp.bfloat16)
            return carry

        lax.fori_loop(0, req, fresh, 0)
        load_pool.wait()

        def pack(r):
            over, across = hop(r)
            target = lax.rem(y + over, Y) * 2 + lax.rem(c + across, 2)
            first, second = jnp.int32(0), jnp.int32(0)
            for i in range(req):
                hit = lax.div(owner_ref[sect, i], req) == target
                first += jnp.where(hit, table_ref[sect, 0, i], 0)
                second += jnp.where(hit, table_ref[sect, 1, i], 0)
            return pool[first], pool[second]

        def pack_remote(r, carry):
            a, b = pack(r)
            pk[r, 0:block, :] = a
            pk[r, block:CR, :] = b
            return carry

        lax.fori_loop(1, sections, pack_remote, 0)
        a, b = pack(0)
        keys[0, 0:block, :] = a
        keys[0, block:CR, :] = b

        pl.semaphore_wait(barrier, len(peers))

        def cache_args(r):
            return pk.at[r], keys.at[r, pl.ds(0, CR), :], cs.at[r], cr.at[r], at_sect(r)

        for r in range(1, sections):
            send(*cache_args(r))

        wrows = pl.ds(pl.multiple_of(piece * PW, PW), PW)

        VH = lat_w // 2
        ways = Z // 2

        def core_rows(core):
            return pl.ds(pl.multiple_of(core * VH, VH), VH)

        def v1_args(h, d):
            sign = 1 - 2 * d
            some = pl.ds(d * (HD // 2), HD // 2) if h == ways else pl.ds(0, HD)
            rows = core_rows(c)
            if h == 1:
                part = vu_hbm.at[some, rows, :]
            else:
                part = vu.at[sign * (h - 1) % Z, some, rows, :]
            return part, vu.at[sign * h % Z, some, rows, :], v1s.at[d, h], v1r.at[d, h], at_z(sign + Z)

        def v3_args(r, core):
            part = vu.at[r, :, core_rows(core), :]
            return part, part, v3s.at[r], v3r.at[r], (sibling, dev)

        def v_step(h):
            if h > 1:
                for d in range(2):
                    arrived(*v1_args(h - 1, d))
            if h <= ways:
                for d in range(2):
                    send(*v1_args(h, d))
            if 1 < h <= ways:
                for r in (h - 1, Z - h + 1):
                    send(*v3_args(r, c))
            if h == ways + 1:
                send(*v3_args(ways, c))

        def w1_args(r):
            cols = pl.ds(pl.multiple_of(((x + r) % X) % 2 * NX, 128), NX)
            return op_hbm.at[wrows, cols], w.at[r, wrows, :], w1s.at[r], w1r.at[r], at_x(r)

        def from_y(r, size, part, parts):
            start = (c * Y + (y - r + Y) % Y) * size + part * (size // parts)
            return pl.ds(pl.multiple_of(start, size // parts), size // parts)

        def w2_args(r, rows, slot):
            part = w.at[pl.ds(1, X - 1), rows, :]
            return part, part, w2s.at[slot], w2r.at[slot], at_y(r)

        def y_start(args, size):
            send(*args(1, from_y(0, size, 0, 1), 0))
            if Y > 2:
                send(*args(Y - 1, from_y(0, size, 0, 1), 1))

        def w3_args(r, core):
            rows = pl.ds(pl.multiple_of((core * Y + (y - r + Y) % Y) * PW, PW), PW)
            part = w.at[pl.ds(1, X - 1), rows, :]
            return part, part, w3s.at[r], w3r.at[r], (sibling, dev)

        def y_forward(args, size, across):
            send(*across(0, c))
            arrived(*args(1, from_y(1, size, 0, 1), 0))
            if Y > 2:
                send(*args(1, from_y(1, size, 0, 2), 2))
                arrived(*args(Y - 1, from_y(Y - 1, size, 0, 1), 1))
                send(*args(Y - 1, from_y(Y - 1, size, 1, 2), 3))
                send(*across(Y - 1, c))
            send(*across(1, c))

        def y_finish(args, size, across):
            if Y > 2:
                arrived(*args(1, from_y(2, size, 0, 2), 2))
                arrived(*args(Y - 1, from_y(2, size, 1, 2), 3))
                send(*across(2, c))

        v_step(1)
        for r in range(1, X):
            send(*w1_args(r))

        swap_out = lax.broadcasted_iota(jnp.int32, (HZ * PS, HZ * PS), 0)
        swap_in = lax.broadcasted_iota(jnp.int32, (HZ * PS, HZ * PS), 1)
        swap = ((swap_out >> ilog2(PS)) == (swap_in & (HZ - 1))) & (
            (swap_out & (PS - 1)) == (swap_in >> ilog2(HZ))
        )
        swap = swap.astype(jnp.bfloat16)
        load_q.wait()

        def attend(k, k4):
            slot, length = slot_and_length(k)
            key_rows = keys[k]
            key_lat = keys[k, :, 0:lat_w]
            q_cols = jnp.concatenate([q[s, slot] for s in range(steps)], axis=1)
            scores = mm(key_rows, q_cols) * score_scale
            row = lax.broadcasted_iota(jnp.int32, scores.shape, 0)
            step = lax.broadcasted_iota(jnp.int32, scores.shape, 1) >> ilog2(heads)
            held = jnp.where(row < CR, length, CR + 1 + step)
            scores = jnp.where(row < held, scores, masked_score)
            weights = jnp.exp(scores - jnp.max(scores, axis=0, keepdims=True))
            probs = weights * (1.0 / jnp.sum(weights, axis=0, keepdims=True))
            out = tn_dot(probs.astype(jnp.bfloat16), key_lat).astype(jnp.bfloat16)
            lat[k4] = out.reshape(steps, heads, lat_w)

        def latent_args(r, pg):
            to = (x + r) % X
            return snd.at[to, pg], rcv.at[x, pg], ls.at[pg, r], lr.at[pg, r], at_x(r)

        def latent_from(r, pg):
            source = (x - r + X) % X
            return snd.at[source, pg], rcv.at[source, pg], ls.at[pg, r], lr.at[pg, r], at_x(r)

        local_latents = []

        def attention(pg):
            def one(k4, carry):
                k = pg * GROUP + k4

                @pl.when(k > 0)
                def _():
                    arrived(pk.at[k], keys.at[k, pl.ds(0, CR), :], cs.at[k], cr.at[k], at_sect(1))

                attend(k, k4)
                return carry

            lax.fori_loop(0, GROUP, one, 0)

            def turn(zz, carry):
                part = lat[:, :, pl.ds(pl.multiple_of(zz * HZ, HZ), HZ), :]
                turned = mm(swap, part.reshape(PS * HZ, lat_w)).astype(jnp.bfloat16)
                snd[:, pg, zz] = turned.reshape(X, HD * PS, lat_w)
                return carry

            lax.fori_loop(0, Z, turn, 0)
            for r in range(1, X):
                send(*latent_args(r, pg))
            own = pltpu.make_async_copy(snd.at[x, pg], rcv.at[x, pg], lsem.at[4 + pg])
            own.start()
            local_latents.append(own)

        def value_args(r, pg):
            to = (z + r) % Z
            return val.at[to, pg], vz.at[pg, :, z], zs.at[pg, r], zr.at[pg, r], at_z(r)

        def value_from(r, pg):
            source = (z - r + Z) % Z
            return val.at[source, pg], vz.at[pg, :, source], zs.at[pg, r], zr.at[pg, r], at_z(r)

        local_values = []

        def values(pg):
            for r in range(1, X):
                arrived(*latent_from(r, pg))
            local_latents[pg].wait()

            def ring(r, carry):
                zz = lax.rem(z - r + Z, Z)
                maps = jnp.concatenate([vu[r, hh] for hh in range(HD)], axis=1)
                full = mm(rcv[:, pg, zz].reshape(X * HD * PS, lat_w), maps)
                full = full.reshape(X, HD, PS, KD)
                for hh in range(HD):
                    cols = slice(hh * vdim, (hh + 1) * vdim)
                    part = full[:, hh, :, cols].reshape(PAIRS, PR, vdim).astype(jnp.bfloat16)
                    val[zz, pg, :, :, cols] = part
                return carry

            lax.fori_loop(0, Z, ring, 0)
            for r in range(1, Z):
                send(*value_args(r, pg))
            own = pltpu.make_async_copy(val.at[z, pg], vz.at[pg, :, z], lsem.at[4 + NG + pg])
            own.start()
            local_values.append(own)

        def gather_args(r, pg):
            to = ((x + r) % X) // 2
            return vz.at[pg, to], va.at[r, pg], gs.at[pg, r], gr.at[pg, r], at_x(r)

        def gather_start(pg):
            for r in range(1, Z):
                arrived(*value_from(r, pg))
            local_values[pg].wait()
            for r in range(1, X):
                send(*gather_args(r, pg))

        def ring_args(d, i, g):
            sign = 1 - 2 * d
            target = (z - sign * (1 + i) + Z) % Z
            held = po.at[target, g, d] if i == 0 else rs.at[d, g, i - 1]
            return held, rs.at[d, g, i], ss.at[d, g, i], sr.at[d, g, i], at_z(sign + Z)

        def ring_step(i, g):
            for d in range(2):
                arrived(*ring_args(d, i - 1, g))
                target = (z - (1 - 2 * d) * (1 + i) + 2 * Z) % Z
                total = rs[d, g, i - 1].astype(jnp.float32)
                total += po[target, g, d].astype(jnp.float32)
                rs[d, g, i - 1] = total.astype(jnp.bfloat16)
                send(*ring_args(d, i, g))

        def project(g):
            for r in range(1, X):
                arrived(*gather_args(r, g))
            for d in range(2):

                def tile(n, carry):
                    cols = pl.ds(pl.multiple_of(d * HX + n * NT, NT), NT)
                    acc = mm(vz[g, pair].reshape(Z * PR, KD), w[0, :, cols])
                    for r in range(1, X):
                        acc += mm(va[r, g].reshape(Z * PR, KD), w[r, :, cols])
                    part = acc.astype(jnp.bfloat16).reshape(Z, PR, NT)
                    po[:, g, d, :, pl.ds(pl.multiple_of(n * NT, NT), NT)] = part
                    return carry

                lax.fori_loop(0, HX // NT, tile, 0)
                send(*ring_args(d, 0, g))

        def final_args(pg, side):
            return so.at[pg, 1 - side], fin.at[side, pg], fs.at[pg], fr.at[pg], at_x(1 - 2 * half + X)

        local_final = []

        def reduce(pg):
            for d in range(2):
                totals = []
                for g in (2 * pg, 2 * pg + 1):
                    arrived(*ring_args(d, Z - 2, g))
                    total = po[z, g, d].astype(jnp.float32)
                    totals.append(total + rs[d, g, Z - 2].astype(jnp.float32))
                for m in range(2):
                    rows = jnp.concatenate([t[m * PS : (m + 1) * PS] for t in totals], axis=0)
                    so[pg, m, :, pl.ds(d * HX, HX)] = rows.astype(jnp.bfloat16)
            send(*final_args(pg, half))
            own = pltpu.make_async_copy(so.at[pg, half], fin.at[half, pg], lsem.at[4 + 2 * NG + pg])
            own.start()
            local_final.append(own)

        step = 2
        for g in range(NG):
            attention(g)
            if g != 1 and step <= ways:
                v_step(step)
                step += 1
        for r in range(1, X):
            arrived(*w1_args(r))
        y_start(w2_args, PW)
        while step <= ways + 1:
            v_step(step)
            step += 1
        load_vu.wait()
        for r in range(1, Z):
            arrived(*v3_args(r, 1 - c))
        for g in range(NG):
            values(g)
            if g:
                gather_start(g - 1)
            if g == 1:
                y_forward(w2_args, PW, w3_args)
            if g == NG - 2:
                y_finish(w2_args, PW, w3_args)
        load_w.wait()
        for r in range(Y):
            arrived(*w3_args(r, 1 - c))
        project(0)
        gather_start(NG - 1)
        rings = [1]
        while min(rings) < Z:
            started = len(rings)
            if started < NG:
                project(started)
            for g in range(started):
                if rings[g] < Z - 1:
                    ring_step(rings[g], g)
                elif rings[g] == Z - 1 and g % 2:
                    reduce(g // 2)
                rings[g] += 1
            if started < NG:
                rings.append(1)

        place_out = lax.broadcasted_iota(jnp.int32, (steps * req, steps * req), 0)
        place_in = lax.broadcasted_iota(jnp.int32, (steps * req, steps * req), 1)
        slots = jnp.zeros((steps * req, steps * req), jnp.int32)
        for k in range(req):
            slot, _ = slot_and_length(k)
            slots = jnp.where((place_in >> ilog2(steps)) == k, slot, slots)
        place = ((place_out >> ilog2(req)) == (place_in & (steps - 1))) & (
            (place_out & (req - 1)) == slots
        )
        place = place.astype(jnp.bfloat16)
        for pg in range(NPG):
            arrived(*final_args(pg, 1 - half))
            local_final[pg].wait()
        for side in range(2):
            rows = mm(place, fin[side].reshape(steps * req, NX))
            for s in range(steps):
                part = rows[s * req : (s + 1) * req].astype(jnp.bfloat16)
                out_ref[s, :, side * NX : (side + 1) * NX] = part

        for copy in sends:
            copy.wait_send()

    bf = jnp.bfloat16
    dma = pltpu.SemaphoreType.DMA
    scratch = [
        pltpu.VMEM((2 * req, block, width), bf),
        pltpu.VMEM((steps, req, width, heads), bf),
        pltpu.VMEM((sections, CR, width), bf),
        pltpu.VMEM((req, KR, width), bf),
        pltpu.VMEM((GROUP, steps, heads, lat_w), bf),
        pltpu.VMEM((X, NG, Z, HD * PS, lat_w), bf),
        pltpu.VMEM((X, NG, Z, HD * PS, lat_w), bf),
        pltpu.VMEM((Z, HD, lat_w, vdim), bf),
        pltpu.VMEM((Z, NG, PAIRS, PR, KD), bf),
        pltpu.VMEM((NG, PAIRS, Z, PR, KD), bf),
        pltpu.VMEM((X, NG, Z, PR, KD), bf),
        pltpu.VMEM((X, KD, NX), bf),
        pltpu.VMEM((Z, NG, 2, PR, HX), bf),
        pltpu.VMEM((2, NG, Z - 1, PR, HX), bf),
        pltpu.VMEM((NPG, 2, 2 * PS, NX), bf),
        pltpu.VMEM((2, NPG, 2 * PS, NX), bf),
        dma((4 + 2 * NG + NPG,)),
        dma((sections,)), dma((sections,)),
        dma((2, Z)), dma((2, Z)), dma((Z,)), dma((Z,)),
        dma((X,)), dma((X,)), dma((4,)), dma((4,)), dma((Y,)), dma((Y,)),
        dma((NG, X)), dma((NG, X)), dma((NG, Z)), dma((NG, Z)),
        dma((NG, X)), dma((NG, X)), dma((2, NG, Z)), dma((2, NG, Z)),
        dma((NPG,)), dma((NPG,)),
    ]
    return kernel, scratch


def on_device(
    prompt_lengths, owner_map, block_table, pool_blocks, queries, new_latents, value_up, out_proj
):
    sections, devices = lax.axis_size("sect"), lax.axis_size("dev")
    steps, req, heads, width = queries.shape
    _, lat_w, vdim = value_up.shape
    model = out_proj.shape[1]
    block = pool_blocks.shape[2]
    kernel, scratch = make_kernel(
        sections, devices // CHIPS_X, CHIPS_X, steps, req, heads, lat_w, width, vdim, model, block
    )
    smem = pl.BlockSpec(memory_space=pltpu.SMEM)
    vmem = pl.BlockSpec(memory_space=pltpu.VMEM)
    hbm = pl.BlockSpec(memory_space=pl.ANY)
    return pl.pallas_call(
        kernel,
        out_shape=jax.ShapeDtypeStruct((steps, req, model), jnp.bfloat16),
        in_specs=[smem, smem, smem, hbm, hbm, vmem, hbm, hbm],
        out_specs=vmem,
        scratch_shapes=scratch,
        compiler_params=pltpu.CompilerParams(
            collective_id=0, has_side_effects=True, vmem_limit_bytes=60 * 1024 * 1024
        ),
    )(
        owner_map,
        jnp.swapaxes(block_table, 1, 2),
        prompt_lengths,
        pool_blocks,
        jnp.swapaxes(queries, 2, 3),
        new_latents,
        value_up,
        out_proj,
    )


def solution(mesh):
    in_specs = (
        P(None, "dev"),
        P(None, "dev"),
        P(None, "dev", None),
        P("sect", "dev", None, None),
        P(None, ("sect", "dev"), None, None),
        P(None, ("sect", "dev"), None),
        P("dev", None, None),
        P("dev", None),
    )
    out_specs = P(None, ("sect", "dev"), None)
    return jax.shard_map(
        on_device, mesh=mesh, in_specs=in_specs, out_specs=out_specs, check_vma=False
    )
```

```python
import jax
import jax.numpy as jnp
from jax import lax
from jax.experimental import pallas as pl
from jax.experimental.pallas import tpu as pltpu
from jax.sharding import PartitionSpec as P

MESH = pl.DeviceIdType.MESH
CHIPS_X = 4
GROUP = 2
score_scale = 192.0 ** (-0.5)
masked_score = -1e30


def ilog2(n):
    return n.bit_length() - 1


def tn_dot(a, b):
    return lax.dot_general(a, b, (((0,), (0,)), ((), ())), preferred_element_type=jnp.float32)


def mm(a, b):
    return jnp.dot(a, b, preferred_element_type=jnp.float32)


def make_kernel(sections, chips_z, chips_x, steps, req, heads, lat_w, width, vdim, model, block):
    Y, Z, X = sections // 2, chips_z, chips_x
    HD = heads // (Z * X)
    HZ = HD * X
    NG = req // GROUP
    NPG = NG // 2
    PS = GROUP * steps
    CR = 2 * block
    KR = CR + 16
    PAIRS = X // 2
    NX = model // 2
    HX = NX // 2
    PR = 2 * PS
    NT = 256
    KD = HD * vdim
    PW = KD // (2 * Y)

    def kernel(
        owner_ref, table_ref, len_ref, pool_hbm, q_hbm, new_ref, vu_hbm, op_hbm, out_ref,
        pool, q, pk, keys, lat, snd, rcv, vu, val, vz, va, w, po, rs, so, fin,
        lsem, cs, cr, v1s, v1r, v3s, v3r, w1s, w1r, w2s, w2r, w3s, w3r,
        ls, lr, zs, zr, gs, gr, ss, sr, fs, fr,
    ):
        sect = lax.axis_index("sect")
        dev = lax.axis_index("dev")
        y, c = sect // 2, sect % 2
        z, x = dev // X, dev % X
        sibling = y * 2 + (1 - c)
        piece = c * Y + y
        pair, half = x // 2, x % 2
        sends = []

        hops = [(0, 0), (0, 1), (1, 0), (Y - 1, 0), (1, 1), (Y - 1, 1), (2, 0), (2, 1)]
        if Y == 2:
            hops = [(0, 0), (0, 1), (1, 0), (1, 1)]

        def hop(k):
            if isinstance(k, int):
                return hops[k]
            over, across = jnp.int32(0), jnp.int32(0)
            for i, (a, b) in enumerate(hops):
                over += jnp.where(k == i, a, 0)
                across += jnp.where(k == i, b, 0)
            return over, across

        def at_sect(k):
            over, across = hops[k]
            return ((y + over) % Y * 2 + (c + across) % 2, dev)

        def at_y(r):
            return (((y + r) % Y) * 2 + c, dev)

        def at_z(r):
            return (sect, ((z + r) % Z) * X + x)

        def at_x(r):
            return (sect, z * X + (x + r) % X)

        def remote(src, dst, send_sem, recv_sem, to):
            return pltpu.make_async_remote_copy(
                src_ref=src, dst_ref=dst, send_sem=send_sem, recv_sem=recv_sem,
                device_id=to, device_id_type=MESH,
            )

        def send(src, dst, send_sem, recv_sem, to):
            copy = remote(src, dst, send_sem, recv_sem, to)
            copy.start()
            sends.append(copy)

        def arrived(src, dst, send_sem, recv_sem, to):
            remote(src, dst, send_sem, recv_sem, to).wait_recv()

        load_pool = pltpu.make_async_copy(pool_hbm.at[0], pool, lsem.at[0])
        load_q = pltpu.make_async_copy(q_hbm, q, lsem.at[1])
        load_vu = pltpu.make_async_copy(vu_hbm, vu.at[0], lsem.at[2])
        own_cols = pl.ds(pl.multiple_of(half * NX, 128), NX)
        load_w = pltpu.make_async_copy(op_hbm.at[:, own_cols], w.at[0], lsem.at[3])
        load_pool.start()
        load_q.start()
        load_vu.start()
        load_w.start()

        barrier = pltpu.get_barrier_semaphore()
        peers = [at_sect(r) for r in range(1, sections)]
        peers += [at_z(r) for r in range(1, Z)] + [at_x(r) for r in range(1, X)]
        for peer in peers:
            pl.semaphore_signal(barrier, inc=1, device_id=peer, device_id_type=MESH)

        new_rows = new_ref[...].astype(jnp.float32).reshape(steps * req, width)
        new_rows = new_rows.astype(jnp.bfloat16)
        pick_u = lax.broadcasted_iota(jnp.int32, (16, steps * req), 0)
        pick_i = lax.broadcasted_iota(jnp.int32, (16, steps * req), 1)

        def slot_and_length(k):
            over, across = hop(k)
            source = lax.rem(y - over + Y, Y) * 2 + lax.rem(c + across, 2)
            slot, length = jnp.int32(0), jnp.int32(0)
            for i in range(req):
                owner = owner_ref[source, i]
                mine = lax.div(owner, req) == sect
                slot += jnp.where(mine, lax.rem(owner, req), 0)
                length += jnp.where(mine, len_ref[source, i], 0)
            return slot, length

        def fresh(k, carry):
            slot, _ = slot_and_length(k)
            pick = (pick_u == (pick_i >> ilog2(req))) & ((pick_i & (req - 1)) == slot)
            rows = mm(pick.astype(jnp.bfloat16), new_rows)
            keys[k, pl.ds(CR, 16), :] = rows.astype(jnp.bfloat16)
            return carry

        lax.fori_loop(0, req, fresh, 0)
        load_pool.wait()

        def pack(r):
            over, across = hop(r)
            target = lax.rem(y + over, Y) * 2 + lax.rem(c + across, 2)
            first, second = jnp.int32(0), jnp.int32(0)
            for i in range(req):
                hit = lax.div(owner_ref[sect, i], req) == target
                first += jnp.where(hit, table_ref[sect, 0, i], 0)
                second += jnp.where(hit, table_ref[sect, 1, i], 0)
            return pool[first], pool[second]

        def pack_remote(r, carry):
            a, b = pack(r)
            pk[r, 0:block, :] = a
            pk[r, block:CR, :] = b
            return carry

        lax.fori_loop(1, sections, pack_remote, 0)
        a, b = pack(0)
        keys[0, 0:block, :] = a
        keys[0, block:CR, :] = b

        pl.semaphore_wait(barrier, len(peers))

        def cache_args(r):
            return pk.at[r], keys.at[r, pl.ds(0, CR), :], cs.at[r], cr.at[r], at_sect(r)

        for r in range(1, sections):
            send(*cache_args(r))

        wrows = pl.ds(pl.multiple_of(piece * PW, PW), PW)

        VH = lat_w // 2
        ways = Z // 2

        def core_rows(core):
            return pl.ds(pl.multiple_of(core * VH, VH), VH)

        def v1_args(h, d):
            sign = 1 - 2 * d
            some = pl.ds(d * (HD // 2), HD // 2) if h == ways else pl.ds(0, HD)
            rows = core_rows(c)
            if h == 1:
                part = vu_hbm.at[some, rows, :]
            else:
                part = vu.at[sign * (h - 1) % Z, some, rows, :]
            return part, vu.at[sign * h % Z, some, rows, :], v1s.at[d, h], v1r.at[d, h], at_z(sign + Z)

        def v3_args(r, core):
            part = vu.at[r, :, core_rows(core), :]
            return part, part, v3s.at[r], v3r.at[r], (sibling, dev)

        def v_step(h):
            if h > 1:
                for d in range(2):
                    arrived(*v1_args(h - 1, d))
            if h <= ways:
                for d in range(2):
                    send(*v1_args(h, d))
            if 1 < h <= ways:
                for r in (h - 1, Z - h + 1):
                    send(*v3_args(r, c))
            if h == ways + 1:
                send(*v3_args(ways, c))

        def w1_args(r):
            cols = pl.ds(pl.multiple_of(((x + r) % X) % 2 * NX, 128), NX)
            return op_hbm.at[wrows, cols], w.at[r, wrows, :], w1s.at[r], w1r.at[r], at_x(r)

        def from_y(r, size, part, parts):
            start = (c * Y + (y - r + Y) % Y) * size + part * (size // parts)
            return pl.ds(pl.multiple_of(start, size // parts), size // parts)

        def w2_args(r, rows, slot):
            part = w.at[pl.ds(1, X - 1), rows, :]
            return part, part, w2s.at[slot], w2r.at[slot], at_y(r)

        def y_start(args, size):
            send(*args(1, from_y(0, size, 0, 1), 0))
            if Y > 2:
                send(*args(Y - 1, from_y(0, size, 0, 1), 1))

        def w3_args(r, core):
            rows = pl.ds(pl.multiple_of((core * Y + (y - r + Y) % Y) * PW, PW), PW)
            part = w.at[pl.ds(1, X - 1), rows, :]
            return part, part, w3s.at[r], w3r.at[r], (sibling, dev)

        def y_forward(args, size, across):
            send(*across(0, c))
            arrived(*args(1, from_y(1, size, 0, 1), 0))
            if Y > 2:
                send(*args(1, from_y(1, size, 0, 2), 2))
                arrived(*args(Y - 1, from_y(Y - 1, size, 0, 1), 1))
                send(*args(Y - 1, from_y(Y - 1, size, 1, 2), 3))
                send(*across(Y - 1, c))
            send(*across(1, c))

        def y_finish(args, size, across):
            if Y > 2:
                arrived(*args(1, from_y(2, size, 0, 2), 2))
                arrived(*args(Y - 1, from_y(2, size, 1, 2), 3))
                send(*across(2, c))

        v_step(1)
        for r in range(1, X):
            send(*w1_args(r))

        swap_out = lax.broadcasted_iota(jnp.int32, (HZ * PS, HZ * PS), 0)
        swap_in = lax.broadcasted_iota(jnp.int32, (HZ * PS, HZ * PS), 1)
        swap = ((swap_out >> ilog2(PS)) == (swap_in & (HZ - 1))) & (
            (swap_out & (PS - 1)) == (swap_in >> ilog2(HZ))
        )
        swap = swap.astype(jnp.bfloat16)
        load_q.wait()

        def attend(k, k4):
            slot, length = slot_and_length(k)
            key_rows = keys[k]
            key_lat = keys[k, :, 0:lat_w]
            q_cols = jnp.concatenate([q[s, slot] for s in range(steps)], axis=1)
            scores = mm(key_rows, q_cols) * score_scale
            row = lax.broadcasted_iota(jnp.int32, scores.shape, 0)
            step = lax.broadcasted_iota(jnp.int32, scores.shape, 1) >> ilog2(heads)
            held = jnp.where(row < CR, length, CR + 1 + step)
            scores = jnp.where(row < held, scores, masked_score)
            weights = jnp.exp(scores - jnp.max(scores, axis=0, keepdims=True))
            probs = weights * (1.0 / jnp.sum(weights, axis=0, keepdims=True))
            out = tn_dot(probs.astype(jnp.bfloat16), key_lat).astype(jnp.bfloat16)
            lat[k4] = out.reshape(steps, heads, lat_w)

        def latent_args(r, pg):
            to = (x + r) % X
            return snd.at[to, pg], rcv.at[x, pg], ls.at[pg, r], lr.at[pg, r], at_x(r)

        def latent_from(r, pg):
            source = (x - r + X) % X
            return snd.at[source, pg], rcv.at[source, pg], ls.at[pg, r], lr.at[pg, r], at_x(r)

        local_latents = []

        def attention(pg):
            def one(k4, carry):
                k = pg * GROUP + k4

                @pl.when(k > 0)
                def _():
                    arrived(pk.at[k], keys.at[k, pl.ds(0, CR), :], cs.at[k], cr.at[k], at_sect(1))

                attend(k, k4)
                return carry

            lax.fori_loop(0, GROUP, one, 0)

            def turn(zz, carry):
                part = lat[:, :, pl.ds(pl.multiple_of(zz * HZ, HZ), HZ), :]
                turned = mm(swap, part.reshape(PS * HZ, lat_w)).astype(jnp.bfloat16)
                snd[:, pg, zz] = turned.reshape(X, HD * PS, lat_w)
                return carry

            lax.fori_loop(0, Z, turn, 0)
            for r in range(1, X):
                send(*latent_args(r, pg))
            own = pltpu.make_async_copy(snd.at[x, pg], rcv.at[x, pg], lsem.at[4 + pg])
            own.start()
            local_latents.append(own)

        def value_args(r, pg):
            to = (z + r) % Z
            return val.at[to, pg], vz.at[pg, :, z], zs.at[pg, r], zr.at[pg, r], at_z(r)

        def value_from(r, pg):
            source = (z - r + Z) % Z
            return val.at[source, pg], vz.at[pg, :, source], zs.at[pg, r], zr.at[pg, r], at_z(r)

        local_values = []

        def values(pg):
            for r in range(1, X):
                arrived(*latent_from(r, pg))
            local_latents[pg].wait()

            def ring(r, carry):
                zz = lax.rem(z - r + Z, Z)
                maps = jnp.concatenate([vu[r, hh] for hh in range(HD)], axis=1)
                full = mm(rcv[:, pg, zz].reshape(X * HD * PS, lat_w), maps)
                full = full.reshape(X, HD, PS, KD)
                for hh in range(HD):
                    cols = slice(hh * vdim, (hh + 1) * vdim)
                    part = full[:, hh, :, cols].reshape(PAIRS, PR, vdim).astype(jnp.bfloat16)
                    val[zz, pg, :, :, cols] = part
                return carry

            lax.fori_loop(0, Z, ring, 0)
            for r in range(1, Z):
                send(*value_args(r, pg))
            own = pltpu.make_async_copy(val.at[z, pg], vz.at[pg, :, z], lsem.at[4 + NG + pg])
            own.start()
            local_values.append(own)

        def gather_args(r, pg):
            to = ((x + r) % X) // 2
            return vz.at[pg, to], va.at[r, pg], gs.at[pg, r], gr.at[pg, r], at_x(r)

        def gather_start(pg):
            for r in range(1, Z):
                arrived(*value_from(r, pg))
            local_values[pg].wait()
            for r in range(1, X):
                send(*gather_args(r, pg))

        def ring_args(d, i, g):
            sign = 1 - 2 * d
            target = (z - sign * (1 + i) + Z) % Z
            held = po.at[target, g, d] if i == 0 else rs.at[d, g, i - 1]
            return held, rs.at[d, g, i], ss.at[d, g, i], sr.at[d, g, i], at_z(sign + Z)

        def ring_step(i, g):
            for d in range(2):
                arrived(*ring_args(d, i - 1, g))
                target = (z - (1 - 2 * d) * (1 + i) + 2 * Z) % Z
                total = rs[d, g, i - 1].astype(jnp.float32)
                total += po[target, g, d].astype(jnp.float32)
                rs[d, g, i - 1] = total.astype(jnp.bfloat16)
                send(*ring_args(d, i, g))

        def project(g):
            for r in range(1, X):
                arrived(*gather_args(r, g))
            for d in range(2):

                def tile(n, carry):
                    cols = pl.ds(pl.multiple_of(d * HX + n * NT, NT), NT)
                    acc = mm(vz[g, pair].reshape(Z * PR, KD), w[0, :, cols])
                    for r in range(1, X):
                        acc += mm(va[r, g].reshape(Z * PR, KD), w[r, :, cols])
                    part = acc.astype(jnp.bfloat16).reshape(Z, PR, NT)
                    po[:, g, d, :, pl.ds(pl.multiple_of(n * NT, NT), NT)] = part
                    return carry

                lax.fori_loop(0, HX // NT, tile, 0)
                send(*ring_args(d, 0, g))

        def final_args(pg, side):
            return so.at[pg, 1 - side], fin.at[side, pg], fs.at[pg], fr.at[pg], at_x(1 - 2 * half + X)

        local_final = []

        def reduce(pg):
            for d in range(2):
                totals = []
                for g in (2 * pg, 2 * pg + 1):
                    arrived(*ring_args(d, Z - 2, g))
                    total = po[z, g, d].astype(jnp.float32)
                    totals.append(total + rs[d, g, Z - 2].astype(jnp.float32))
                for m in range(2):
                    rows = jnp.concatenate([t[m * PS : (m + 1) * PS] for t in totals], axis=0)
                    so[pg, m, :, pl.ds(d * HX, HX)] = rows.astype(jnp.bfloat16)
            send(*final_args(pg, half))
            own = pltpu.make_async_copy(so.at[pg, half], fin.at[half, pg], lsem.at[4 + 2 * NG + pg])
            own.start()
            local_final.append(own)

        step = 2
        for g in range(NG):
            attention(g)
            if g != 1 and step <= ways:
                v_step(step)
                step += 1
        for r in range(1, X):
            arrived(*w1_args(r))
        y_start(w2_args, PW)
        while step <= ways + 1:
            v_step(step)
            step += 1
        load_vu.wait()
        for r in range(1, Z):
            arrived(*v3_args(r, 1 - c))
        for g in range(NG):
            values(g)
            if g:
                gather_start(g - 1)
            if g == 1:
                y_forward(w2_args, PW, w3_args)
            if g == max(NG - 2, 1):
                y_finish(w2_args, PW, w3_args)
                load_w.wait()
                for r in range(Y):
                    arrived(*w3_args(r, 1 - c))
                project(0)

        rings = [1]

        def hop_all(started):
            for g in range(started):
                if rings[g] < Z - 1:
                    ring_step(rings[g], g)
                elif rings[g] == Z - 1 and g % 2:
                    reduce(g // 2)
                rings[g] += 1

        if NG > 2:
            hop_all(1)
            project(1)
            rings.append(1)
        gather_start(NG - 1)
        while min(rings) < Z:
            started = len(rings)
            if started < NG:
                project(started)
            hop_all(started)
            if started < NG:
                rings.append(1)

        place_out = lax.broadcasted_iota(jnp.int32, (steps * req, steps * req), 0)
        place_in = lax.broadcasted_iota(jnp.int32, (steps * req, steps * req), 1)
        slots = jnp.zeros((steps * req, steps * req), jnp.int32)
        for k in range(req):
            slot, _ = slot_and_length(k)
            slots = jnp.where((place_in >> ilog2(steps)) == k, slot, slots)
        place = ((place_out >> ilog2(req)) == (place_in & (steps - 1))) & (
            (place_out & (req - 1)) == slots
        )
        place = place.astype(jnp.bfloat16)
        for pg in range(NPG):
            arrived(*final_args(pg, 1 - half))
            local_final[pg].wait()
        for side in range(2):
            rows = mm(place, fin[side].reshape(steps * req, NX))
            for s in range(steps):
                part = rows[s * req : (s + 1) * req].astype(jnp.bfloat16)
                out_ref[s, :, side * NX : (side + 1) * NX] = part

        for copy in sends:
            copy.wait_send()

    bf = jnp.bfloat16
    dma = pltpu.SemaphoreType.DMA
    scratch = [
        pltpu.VMEM((2 * req, block, width), bf),
        pltpu.VMEM((steps, req, width, heads), bf),
        pltpu.VMEM((sections, CR, width), bf),
        pltpu.VMEM((req, KR, width), bf),
        pltpu.VMEM((GROUP, steps, heads, lat_w), bf),
        pltpu.VMEM((X, NG, Z, HD * PS, lat_w), bf),
        pltpu.VMEM((X, NG, Z, HD * PS, lat_w), bf),
        pltpu.VMEM((Z, HD, lat_w, vdim), bf),
        pltpu.VMEM((Z, NG, PAIRS, PR, KD), bf),
        pltpu.VMEM((NG, PAIRS, Z, PR, KD), bf),
        pltpu.VMEM((X, NG, Z, PR, KD), bf),
        pltpu.VMEM((X, KD, NX), bf),
        pltpu.VMEM((Z, NG, 2, PR, HX), bf),
        pltpu.VMEM((2, NG, Z - 1, PR, HX), bf),
        pltpu.VMEM((NPG, 2, 2 * PS, NX), bf),
        pltpu.VMEM((2, NPG, 2 * PS, NX), bf),
        dma((4 + 2 * NG + NPG,)),
        dma((sections,)), dma((sections,)),
        dma((2, Z)), dma((2, Z)), dma((Z,)), dma((Z,)),
        dma((X,)), dma((X,)), dma((4,)), dma((4,)), dma((Y,)), dma((Y,)),
        dma((NG, X)), dma((NG, X)), dma((NG, Z)), dma((NG, Z)),
        dma((NG, X)), dma((NG, X)), dma((2, NG, Z)), dma((2, NG, Z)),
        dma((NPG,)), dma((NPG,)),
    ]
    return kernel, scratch


def on_device(
    prompt_lengths, owner_map, block_table, pool_blocks, queries, new_latents, value_up, out_proj
):
    sections, devices = lax.axis_size("sect"), lax.axis_size("dev")
    steps, req, heads, width = queries.shape
    _, lat_w, vdim = value_up.shape
    model = out_proj.shape[1]
    block = pool_blocks.shape[2]
    kernel, scratch = make_kernel(
        sections, devices // CHIPS_X, CHIPS_X, steps, req, heads, lat_w, width, vdim, model, block
    )
    smem = pl.BlockSpec(memory_space=pltpu.SMEM)
    vmem = pl.BlockSpec(memory_space=pltpu.VMEM)
    hbm = pl.BlockSpec(memory_space=pl.ANY)
    return pl.pallas_call(
        kernel,
        out_shape=jax.ShapeDtypeStruct((steps, req, model), jnp.bfloat16),
        in_specs=[smem, smem, smem, hbm, hbm, vmem, hbm, hbm],
        out_specs=vmem,
        scratch_shapes=scratch,
        compiler_params=pltpu.CompilerParams(
            collective_id=0, has_side_effects=True, vmem_limit_bytes=60 * 1024 * 1024
        ),
    )(
        owner_map,
        jnp.swapaxes(block_table, 1, 2),
        prompt_lengths,
        pool_blocks,
        jnp.swapaxes(queries, 2, 3),
        new_latents,
        value_up,
        out_proj,
    )


def solution(mesh):
    in_specs = (
        P(None, "dev"),
        P(None, "dev"),
        P(None, "dev", None),
        P("sect", "dev", None, None),
        P(None, ("sect", "dev"), None, None),
        P(None, ("sect", "dev"), None),
        P("dev", None, None),
        P("dev", None),
    )
    out_specs = P(None, ("sect", "dev"), None)
    return jax.shard_map(
        on_device, mesh=mesh, in_specs=in_specs, out_specs=out_specs, check_vma=False
    )
```

```python
import jax
import jax.numpy as jnp
from jax import lax
from jax.experimental import pallas as pl
from jax.experimental.pallas import tpu as pltpu
from jax.sharding import PartitionSpec as P

MESH = pl.DeviceIdType.MESH
CHIPS_X = 4
GROUP = 2
score_scale = 192.0 ** (-0.5)
masked_score = -1e30


def ilog2(n):
    return n.bit_length() - 1


def tn_dot(a, b):
    return lax.dot_general(a, b, (((0,), (0,)), ((), ())), preferred_element_type=jnp.float32)


def mm(a, b):
    return jnp.dot(a, b, preferred_element_type=jnp.float32)


def make_kernel(sections, chips_z, chips_x, steps, req, heads, lat_w, width, vdim, model, block):
    Y, Z, X = sections // 2, chips_z, chips_x
    HD = heads // (Z * X)
    HZ = HD * X
    NG = req // GROUP
    NPG = NG // 2
    PS = GROUP * steps
    CR = 2 * block
    KR = CR + 16
    PAIRS = X // 2
    NX = model // 2
    HX = NX // 2
    PR = 2 * PS
    NT = 256
    KD = HD * vdim
    PW = KD // (2 * Y)

    def kernel(
        owner_ref, table_ref, len_ref, pool_hbm, q_hbm, new_ref, vu_hbm, op_hbm, out_ref,
        pool, q, pk, keys, lat, snd, rcv, vu, val, vz, va, w, po, rs, so, fin,
        lsem, cs, cr, v1s, v1r, v3s, v3r, w1s, w1r, w2s, w2r, w3s, w3r,
        ls, lr, zs, zr, gs, gr, ss, sr, fs, fr,
    ):
        sect = lax.axis_index("sect")
        dev = lax.axis_index("dev")
        y, c = sect // 2, sect % 2
        z, x = dev // X, dev % X
        sibling = y * 2 + (1 - c)
        piece = c * Y + y
        pair, half = x // 2, x % 2
        sends = []

        hops = [(0, 0), (0, 1), (1, 0), (Y - 1, 0), (1, 1), (Y - 1, 1), (2, 0), (2, 1)]
        if Y == 2:
            hops = [(0, 0), (0, 1), (1, 0), (1, 1)]

        def hop(k):
            if isinstance(k, int):
                return hops[k]
            over, across = jnp.int32(0), jnp.int32(0)
            for i, (a, b) in enumerate(hops):
                over += jnp.where(k == i, a, 0)
                across += jnp.where(k == i, b, 0)
            return over, across

        def at_sect(k):
            over, across = hops[k]
            return ((y + over) % Y * 2 + (c + across) % 2, dev)

        def at_y(r):
            return (((y + r) % Y) * 2 + c, dev)

        def at_z(r):
            return (sect, ((z + r) % Z) * X + x)

        def at_x(r):
            return (sect, z * X + (x + r) % X)

        def remote(src, dst, send_sem, recv_sem, to):
            return pltpu.make_async_remote_copy(
                src_ref=src, dst_ref=dst, send_sem=send_sem, recv_sem=recv_sem,
                device_id=to, device_id_type=MESH,
            )

        def send(src, dst, send_sem, recv_sem, to):
            copy = remote(src, dst, send_sem, recv_sem, to)
            copy.start()
            sends.append(copy)

        def arrived(src, dst, send_sem, recv_sem, to):
            remote(src, dst, send_sem, recv_sem, to).wait_recv()

        load_pool = pltpu.make_async_copy(pool_hbm.at[0], pool, lsem.at[0])
        load_q = pltpu.make_async_copy(q_hbm, q, lsem.at[1])
        load_vu = pltpu.make_async_copy(vu_hbm, vu.at[0], lsem.at[2])
        own_cols = pl.ds(pl.multiple_of(half * NX, 128), NX)
        load_w = pltpu.make_async_copy(op_hbm.at[:, own_cols], w.at[0], lsem.at[3])
        load_pool.start()
        load_q.start()
        load_vu.start()
        load_w.start()

        barrier = pltpu.get_barrier_semaphore()
        peers = [at_sect(r) for r in range(1, sections)]
        peers += [at_z(r) for r in range(1, Z)] + [at_x(r) for r in range(1, X)]
        for peer in peers:
            pl.semaphore_signal(barrier, inc=1, device_id=peer, device_id_type=MESH)

        new_rows = new_ref[...].astype(jnp.float32).reshape(steps * req, width)
        new_rows = new_rows.astype(jnp.bfloat16)
        pick_u = lax.broadcasted_iota(jnp.int32, (16, steps * req), 0)
        pick_i = lax.broadcasted_iota(jnp.int32, (16, steps * req), 1)

        def slot_and_length(k):
            over, across = hop(k)
            source = lax.rem(y - over + Y, Y) * 2 + lax.rem(c + across, 2)
            slot, length = jnp.int32(0), jnp.int32(0)
            for i in range(req):
                owner = owner_ref[source, i]
                mine = lax.div(owner, req) == sect
                slot += jnp.where(mine, lax.rem(owner, req), 0)
                length += jnp.where(mine, len_ref[source, i], 0)
            return slot, length

        def fresh(k, carry):
            slot, _ = slot_and_length(k)
            pick = (pick_u == (pick_i >> ilog2(req))) & ((pick_i & (req - 1)) == slot)
            rows = mm(pick.astype(jnp.bfloat16), new_rows)
            keys[k, pl.ds(CR, 16), :] = rows.astype(jnp.bfloat16)
            return carry

        lax.fori_loop(0, req, fresh, 0)
        load_pool.wait()

        def pack(r):
            over, across = hop(r)
            target = lax.rem(y + over, Y) * 2 + lax.rem(c + across, 2)
            first, second = jnp.int32(0), jnp.int32(0)
            for i in range(req):
                hit = lax.div(owner_ref[sect, i], req) == target
                first += jnp.where(hit, table_ref[sect, 0, i], 0)
                second += jnp.where(hit, table_ref[sect, 1, i], 0)
            return pool[first], pool[second]

        def pack_remote(r, carry):
            a, b = pack(r)
            pk[r, 0:block, :] = a
            pk[r, block:CR, :] = b
            return carry

        lax.fori_loop(1, sections, pack_remote, 0)
        a, b = pack(0)
        keys[0, 0:block, :] = a
        keys[0, block:CR, :] = b

        pl.semaphore_wait(barrier, len(peers))

        def cache_args(r):
            return pk.at[r], keys.at[r, pl.ds(0, CR), :], cs.at[r], cr.at[r], at_sect(r)

        for r in range(1, sections):
            send(*cache_args(r))

        wrows = pl.ds(pl.multiple_of(piece * PW, PW), PW)

        VH = lat_w // 2
        ways = Z // 2

        def core_rows(core):
            return pl.ds(pl.multiple_of(core * VH, VH), VH)

        def v1_args(h, d):
            sign = 1 - 2 * d
            some = pl.ds(d * (HD // 2), HD // 2) if h == ways else pl.ds(0, HD)
            rows = core_rows(c)
            if h == 1:
                part = vu_hbm.at[some, rows, :]
            else:
                part = vu.at[sign * (h - 1) % Z, some, rows, :]
            return part, vu.at[sign * h % Z, some, rows, :], v1s.at[d, h], v1r.at[d, h], at_z(sign + Z)

        def v3_args(r, core):
            part = vu.at[r, :, core_rows(core), :]
            return part, part, v3s.at[r], v3r.at[r], (sibling, dev)

        def v_step(h):
            if h > 1:
                for d in range(2):
                    arrived(*v1_args(h - 1, d))
            if h <= ways:
                for d in range(2):
                    send(*v1_args(h, d))
            if 1 < h <= ways:
                for r in (h - 1, Z - h + 1):
                    send(*v3_args(r, c))
            if h == ways + 1:
                send(*v3_args(ways, c))

        def w1_args(r):
            cols = pl.ds(pl.multiple_of(((x + r) % X) % 2 * NX, 128), NX)
            return op_hbm.at[wrows, cols], w.at[r, wrows, :], w1s.at[r], w1r.at[r], at_x(r)

        def from_y(r, size, part, parts):
            start = (c * Y + (y - r + Y) % Y) * size + part * (size // parts)
            return pl.ds(pl.multiple_of(start, size // parts), size // parts)

        def w2_args(shard):
            def args(r, rows, slot):
                part = w.at[shard, rows, :]
                return part, part, w2s.at[shard, slot], w2r.at[shard, slot], at_y(r)

            return args

        def y_start(args, size):
            send(*args(1, from_y(0, size, 0, 1), 0))
            if Y > 2:
                send(*args(Y - 1, from_y(0, size, 0, 1), 1))

        def w3_args(shard):
            def args(r, core):
                rows = pl.ds(pl.multiple_of((core * Y + (y - r + Y) % Y) * PW, PW), PW)
                part = w.at[shard, rows, :]
                return part, part, w3s.at[shard, r], w3r.at[shard, r], (sibling, dev)

            return args

        def y_forward(args, size, across):
            send(*across(0, c))
            arrived(*args(1, from_y(1, size, 0, 1), 0))
            if Y > 2:
                send(*args(1, from_y(1, size, 0, 2), 2))
                arrived(*args(Y - 1, from_y(Y - 1, size, 0, 1), 1))
                send(*args(Y - 1, from_y(Y - 1, size, 1, 2), 3))
                send(*across(Y - 1, c))
            send(*across(1, c))

        def y_finish(args, size, across):
            if Y > 2:
                arrived(*args(1, from_y(2, size, 0, 2), 2))
                arrived(*args(Y - 1, from_y(2, size, 1, 2), 3))
                send(*across(2, c))

        v_step(1)
        blocks = [1, X - 1, 2] if X > 2 else [1]
        for r in blocks:
            send(*w1_args(r))

        swap_out = lax.broadcasted_iota(jnp.int32, (HZ * PS, HZ * PS), 0)
        swap_in = lax.broadcasted_iota(jnp.int32, (HZ * PS, HZ * PS), 1)
        swap = ((swap_out >> ilog2(PS)) == (swap_in & (HZ - 1))) & (
            (swap_out & (PS - 1)) == (swap_in >> ilog2(HZ))
        )
        swap = swap.astype(jnp.bfloat16)
        load_q.wait()

        def attend(k, k4):
            slot, length = slot_and_length(k)
            key_rows = keys[k]
            key_lat = keys[k, :, 0:lat_w]
            q_cols = jnp.concatenate([q[s, slot] for s in range(steps)], axis=1)
            scores = mm(key_rows, q_cols) * score_scale
            row = lax.broadcasted_iota(jnp.int32, scores.shape, 0)
            step = lax.broadcasted_iota(jnp.int32, scores.shape, 1) >> ilog2(heads)
            held = jnp.where(row < CR, length, CR + 1 + step)
            scores = jnp.where(row < held, scores, masked_score)
            weights = jnp.exp(scores - jnp.max(scores, axis=0, keepdims=True))
            probs = weights * (1.0 / jnp.sum(weights, axis=0, keepdims=True))
            out = tn_dot(probs.astype(jnp.bfloat16), key_lat).astype(jnp.bfloat16)
            lat[k4] = out.reshape(steps, heads, lat_w)

        def latent_args(r, pg):
            to = (x + r) % X
            return snd.at[to, pg], rcv.at[x, pg], ls.at[pg, r], lr.at[pg, r], at_x(r)

        def latent_from(r, pg):
            source = (x - r + X) % X
            return snd.at[source, pg], rcv.at[source, pg], ls.at[pg, r], lr.at[pg, r], at_x(r)

        local_latents = []

        def attention(pg):
            def one(k4, carry):
                k = pg * GROUP + k4

                @pl.when(k > 0)
                def _():
                    arrived(pk.at[k], keys.at[k, pl.ds(0, CR), :], cs.at[k], cr.at[k], at_sect(1))

                attend(k, k4)
                return carry

            lax.fori_loop(0, GROUP, one, 0)

            def turn(zz, carry):
                part = lat[:, :, pl.ds(pl.multiple_of(zz * HZ, HZ), HZ), :]
                turned = mm(swap, part.reshape(PS * HZ, lat_w)).astype(jnp.bfloat16)
                snd[:, pg, zz] = turned.reshape(X, HD * PS, lat_w)
                return carry

            lax.fori_loop(0, Z, turn, 0)
            for r in range(1, X):
                send(*latent_args(r, pg))
            own = pltpu.make_async_copy(snd.at[x, pg], rcv.at[x, pg], lsem.at[4 + pg])
            own.start()
            local_latents.append(own)

        def value_args(r, pg):
            to = (z + r) % Z
            return val.at[to, pg], vz.at[pg, :, z], zs.at[pg, r], zr.at[pg, r], at_z(r)

        def value_from(r, pg):
            source = (z - r + Z) % Z
            return val.at[source, pg], vz.at[pg, :, source], zs.at[pg, r], zr.at[pg, r], at_z(r)

        local_values = []

        def values(pg):
            for r in range(1, X):
                arrived(*latent_from(r, pg))
            local_latents[pg].wait()

            def ring(r, carry):
                zz = lax.rem(z - r + Z, Z)
                maps = jnp.concatenate([vu[r, hh] for hh in range(HD)], axis=1)
                full = mm(rcv[:, pg, zz].reshape(X * HD * PS, lat_w), maps)
                full = full.reshape(X, HD, PS, KD)
                for hh in range(HD):
                    cols = slice(hh * vdim, (hh + 1) * vdim)
                    part = full[:, hh, :, cols].reshape(PAIRS, PR, vdim).astype(jnp.bfloat16)
                    val[zz, pg, :, :, cols] = part
                return carry

            lax.fori_loop(0, Z, ring, 0)
            for r in range(1, Z):
                send(*value_args(r, pg))
            own = pltpu.make_async_copy(val.at[z, pg], vz.at[pg, :, z], lsem.at[4 + NG + pg])
            own.start()
            local_values.append(own)

        def gather_args(r, pg):
            to = ((x + r) % X) // 2
            return vz.at[pg, to], va.at[r, pg], gs.at[pg, r], gr.at[pg, r], at_x(r)

        def gather_start(pg):
            for r in range(1, Z):
                arrived(*value_from(r, pg))
            local_values[pg].wait()
            for r in range(1, X):
                send(*gather_args(r, pg))

        def ring_args(d, i, g):
            sign = 1 - 2 * d
            target = (z - sign * (1 + i) + Z) % Z
            held = po.at[target, g, d] if i == 0 else rs.at[d, g, i - 1]
            return held, rs.at[d, g, i], ss.at[d, g, i], sr.at[d, g, i], at_z(sign + Z)

        def ring_step(i, g):
            for d in range(2):
                arrived(*ring_args(d, i - 1, g))
                target = (z - (1 - 2 * d) * (1 + i) + 2 * Z) % Z
                total = rs[d, g, i - 1].astype(jnp.float32)
                total += po[target, g, d].astype(jnp.float32)
                rs[d, g, i - 1] = total.astype(jnp.bfloat16)
                send(*ring_args(d, i, g))

        def project(g):
            for r in range(1, X):
                arrived(*gather_args(r, g))
            for d in range(2):

                def tile(n, carry):
                    cols = pl.ds(pl.multiple_of(d * HX + n * NT, NT), NT)
                    acc = mm(vz[g, pair].reshape(Z * PR, KD), w[0, :, cols])
                    for r in range(1, X):
                        acc += mm(va[r, g].reshape(Z * PR, KD), w[r, :, cols])
                    part = acc.astype(jnp.bfloat16).reshape(Z, PR, NT)
                    po[:, g, d, :, pl.ds(pl.multiple_of(n * NT, NT), NT)] = part
                    return carry

                lax.fori_loop(0, HX // NT, tile, 0)
                send(*ring_args(d, 0, g))

        def final_args(pg, side):
            return so.at[pg, 1 - side], fin.at[side, pg], fs.at[pg], fr.at[pg], at_x(1 - 2 * half + X)

        local_final = []

        def reduce(pg):
            for d in range(2):
                totals = []
                for g in (2 * pg, 2 * pg + 1):
                    arrived(*ring_args(d, Z - 2, g))
                    total = po[z, g, d].astype(jnp.float32)
                    totals.append(total + rs[d, g, Z - 2].astype(jnp.float32))
                for m in range(2):
                    rows = jnp.concatenate([t[m * PS : (m + 1) * PS] for t in totals], axis=0)
                    so[pg, m, :, pl.ds(d * HX, HX)] = rows.astype(jnp.bfloat16)
            send(*final_args(pg, half))
            own = pltpu.make_async_copy(so.at[pg, half], fin.at[half, pg], lsem.at[4 + 2 * NG + pg])
            own.start()
            local_final.append(own)

        step = 2
        for g in range(NG):
            attention(g)
            if g != 1 and step <= ways:
                v_step(step)
                step += 1
        for r in blocks[:2]:
            arrived(*w1_args(r))
            y_start(w2_args(r), PW)
        while step <= ways + 1:
            v_step(step)
            step += 1
        load_vu.wait()
        for r in range(1, Z):
            arrived(*v3_args(r, 1 - c))
        for r in blocks[2:]:
            arrived(*w1_args(r))
            y_start(w2_args(r), PW)
        for g in range(NG):
            values(g)
            if g == 0:
                for r in blocks[:2]:
                    y_forward(w2_args(r), PW, w3_args(r))
            if g:
                gather_start(g - 1)
            if g == 1:
                for r in blocks[2:]:
                    y_forward(w2_args(r), PW, w3_args(r))
            if g == NG - 2:
                for r in blocks:
                    y_finish(w2_args(r), PW, w3_args(r))
        load_w.wait()
        for shard in blocks:
            for r in range(Y):
                arrived(*w3_args(shard)(r, 1 - c))
        project(0)
        gather_start(NG - 1)
        rings = [1]
        while min(rings) < Z:
            started = len(rings)
            if started < NG:
                project(started)
            for g in range(started):
                if rings[g] < Z - 1:
                    ring_step(rings[g], g)
                elif rings[g] == Z - 1 and g % 2:
                    reduce(g // 2)
                rings[g] += 1
            if started < NG:
                rings.append(1)

        place_out = lax.broadcasted_iota(jnp.int32, (steps * req, steps * req), 0)
        place_in = lax.broadcasted_iota(jnp.int32, (steps * req, steps * req), 1)
        slots = jnp.zeros((steps * req, steps * req), jnp.int32)
        for k in range(req):
            slot, _ = slot_and_length(k)
            slots = jnp.where((place_in >> ilog2(steps)) == k, slot, slots)
        place = ((place_out >> ilog2(req)) == (place_in & (steps - 1))) & (
            (place_out & (req - 1)) == slots
        )
        place = place.astype(jnp.bfloat16)
        for pg in range(NPG):
            arrived(*final_args(pg, 1 - half))
            local_final[pg].wait()
        for side in range(2):
            rows = mm(place, fin[side].reshape(steps * req, NX))
            for s in range(steps):
                part = rows[s * req : (s + 1) * req].astype(jnp.bfloat16)
                out_ref[s, :, side * NX : (side + 1) * NX] = part

        for copy in sends:
            copy.wait_send()

    bf = jnp.bfloat16
    dma = pltpu.SemaphoreType.DMA
    scratch = [
        pltpu.VMEM((2 * req, block, width), bf),
        pltpu.VMEM((steps, req, width, heads), bf),
        pltpu.VMEM((sections, CR, width), bf),
        pltpu.VMEM((req, KR, width), bf),
        pltpu.VMEM((GROUP, steps, heads, lat_w), bf),
        pltpu.VMEM((X, NG, Z, HD * PS, lat_w), bf),
        pltpu.VMEM((X, NG, Z, HD * PS, lat_w), bf),
        pltpu.VMEM((Z, HD, lat_w, vdim), bf),
        pltpu.VMEM((Z, NG, PAIRS, PR, KD), bf),
        pltpu.VMEM((NG, PAIRS, Z, PR, KD), bf),
        pltpu.VMEM((X, NG, Z, PR, KD), bf),
        pltpu.VMEM((X, KD, NX), bf),
        pltpu.VMEM((Z, NG, 2, PR, HX), bf),
        pltpu.VMEM((2, NG, Z - 1, PR, HX), bf),
        pltpu.VMEM((NPG, 2, 2 * PS, NX), bf),
        pltpu.VMEM((2, NPG, 2 * PS, NX), bf),
        dma((4 + 2 * NG + NPG,)),
        dma((sections,)), dma((sections,)),
        dma((2, Z)), dma((2, Z)), dma((Z,)), dma((Z,)),
        dma((X,)), dma((X,)), dma((X, 4)), dma((X, 4)), dma((X, Y)), dma((X, Y)),
        dma((NG, X)), dma((NG, X)), dma((NG, Z)), dma((NG, Z)),
        dma((NG, X)), dma((NG, X)), dma((2, NG, Z)), dma((2, NG, Z)),
        dma((NPG,)), dma((NPG,)),
    ]
    return kernel, scratch


def on_device(
    prompt_lengths, owner_map, block_table, pool_blocks, queries, new_latents, value_up, out_proj
):
    sections, devices = lax.axis_size("sect"), lax.axis_size("dev")
    steps, req, heads, width = queries.shape
    _, lat_w, vdim = value_up.shape
    model = out_proj.shape[1]
    block = pool_blocks.shape[2]
    kernel, scratch = make_kernel(
        sections, devices // CHIPS_X, CHIPS_X, steps, req, heads, lat_w, width, vdim, model, block
    )
    smem = pl.BlockSpec(memory_space=pltpu.SMEM)
    vmem = pl.BlockSpec(memory_space=pltpu.VMEM)
    hbm = pl.BlockSpec(memory_space=pl.ANY)
    return pl.pallas_call(
        kernel,
        out_shape=jax.ShapeDtypeStruct((steps, req, model), jnp.bfloat16),
        in_specs=[smem, smem, smem, hbm, hbm, vmem, hbm, hbm],
        out_specs=vmem,
        scratch_shapes=scratch,
        compiler_params=pltpu.CompilerParams(
            collective_id=0, has_side_effects=True, vmem_limit_bytes=60 * 1024 * 1024
        ),
    )(
        owner_map,
        jnp.swapaxes(block_table, 1, 2),
        prompt_lengths,
        pool_blocks,
        jnp.swapaxes(queries, 2, 3),
        new_latents,
        value_up,
        out_proj,
    )


def solution(mesh):
    in_specs = (
        P(None, "dev"),
        P(None, "dev"),
        P(None, "dev", None),
        P("sect", "dev", None, None),
        P(None, ("sect", "dev"), None, None),
        P(None, ("sect", "dev"), None),
        P("dev", None, None),
        P("dev", None),
    )
    out_specs = P(None, ("sect", "dev"), None)
    return jax.shard_map(
        on_device, mesh=mesh, in_specs=in_specs, out_specs=out_specs, check_vma=False
    )
```

```python
import jax
import jax.numpy as jnp
from jax import lax
from jax.experimental import pallas as pl
from jax.experimental.pallas import tpu as pltpu
from jax.sharding import PartitionSpec as P

MESH = pl.DeviceIdType.MESH
CHIPS_X = 4
GROUP = 2
score_scale = 192.0 ** (-0.5)
masked_score = -1e30


def ilog2(n):
    return n.bit_length() - 1


def tn_dot(a, b):
    return lax.dot_general(a, b, (((0,), (0,)), ((), ())), preferred_element_type=jnp.float32)


def mm(a, b):
    return jnp.dot(a, b, preferred_element_type=jnp.float32)


def make_kernel(sections, chips_z, chips_x, steps, req, heads, lat_w, width, vdim, model, block):
    Y, Z, X = sections // 2, chips_z, chips_x
    HD = heads // (Z * X)
    HZ = HD * X
    NG = req // GROUP
    NPG = NG // 2
    PS = GROUP * steps
    CR = 2 * block
    KR = CR + 16
    PAIRS = X // 2
    NX = model // 2
    HX = NX // 2
    PR = 2 * PS
    NT = HX // 2
    KD = HD * vdim
    PW = KD // (2 * Y)

    def kernel(
        owner_ref, table_ref, len_ref, pool_hbm, q_hbm, new_ref, vu_hbm, op_hbm, out_ref,
        pool, q, pk, keys, lat, snd, rcv, vu, val, vz, va, w, po, rs, so, fin,
        lsem, cs, cr, v1s, v1r, v3s, v3r, w1s, w1r, w2s, w2r, w3s, w3r,
        ls, lr, zs, zr, gs, gr, ss, sr, fs, fr,
    ):
        sect = lax.axis_index("sect")
        dev = lax.axis_index("dev")
        y, c = sect // 2, sect % 2
        z, x = dev // X, dev % X
        sibling = y * 2 + (1 - c)
        piece = c * Y + y
        pair, half = x // 2, x % 2
        sends = []

        hops = [(0, 0), (0, 1), (1, 0), (Y - 1, 0), (1, 1), (Y - 1, 1), (2, 0), (2, 1)]
        if Y == 2:
            hops = [(0, 0), (0, 1), (1, 0), (1, 1)]

        def hop(k):
            if isinstance(k, int):
                return hops[k]
            over, across = jnp.int32(0), jnp.int32(0)
            for i, (a, b) in enumerate(hops):
                over += jnp.where(k == i, a, 0)
                across += jnp.where(k == i, b, 0)
            return over, across

        def at_sect(k):
            over, across = hops[k]
            return ((y + over) % Y * 2 + (c + across) % 2, dev)

        def at_y(r):
            return (((y + r) % Y) * 2 + c, dev)

        def at_z(r):
            return (sect, ((z + r) % Z) * X + x)

        def at_x(r):
            return (sect, z * X + (x + r) % X)

        def remote(src, dst, send_sem, recv_sem, to):
            return pltpu.make_async_remote_copy(
                src_ref=src, dst_ref=dst, send_sem=send_sem, recv_sem=recv_sem,
                device_id=to, device_id_type=MESH,
            )

        def send(src, dst, send_sem, recv_sem, to):
            copy = remote(src, dst, send_sem, recv_sem, to)
            copy.start()
            sends.append(copy)

        def arrived(src, dst, send_sem, recv_sem, to):
            remote(src, dst, send_sem, recv_sem, to).wait_recv()

        load_pool = pltpu.make_async_copy(pool_hbm.at[0], pool, lsem.at[0])
        load_q = pltpu.make_async_copy(q_hbm, q, lsem.at[1])
        load_vu = pltpu.make_async_copy(vu_hbm, vu.at[0], lsem.at[2])
        own_cols = pl.ds(pl.multiple_of(half * NX, 128), NX)
        load_w = pltpu.make_async_copy(op_hbm.at[:, own_cols], w.at[0], lsem.at[3])
        load_pool.start()
        load_q.start()
        load_vu.start()
        load_w.start()

        barrier = pltpu.get_barrier_semaphore()
        peers = [at_sect(r) for r in range(1, sections)]
        peers += [at_z(r) for r in range(1, Z)] + [at_x(r) for r in range(1, X)]
        for peer in peers:
            pl.semaphore_signal(barrier, inc=1, device_id=peer, device_id_type=MESH)

        new_rows = new_ref[...].astype(jnp.float32).reshape(steps * req, width)
        new_rows = new_rows.astype(jnp.bfloat16)
        pick_u = lax.broadcasted_iota(jnp.int32, (16, steps * req), 0)
        pick_i = lax.broadcasted_iota(jnp.int32, (16, steps * req), 1)

        def slot_and_length(k):
            over, across = hop(k)
            source = lax.rem(y - over + Y, Y) * 2 + lax.rem(c + across, 2)
            slot, length = jnp.int32(0), jnp.int32(0)
            for i in range(req):
                owner = owner_ref[source, i]
                mine = lax.div(owner, req) == sect
                slot += jnp.where(mine, lax.rem(owner, req), 0)
                length += jnp.where(mine, len_ref[source, i], 0)
            return slot, length

        def fresh(k, carry):
            slot, _ = slot_and_length(k)
            pick = (pick_u == (pick_i >> ilog2(req))) & ((pick_i & (req - 1)) == slot)
            rows = mm(pick.astype(jnp.bfloat16), new_rows)
            keys[k, pl.ds(CR, 16), :] = rows.astype(jnp.bfloat16)
            return carry

        lax.fori_loop(0, req, fresh, 0)
        load_pool.wait()

        def pack(r):
            over, across = hop(r)
            target = lax.rem(y + over, Y) * 2 + lax.rem(c + across, 2)
            first, second = jnp.int32(0), jnp.int32(0)
            for i in range(req):
                hit = lax.div(owner_ref[sect, i], req) == target
                first += jnp.where(hit, table_ref[sect, 0, i], 0)
                second += jnp.where(hit, table_ref[sect, 1, i], 0)
            return pool[first], pool[second]

        def pack_remote(r, carry):
            a, b = pack(r)
            pk[r, 0:block, :] = a
            pk[r, block:CR, :] = b
            return carry

        lax.fori_loop(1, sections, pack_remote, 0)
        a, b = pack(0)
        keys[0, 0:block, :] = a
        keys[0, block:CR, :] = b

        pl.semaphore_wait(barrier, len(peers))

        def cache_args(r):
            return pk.at[r], keys.at[r, pl.ds(0, CR), :], cs.at[r], cr.at[r], at_sect(r)

        for r in range(1, sections):
            send(*cache_args(r))

        wrows = pl.ds(pl.multiple_of(piece * PW, PW), PW)

        VH = lat_w // 2
        ways = Z // 2

        def core_rows(core):
            return pl.ds(pl.multiple_of(core * VH, VH), VH)

        def v1_args(h, d):
            sign = 1 - 2 * d
            some = pl.ds(d * (HD // 2), HD // 2) if h == ways else pl.ds(0, HD)
            rows = core_rows(c)
            if h == 1:
                part = vu_hbm.at[some, rows, :]
            else:
                part = vu.at[sign * (h - 1) % Z, some, rows, :]
            return part, vu.at[sign * h % Z, some, rows, :], v1s.at[d, h], v1r.at[d, h], at_z(sign + Z)

        def v3_args(r, core):
            part = vu.at[r, :, core_rows(core), :]
            return part, part, v3s.at[r], v3r.at[r], (sibling, dev)

        def v_step(h):
            if h > 1:
                for d in range(2):
                    arrived(*v1_args(h - 1, d))
            if h <= ways:
                for d in range(2):
                    send(*v1_args(h, d))
            if 1 < h <= ways:
                for r in (h - 1, Z - h + 1):
                    send(*v3_args(r, c))
            if h == ways + 1:
                send(*v3_args(ways, c))

        def w1_args(r):
            cols = pl.ds(pl.multiple_of(((x + r) % X) % 2 * NX, 128), NX)
            return op_hbm.at[wrows, cols], w.at[r, wrows, :], w1s.at[r], w1r.at[r], at_x(r)

        def from_y(r, size, part, parts):
            start = (c * Y + (y - r + Y) % Y) * size + part * (size // parts)
            return pl.ds(pl.multiple_of(start, size // parts), size // parts)

        def w2_args(r, rows, slot):
            part = w.at[pl.ds(1, X - 1), rows, :]
            return part, part, w2s.at[slot], w2r.at[slot], at_y(r)

        def y_start(args, size):
            send(*args(1, from_y(0, size, 0, 1), 0))
            if Y > 2:
                send(*args(Y - 1, from_y(0, size, 0, 1), 1))

        def w3_args(r, core):
            rows = pl.ds(pl.multiple_of((core * Y + (y - r + Y) % Y) * PW, PW), PW)
            part = w.at[pl.ds(1, X - 1), rows, :]
            return part, part, w3s.at[r], w3r.at[r], (sibling, dev)

        def y_forward(args, size, across):
            send(*across(0, c))
            arrived(*args(1, from_y(1, size, 0, 1), 0))
            if Y > 2:
                send(*args(1, from_y(1, size, 0, 2), 2))
                arrived(*args(Y - 1, from_y(Y - 1, size, 0, 1), 1))
                send(*args(Y - 1, from_y(Y - 1, size, 1, 2), 3))
                send(*across(Y - 1, c))
            send(*across(1, c))

        def y_finish(args, size, across):
            if Y > 2:
                arrived(*args(1, from_y(2, size, 0, 2), 2))
                arrived(*args(Y - 1, from_y(2, size, 1, 2), 3))
                send(*across(2, c))

        v_step(1)
        for r in range(1, X):
            send(*w1_args(r))

        swap_out = lax.broadcasted_iota(jnp.int32, (HZ * PS, HZ * PS), 0)
        swap_in = lax.broadcasted_iota(jnp.int32, (HZ * PS, HZ * PS), 1)
        swap = ((swap_out >> ilog2(PS)) == (swap_in & (HZ - 1))) & (
            (swap_out & (PS - 1)) == (swap_in >> ilog2(HZ))
        )
        swap = swap.astype(jnp.bfloat16)
        load_q.wait()

        def attend(k, k4):
            slot, length = slot_and_length(k)
            key_rows = keys[k]
            key_lat = keys[k, :, 0:lat_w]
            q_cols = jnp.concatenate([q[s, slot] for s in range(steps)], axis=1)
            scores = mm(key_rows, q_cols) * score_scale
            row = lax.broadcasted_iota(jnp.int32, scores.shape, 0)
            step = lax.broadcasted_iota(jnp.int32, scores.shape, 1) >> ilog2(heads)
            held = jnp.where(row < CR, length, CR + 1 + step)
            scores = jnp.where(row < held, scores, masked_score)
            weights = jnp.exp(scores - jnp.max(scores, axis=0, keepdims=True))
            probs = weights * (1.0 / jnp.sum(weights, axis=0, keepdims=True))
            out = tn_dot(probs.astype(jnp.bfloat16), key_lat).astype(jnp.bfloat16)
            lat[k4] = out.reshape(steps, heads, lat_w)

        def latent_args(r, pg):
            to = (x + r) % X
            return snd.at[to, pg], rcv.at[x, pg], ls.at[pg, r], lr.at[pg, r], at_x(r)

        def latent_from(r, pg):
            source = (x - r + X) % X
            return snd.at[source, pg], rcv.at[source, pg], ls.at[pg, r], lr.at[pg, r], at_x(r)

        local_latents = []

        def attention(pg):
            def one(k4, carry):
                k = pg * GROUP + k4

                @pl.when(k > 0)
                def _():
                    arrived(pk.at[k], keys.at[k, pl.ds(0, CR), :], cs.at[k], cr.at[k], at_sect(1))

                attend(k, k4)
                return carry

            lax.fori_loop(0, GROUP, one, 0)

            def turn(zz, carry):
                part = lat[:, :, pl.ds(pl.multiple_of(zz * HZ, HZ), HZ), :]
                turned = mm(swap, part.reshape(PS * HZ, lat_w)).astype(jnp.bfloat16)
                snd[:, pg, zz] = turned.reshape(X, HD * PS, lat_w)
                return carry

            lax.fori_loop(0, Z, turn, 0)
            for r in range(1, X):
                send(*latent_args(r, pg))
            own = pltpu.make_async_copy(snd.at[x, pg], rcv.at[x, pg], lsem.at[4 + pg])
            own.start()
            local_latents.append(own)

        def value_args(r, pg):
            to = (z + r) % Z
            return val.at[to, pg], vz.at[pg, :, z], zs.at[pg, r], zr.at[pg, r], at_z(r)

        def value_from(r, pg):
            source = (z - r + Z) % Z
            return val.at[source, pg], vz.at[pg, :, source], zs.at[pg, r], zr.at[pg, r], at_z(r)

        local_values = []

        def values(pg):
            for r in range(1, X):
                arrived(*latent_from(r, pg))
            local_latents[pg].wait()

            def ring(r, carry):
                zz = lax.rem(z - r + Z, Z)
                maps = jnp.concatenate([vu[r, hh] for hh in range(HD)], axis=1)
                full = mm(rcv[:, pg, zz].reshape(X * HD * PS, lat_w), maps)
                full = full.reshape(X, HD, PS, KD)
                for hh in range(HD):
                    cols = slice(hh * vdim, (hh + 1) * vdim)
                    part = full[:, hh, :, cols].reshape(PAIRS, PR, vdim).astype(jnp.bfloat16)
                    val[zz, pg, :, :, cols] = part
                return carry

            lax.fori_loop(0, Z, ring, 0)
            for r in range(1, Z):
                send(*value_args(r, pg))
            own = pltpu.make_async_copy(val.at[z, pg], vz.at[pg, :, z], lsem.at[4 + NG + pg])
            own.start()
            local_values.append(own)

        def gather_args(r, pg):
            to = ((x + r) % X) // 2
            return vz.at[pg, to], va.at[r, pg], gs.at[pg, r], gr.at[pg, r], at_x(r)

        def gather_start(pg):
            for r in range(1, Z):
                arrived(*value_from(r, pg))
            local_values[pg].wait()
            for r in range(1, X):
                send(*gather_args(r, pg))

        def ring_args(d, i, g):
            sign = 1 - 2 * d
            target = (z - sign * (1 + i) + Z) % Z
            held = po.at[target, g, d] if i == 0 else rs.at[d, g, i - 1]
            return held, rs.at[d, g, i], ss.at[d, g, i], sr.at[d, g, i], at_z(sign + Z)

        def ring_step(i, g):
            for d in range(2):
                arrived(*ring_args(d, i - 1, g))
                target = (z - (1 - 2 * d) * (1 + i) + 2 * Z) % Z
                total = rs[d, g, i - 1].astype(jnp.float32)
                total += po[target, g, d].astype(jnp.float32)
                rs[d, g, i - 1] = total.astype(jnp.bfloat16)
                send(*ring_args(d, i, g))

        def project(g):
            for r in range(1, X):
                arrived(*gather_args(r, g))
            rows = [vz[g, pair]] + [va[r, g] for r in range(1, X)]
            rows = jnp.concatenate([part.reshape(Z * PR, KD) for part in rows], axis=1)
            for d in range(2):

                def tile(n, carry):
                    cols = pl.ds(pl.multiple_of(d * HX + n * NT, NT), NT)
                    acc = mm(rows, w[:, :, cols].reshape(X * KD, NT))
                    part = acc.astype(jnp.bfloat16).reshape(Z, PR, NT)
                    po[:, g, d, :, pl.ds(pl.multiple_of(n * NT, NT), NT)] = part
                    return carry

                lax.fori_loop(0, HX // NT, tile, 0)
                send(*ring_args(d, 0, g))

        def final_args(pg, side):
            return so.at[pg, 1 - side], fin.at[side, pg], fs.at[pg], fr.at[pg], at_x(1 - 2 * half + X)

        local_final = []

        def reduce(pg):
            for d in range(2):
                totals = []
                for g in (2 * pg, 2 * pg + 1):
                    arrived(*ring_args(d, Z - 2, g))
                    total = po[z, g, d].astype(jnp.float32)
                    totals.append(total + rs[d, g, Z - 2].astype(jnp.float32))
                for m in range(2):
                    rows = jnp.concatenate([t[m * PS : (m + 1) * PS] for t in totals], axis=0)
                    so[pg, m, :, pl.ds(d * HX, HX)] = rows.astype(jnp.bfloat16)
            send(*final_args(pg, half))
            own = pltpu.make_async_copy(so.at[pg, half], fin.at[half, pg], lsem.at[4 + 2 * NG + pg])
            own.start()
            local_final.append(own)

        step = 2
        for g in range(NG):
            attention(g)
            if g != 1 and step <= ways:
                v_step(step)
                step += 1
        for r in range(1, X):
            arrived(*w1_args(r))
        y_start(w2_args, PW)
        while step <= ways + 1:
            v_step(step)
            step += 1
        load_vu.wait()
        for r in range(1, Z):
            arrived(*v3_args(r, 1 - c))
        for g in range(NG):
            values(g)
            if g:
                gather_start(g - 1)
            if g == 1:
                y_forward(w2_args, PW, w3_args)
            if g == NG - 2:
                y_finish(w2_args, PW, w3_args)
        load_w.wait()
        for r in range(Y):
            arrived(*w3_args(r, 1 - c))
        project(0)
        gather_start(NG - 1)
        rings = [1]
        while min(rings) < Z:
            started = len(rings)
            if started < NG:
                project(started)
            for g in range(started):
                if rings[g] < Z - 1:
                    ring_step(rings[g], g)
                elif rings[g] == Z - 1 and g % 2:
                    reduce(g // 2)
                rings[g] += 1
            if started < NG:
                rings.append(1)

        place_out = lax.broadcasted_iota(jnp.int32, (steps * req, steps * req), 0)
        place_in = lax.broadcasted_iota(jnp.int32, (steps * req, steps * req), 1)
        slots = jnp.zeros((steps * req, steps * req), jnp.int32)
        for k in range(req):
            slot, _ = slot_and_length(k)
            slots = jnp.where((place_in >> ilog2(steps)) == k, slot, slots)
        place = ((place_out >> ilog2(req)) == (place_in & (steps - 1))) & (
            (place_out & (req - 1)) == slots
        )
        place = place.astype(jnp.bfloat16)
        for pg in range(NPG):
            arrived(*final_args(pg, 1 - half))
            local_final[pg].wait()
        for side in range(2):
            rows = mm(place, fin[side].reshape(steps * req, NX))
            for s in range(steps):
                part = rows[s * req : (s + 1) * req].astype(jnp.bfloat16)
                out_ref[s, :, side * NX : (side + 1) * NX] = part

        for copy in sends:
            copy.wait_send()

    bf = jnp.bfloat16
    dma = pltpu.SemaphoreType.DMA
    scratch = [
        pltpu.VMEM((2 * req, block, width), bf),
        pltpu.VMEM((steps, req, width, heads), bf),
        pltpu.VMEM((sections, CR, width), bf),
        pltpu.VMEM((req, KR, width), bf),
        pltpu.VMEM((GROUP, steps, heads, lat_w), bf),
        pltpu.VMEM((X, NG, Z, HD * PS, lat_w), bf),
        pltpu.VMEM((X, NG, Z, HD * PS, lat_w), bf),
        pltpu.VMEM((Z, HD, lat_w, vdim), bf),
        pltpu.VMEM((Z, NG, PAIRS, PR, KD), bf),
        pltpu.VMEM((NG, PAIRS, Z, PR, KD), bf),
        pltpu.VMEM((X, NG, Z, PR, KD), bf),
        pltpu.VMEM((X, KD, NX), bf),
        pltpu.VMEM((Z, NG, 2, PR, HX), bf),
        pltpu.VMEM((2, NG, Z - 1, PR, HX), bf),
        pltpu.VMEM((NPG, 2, 2 * PS, NX), bf),
        pltpu.VMEM((2, NPG, 2 * PS, NX), bf),
        dma((4 + 2 * NG + NPG,)),
        dma((sections,)), dma((sections,)),
        dma((2, Z)), dma((2, Z)), dma((Z,)), dma((Z,)),
        dma((X,)), dma((X,)), dma((4,)), dma((4,)), dma((Y,)), dma((Y,)),
        dma((NG, X)), dma((NG, X)), dma((NG, Z)), dma((NG, Z)),
        dma((NG, X)), dma((NG, X)), dma((2, NG, Z)), dma((2, NG, Z)),
        dma((NPG,)), dma((NPG,)),
    ]
    return kernel, scratch


def on_device(
    prompt_lengths, owner_map, block_table, pool_blocks, queries, new_latents, value_up, out_proj
):
    sections, devices = lax.axis_size("sect"), lax.axis_size("dev")
    steps, req, heads, width = queries.shape
    _, lat_w, vdim = value_up.shape
    model = out_proj.shape[1]
    block = pool_blocks.shape[2]
    kernel, scratch = make_kernel(
        sections, devices // CHIPS_X, CHIPS_X, steps, req, heads, lat_w, width, vdim, model, block
    )
    smem = pl.BlockSpec(memory_space=pltpu.SMEM)
    vmem = pl.BlockSpec(memory_space=pltpu.VMEM)
    hbm = pl.BlockSpec(memory_space=pl.ANY)
    return pl.pallas_call(
        kernel,
        out_shape=jax.ShapeDtypeStruct((steps, req, model), jnp.bfloat16),
        in_specs=[smem, smem, smem, hbm, hbm, vmem, hbm, hbm],
        out_specs=vmem,
        scratch_shapes=scratch,
        compiler_params=pltpu.CompilerParams(
            collective_id=0, has_side_effects=True, vmem_limit_bytes=60 * 1024 * 1024
        ),
    )(
        owner_map,
        jnp.swapaxes(block_table, 1, 2),
        prompt_lengths,
        pool_blocks,
        jnp.swapaxes(queries, 2, 3),
        new_latents,
        value_up,
        out_proj,
    )


def solution(mesh):
    in_specs = (
        P(None, "dev"),
        P(None, "dev"),
        P(None, "dev", None),
        P("sect", "dev", None, None),
        P(None, ("sect", "dev"), None, None),
        P(None, ("sect", "dev"), None),
        P("dev", None, None),
        P("dev", None),
    )
    out_specs = P(None, ("sect", "dev"), None)
    return jax.shard_map(
        on_device, mesh=mesh, in_specs=in_specs, out_specs=out_specs, check_vma=False
    )
```

```python
import jax
import jax.numpy as jnp
from jax import lax
from jax.experimental import pallas as pl
from jax.experimental.pallas import tpu as pltpu
from jax.sharding import PartitionSpec as P

MESH = pl.DeviceIdType.MESH
CHIPS_X = 4
GROUP = 2
score_scale = 192.0 ** (-0.5)
masked_score = -1e30


def ilog2(n):
    return n.bit_length() - 1


def tn_dot(a, b):
    return lax.dot_general(a, b, (((0,), (0,)), ((), ())), preferred_element_type=jnp.float32)


def mm(a, b):
    return jnp.dot(a, b, preferred_element_type=jnp.float32)


def make_kernel(sections, chips_z, chips_x, steps, req, heads, lat_w, width, vdim, model, block):
    Y, Z, X = sections // 2, chips_z, chips_x
    HD = heads // (Z * X)
    HZ = HD * X
    NG = req // GROUP
    NPG = NG // 2
    PS = GROUP * steps
    CR = 2 * block
    KR = CR + 16
    PAIRS = X // 2
    NX = model // 2
    HX = NX // 2
    PR = 2 * PS
    NT = HX // 2
    KD = HD * vdim
    PW = KD // (2 * Y)

    def kernel(
        owner_ref, table_ref, len_ref, pool_hbm, q_hbm, new_ref, vu_hbm, op_hbm, out_ref,
        pool, q, pk, keys, lat, snd, rcv, vu, val, vz, va, w, po, rs, so, fin,
        lsem, cs, cr, v1s, v1r, v3s, v3r, w1s, w1r, w2s, w2r, w3s, w3r,
        ls, lr, zs, zr, gs, gr, ss, sr, fs, fr,
    ):
        sect = lax.axis_index("sect")
        dev = lax.axis_index("dev")
        y, c = sect // 2, sect % 2
        z, x = dev // X, dev % X
        sibling = y * 2 + (1 - c)
        piece = c * Y + y
        pair, half = x // 2, x % 2
        sends = []

        hops = [(0, 0), (0, 1), (1, 0), (Y - 1, 0), (1, 1), (Y - 1, 1), (2, 0), (2, 1)]
        if Y == 2:
            hops = [(0, 0), (0, 1), (1, 0), (1, 1)]

        def hop(k):
            if isinstance(k, int):
                return hops[k]
            over, across = jnp.int32(0), jnp.int32(0)
            for i, (a, b) in enumerate(hops):
                over += jnp.where(k == i, a, 0)
                across += jnp.where(k == i, b, 0)
            return over, across

        def at_sect(k):
            over, across = hops[k]
            return ((y + over) % Y * 2 + (c + across) % 2, dev)

        def at_y(r):
            return (((y + r) % Y) * 2 + c, dev)

        def at_z(r):
            return (sect, ((z + r) % Z) * X + x)

        def at_x(r):
            return (sect, z * X + (x + r) % X)

        def remote(src, dst, send_sem, recv_sem, to):
            return pltpu.make_async_remote_copy(
                src_ref=src, dst_ref=dst, send_sem=send_sem, recv_sem=recv_sem,
                device_id=to, device_id_type=MESH,
            )

        def send(src, dst, send_sem, recv_sem, to):
            copy = remote(src, dst, send_sem, recv_sem, to)
            copy.start()
            sends.append(copy)

        def arrived(src, dst, send_sem, recv_sem, to):
            remote(src, dst, send_sem, recv_sem, to).wait_recv()

        load_pool = pltpu.make_async_copy(pool_hbm.at[0], pool, lsem.at[0])
        load_q = pltpu.make_async_copy(q_hbm, q, lsem.at[1])
        load_vu = pltpu.make_async_copy(vu_hbm, vu.at[0], lsem.at[2])
        own_cols = pl.ds(pl.multiple_of(half * NX, 128), NX)
        load_w = pltpu.make_async_copy(op_hbm.at[:, own_cols], w.at[0], lsem.at[3])
        load_pool.start()
        load_q.start()
        load_vu.start()
        load_w.start()

        barrier = pltpu.get_barrier_semaphore()
        peers = [at_sect(r) for r in range(1, sections)]
        peers += [at_z(r) for r in range(1, Z)] + [at_x(r) for r in range(1, X)]
        for peer in peers:
            pl.semaphore_signal(barrier, inc=1, device_id=peer, device_id_type=MESH)

        new_rows = new_ref[...].astype(jnp.float32).reshape(steps * req, width)
        new_rows = new_rows.astype(jnp.bfloat16)
        pick_u = lax.broadcasted_iota(jnp.int32, (16, steps * req), 0)
        pick_i = lax.broadcasted_iota(jnp.int32, (16, steps * req), 1)

        def slot_and_length(k):
            over, across = hop(k)
            source = lax.rem(y - over + Y, Y) * 2 + lax.rem(c + across, 2)
            slot, length = jnp.int32(0), jnp.int32(0)
            for i in range(req):
                owner = owner_ref[source, i]
                mine = lax.div(owner, req) == sect
                slot += jnp.where(mine, lax.rem(owner, req), 0)
                length += jnp.where(mine, len_ref[source, i], 0)
            return slot, length

        def fresh(k, carry):
            slot, _ = slot_and_length(k)
            pick = (pick_u == (pick_i >> ilog2(req))) & ((pick_i & (req - 1)) == slot)
            rows = mm(pick.astype(jnp.bfloat16), new_rows)
            keys[k, pl.ds(CR, 16), :] = rows.astype(jnp.bfloat16)
            return carry

        lax.fori_loop(0, req, fresh, 0)
        load_pool.wait()

        def pack(r):
            over, across = hop(r)
            target = lax.rem(y + over, Y) * 2 + lax.rem(c + across, 2)
            first, second = jnp.int32(0), jnp.int32(0)
            for i in range(req):
                hit = lax.div(owner_ref[sect, i], req) == target
                first += jnp.where(hit, table_ref[sect, 0, i], 0)
                second += jnp.where(hit, table_ref[sect, 1, i], 0)
            return pool[first], pool[second]

        def pack_remote(r, carry):
            a, b = pack(r)
            pk[r, 0:block, :] = a
            pk[r, block:CR, :] = b
            return carry

        lax.fori_loop(1, sections, pack_remote, 0)
        a, b = pack(0)
        keys[0, 0:block, :] = a
        keys[0, block:CR, :] = b

        pl.semaphore_wait(barrier, len(peers))

        def cache_args(r):
            return pk.at[r], keys.at[r, pl.ds(0, CR), :], cs.at[r], cr.at[r], at_sect(r)

        for r in range(1, sections):
            send(*cache_args(r))

        wrows = pl.ds(pl.multiple_of(piece * PW, PW), PW)

        VH = lat_w // 2
        ways = Z // 2

        def core_rows(core):
            return pl.ds(pl.multiple_of(core * VH, VH), VH)

        def v1_args(h, d):
            sign = 1 - 2 * d
            some = pl.ds(d * (HD // 2), HD // 2) if h == ways else pl.ds(0, HD)
            rows = core_rows(c)
            if h == 1:
                part = vu_hbm.at[some, rows, :]
            else:
                part = vu.at[sign * (h - 1) % Z, some, rows, :]
            return part, vu.at[sign * h % Z, some, rows, :], v1s.at[d, h], v1r.at[d, h], at_z(sign + Z)

        def v3_args(r, core):
            part = vu.at[r, :, core_rows(core), :]
            return part, part, v3s.at[r], v3r.at[r], (sibling, dev)

        def v_step(h):
            if h > 1:
                for d in range(2):
                    arrived(*v1_args(h - 1, d))
            if h <= ways:
                for d in range(2):
                    send(*v1_args(h, d))
            if 1 < h <= ways:
                for r in (h - 1, Z - h + 1):
                    send(*v3_args(r, c))
            if h == ways + 1:
                send(*v3_args(ways, c))

        def w1_args(r):
            cols = pl.ds(pl.multiple_of(((x + r) % X) % 2 * NX, 128), NX)
            return op_hbm.at[wrows, cols], w.at[r, wrows, :], w1s.at[r], w1r.at[r], at_x(r)

        def from_y(r, size, part, parts):
            start = (c * Y + (y - r + Y) % Y) * size + part * (size // parts)
            return pl.ds(pl.multiple_of(start, size // parts), size // parts)

        def w2_args(r, rows, slot):
            part = w.at[pl.ds(1, X - 1), rows, :]
            return part, part, w2s.at[slot], w2r.at[slot], at_y(r)

        def y_start(args, size):
            send(*args(1, from_y(0, size, 0, 1), 0))
            if Y > 2:
                send(*args(Y - 1, from_y(0, size, 0, 1), 1))

        def w3_args(r, core):
            rows = pl.ds(pl.multiple_of((core * Y + (y - r + Y) % Y) * PW, PW), PW)
            part = w.at[pl.ds(1, X - 1), rows, :]
            return part, part, w3s.at[r], w3r.at[r], (sibling, dev)

        def y_forward(args, size, across):
            send(*across(0, c))
            arrived(*args(1, from_y(1, size, 0, 1), 0))
            if Y > 2:
                send(*args(1, from_y(1, size, 0, 2), 2))
                arrived(*args(Y - 1, from_y(Y - 1, size, 0, 1), 1))
                send(*args(Y - 1, from_y(Y - 1, size, 1, 2), 3))
                send(*across(Y - 1, c))
            send(*across(1, c))

        def y_finish(args, size, across):
            if Y > 2:
                arrived(*args(1, from_y(2, size, 0, 2), 2))
                arrived(*args(Y - 1, from_y(2, size, 1, 2), 3))
                send(*across(2, c))

        v_step(1)
        for r in range(1, X):
            send(*w1_args(r))

        swap_out = lax.broadcasted_iota(jnp.int32, (HZ * PS, HZ * PS), 0)
        swap_in = lax.broadcasted_iota(jnp.int32, (HZ * PS, HZ * PS), 1)
        swap = ((swap_out >> ilog2(PS)) == (swap_in & (HZ - 1))) & (
            (swap_out & (PS - 1)) == (swap_in >> ilog2(HZ))
        )
        swap = swap.astype(jnp.bfloat16)
        load_q.wait()

        def attend(k, k4):
            slot, length = slot_and_length(k)
            key_rows = keys[k]
            key_lat = keys[k, :, 0:lat_w]
            q_cols = jnp.concatenate([q[s, slot] for s in range(steps)], axis=1)
            scores = mm(key_rows, q_cols) * score_scale
            row = lax.broadcasted_iota(jnp.int32, scores.shape, 0)
            step = lax.broadcasted_iota(jnp.int32, scores.shape, 1) >> ilog2(heads)
            held = jnp.where(row < CR, length, CR + 1 + step)
            scores = jnp.where(row < held, scores, masked_score)
            weights = jnp.exp(scores - jnp.max(scores, axis=0, keepdims=True))
            probs = weights * (1.0 / jnp.sum(weights, axis=0, keepdims=True))
            out = tn_dot(probs.astype(jnp.bfloat16), key_lat).astype(jnp.bfloat16)
            lat[k4] = out.reshape(steps, heads, lat_w)

        def latent_args(r, pg):
            to = (x + r) % X
            return snd.at[to, pg], rcv.at[x, pg], ls.at[pg, r], lr.at[pg, r], at_x(r)

        def latent_from(r, pg):
            source = (x - r + X) % X
            return snd.at[source, pg], rcv.at[source, pg], ls.at[pg, r], lr.at[pg, r], at_x(r)

        local_latents = []

        def attention(pg):
            def one(k4, carry):
                k = pg * GROUP + k4

                @pl.when(k > 0)
                def _():
                    arrived(pk.at[k], keys.at[k, pl.ds(0, CR), :], cs.at[k], cr.at[k], at_sect(1))

                attend(k, k4)
                return carry

            lax.fori_loop(0, GROUP, one, 0)

            def turn(zz, carry):
                part = lat[:, :, pl.ds(pl.multiple_of(zz * HZ, HZ), HZ), :]
                turned = mm(swap, part.reshape(PS * HZ, lat_w)).astype(jnp.bfloat16)
                snd[:, pg, zz] = turned.reshape(X, HD * PS, lat_w)
                return carry

            lax.fori_loop(0, Z, turn, 0, unroll=2)
            for r in range(1, X):
                send(*latent_args(r, pg))
            own = pltpu.make_async_copy(snd.at[x, pg], rcv.at[x, pg], lsem.at[4 + pg])
            own.start()
            local_latents.append(own)

        def value_args(r, pg):
            to = (z + r) % Z
            return val.at[to, pg], vz.at[pg, :, z], zs.at[pg, r], zr.at[pg, r], at_z(r)

        def value_from(r, pg):
            source = (z - r + Z) % Z
            return val.at[source, pg], vz.at[pg, :, source], zs.at[pg, r], zr.at[pg, r], at_z(r)

        local_values = []

        def values(pg):
            for r in range(1, X):
                arrived(*latent_from(r, pg))
            local_latents[pg].wait()

            def ring(r, carry):
                zz = lax.rem(z - r + Z, Z)
                maps = jnp.concatenate([vu[r, hh] for hh in range(HD)], axis=1)
                full = mm(rcv[:, pg, zz].reshape(X * HD * PS, lat_w), maps)
                full = full.reshape(X, HD, PS, KD)
                for hh in range(HD):
                    cols = slice(hh * vdim, (hh + 1) * vdim)
                    part = full[:, hh, :, cols].reshape(PAIRS, PR, vdim).astype(jnp.bfloat16)
                    val[zz, pg, :, :, cols] = part
                return carry

            lax.fori_loop(0, Z, ring, 0, unroll=2)
            for r in range(1, Z):
                send(*value_args(r, pg))
            own = pltpu.make_async_copy(val.at[z, pg], vz.at[pg, :, z], lsem.at[4 + NG + pg])
            own.start()
            local_values.append(own)

        def gather_args(r, pg):
            to = ((x + r) % X) // 2
            return vz.at[pg, to], va.at[r, pg], gs.at[pg, r], gr.at[pg, r], at_x(r)

        def gather_start(pg):
            for r in range(1, Z):
                arrived(*value_from(r, pg))
            local_values[pg].wait()
            for r in range(1, X):
                send(*gather_args(r, pg))

        def ring_args(d, i, g):
            sign = 1 - 2 * d
            target = (z - sign * (1 + i) + Z) % Z
            held = po.at[target, g, d] if i == 0 else rs.at[d, g, i - 1]
            return held, rs.at[d, g, i], ss.at[d, g, i], sr.at[d, g, i], at_z(sign + Z)

        def ring_step(i, g):
            for d in range(2):
                arrived(*ring_args(d, i - 1, g))
                target = (z - (1 - 2 * d) * (1 + i) + 2 * Z) % Z
                total = rs[d, g, i - 1].astype(jnp.float32)
                total += po[target, g, d].astype(jnp.float32)
                rs[d, g, i - 1] = total.astype(jnp.bfloat16)
                send(*ring_args(d, i, g))

        def project(g):
            for r in range(1, X):
                arrived(*gather_args(r, g))
            rows = [vz[g, pair]] + [va[r, g] for r in range(1, X)]
            rows = jnp.concatenate([part.reshape(Z * PR, KD) for part in rows], axis=1)
            for d in range(2):

                def tile(n, carry):
                    cols = pl.ds(pl.multiple_of(d * HX + n * NT, NT), NT)
                    acc = mm(rows, w[:, :, cols].reshape(X * KD, NT))
                    part = acc.astype(jnp.bfloat16).reshape(Z, PR, NT)
                    po[:, g, d, :, pl.ds(pl.multiple_of(n * NT, NT), NT)] = part
                    return carry

                lax.fori_loop(0, HX // NT, tile, 0)
                send(*ring_args(d, 0, g))

        def final_args(pg, side):
            return so.at[pg, 1 - side], fin.at[side, pg], fs.at[pg], fr.at[pg], at_x(1 - 2 * half + X)

        local_final = []

        def reduce(pg):
            for d in range(2):
                totals = []
                for g in (2 * pg, 2 * pg + 1):
                    arrived(*ring_args(d, Z - 2, g))
                    total = po[z, g, d].astype(jnp.float32)
                    totals.append(total + rs[d, g, Z - 2].astype(jnp.float32))
                for m in range(2):
                    rows = jnp.concatenate([t[m * PS : (m + 1) * PS] for t in totals], axis=0)
                    so[pg, m, :, pl.ds(d * HX, HX)] = rows.astype(jnp.bfloat16)
            send(*final_args(pg, half))
            own = pltpu.make_async_copy(so.at[pg, half], fin.at[half, pg], lsem.at[4 + 2 * NG + pg])
            own.start()
            local_final.append(own)

        step = 2
        for g in range(NG):
            attention(g)
            if g != 1 and step <= ways:
                v_step(step)
                step += 1
        for r in range(1, X):
            arrived(*w1_args(r))
        y_start(w2_args, PW)
        while step <= ways + 1:
            v_step(step)
            step += 1
        load_vu.wait()
        for r in range(1, Z):
            arrived(*v3_args(r, 1 - c))
        for g in range(NG):
            values(g)
            if g:
                gather_start(g - 1)
            if g == 1:
                y_forward(w2_args, PW, w3_args)
            if g == NG - 2:
                y_finish(w2_args, PW, w3_args)
        load_w.wait()
        for r in range(Y):
            arrived(*w3_args(r, 1 - c))
        project(0)
        gather_start(NG - 1)
        rings = [1]
        while min(rings) < Z:
            started = len(rings)
            if started < NG:
                project(started)
            for g in range(started):
                if rings[g] < Z - 1:
                    ring_step(rings[g], g)
                elif rings[g] == Z - 1 and g % 2:
                    reduce(g // 2)
                rings[g] += 1
            if started < NG:
                rings.append(1)

        place_out = lax.broadcasted_iota(jnp.int32, (steps * req, steps * req), 0)
        place_in = lax.broadcasted_iota(jnp.int32, (steps * req, steps * req), 1)
        slots = jnp.zeros((steps * req, steps * req), jnp.int32)
        for k in range(req):
            slot, _ = slot_and_length(k)
            slots = jnp.where((place_in >> ilog2(steps)) == k, slot, slots)
        place = ((place_out >> ilog2(req)) == (place_in & (steps - 1))) & (
            (place_out & (req - 1)) == slots
        )
        place = place.astype(jnp.bfloat16)
        for pg in range(NPG):
            arrived(*final_args(pg, 1 - half))
            local_final[pg].wait()
        for side in range(2):
            rows = mm(place, fin[side].reshape(steps * req, NX))
            for s in range(steps):
                part = rows[s * req : (s + 1) * req].astype(jnp.bfloat16)
                out_ref[s, :, side * NX : (side + 1) * NX] = part

        for copy in sends:
            copy.wait_send()

    bf = jnp.bfloat16
    dma = pltpu.SemaphoreType.DMA
    scratch = [
        pltpu.VMEM((2 * req, block, width), bf),
        pltpu.VMEM((steps, req, width, heads), bf),
        pltpu.VMEM((sections, CR, width), bf),
        pltpu.VMEM((req, KR, width), bf),
        pltpu.VMEM((GROUP, steps, heads, lat_w), bf),
        pltpu.VMEM((X, NG, Z, HD * PS, lat_w), bf),
        pltpu.VMEM((X, NG, Z, HD * PS, lat_w), bf),
        pltpu.VMEM((Z, HD, lat_w, vdim), bf),
        pltpu.VMEM((Z, NG, PAIRS, PR, KD), bf),
        pltpu.VMEM((NG, PAIRS, Z, PR, KD), bf),
        pltpu.VMEM((X, NG, Z, PR, KD), bf),
        pltpu.VMEM((X, KD, NX), bf),
        pltpu.VMEM((Z, NG, 2, PR, HX), bf),
        pltpu.VMEM((2, NG, Z - 1, PR, HX), bf),
        pltpu.VMEM((NPG, 2, 2 * PS, NX), bf),
        pltpu.VMEM((2, NPG, 2 * PS, NX), bf),
        dma((4 + 2 * NG + NPG,)),
        dma((sections,)), dma((sections,)),
        dma((2, Z)), dma((2, Z)), dma((Z,)), dma((Z,)),
        dma((X,)), dma((X,)), dma((4,)), dma((4,)), dma((Y,)), dma((Y,)),
        dma((NG, X)), dma((NG, X)), dma((NG, Z)), dma((NG, Z)),
        dma((NG, X)), dma((NG, X)), dma((2, NG, Z)), dma((2, NG, Z)),
        dma((NPG,)), dma((NPG,)),
    ]
    return kernel, scratch


def on_device(
    prompt_lengths, owner_map, block_table, pool_blocks, queries, new_latents, value_up, out_proj
):
    sections, devices = lax.axis_size("sect"), lax.axis_size("dev")
    steps, req, heads, width = queries.shape
    _, lat_w, vdim = value_up.shape
    model = out_proj.shape[1]
    block = pool_blocks.shape[2]
    kernel, scratch = make_kernel(
        sections, devices // CHIPS_X, CHIPS_X, steps, req, heads, lat_w, width, vdim, model, block
    )
    smem = pl.BlockSpec(memory_space=pltpu.SMEM)
    vmem = pl.BlockSpec(memory_space=pltpu.VMEM)
    hbm = pl.BlockSpec(memory_space=pl.ANY)
    return pl.pallas_call(
        kernel,
        out_shape=jax.ShapeDtypeStruct((steps, req, model), jnp.bfloat16),
        in_specs=[smem, smem, smem, hbm, hbm, vmem, hbm, hbm],
        out_specs=vmem,
        scratch_shapes=scratch,
        compiler_params=pltpu.CompilerParams(
            collective_id=0, has_side_effects=True, vmem_limit_bytes=60 * 1024 * 1024
        ),
    )(
        owner_map,
        jnp.swapaxes(block_table, 1, 2),
        prompt_lengths,
        pool_blocks,
        jnp.swapaxes(queries, 2, 3),
        new_latents,
        value_up,
        out_proj,
    )


def solution(mesh):
    in_specs = (
        P(None, "dev"),
        P(None, "dev"),
        P(None, "dev", None),
        P("sect", "dev", None, None),
        P(None, ("sect", "dev"), None, None),
        P(None, ("sect", "dev"), None),
        P("dev", None, None),
        P("dev", None),
    )
    out_specs = P(None, ("sect", "dev"), None)
    return jax.shard_map(
        on_device, mesh=mesh, in_specs=in_specs, out_specs=out_specs, check_vma=False
    )
```
